32 devices in a mesh: gx: 8 (over y, x, core), gy: 4 (over z).
Axes of the slice: x: 2, y: 2, z: 4, core: 2. Of those that a mesh axis runs over, the one named last changes fastest.
Arguments:
- state_in: float32 [4, 8192, 16, 128], P(None, ('gx', 'gy')), may hold values from -6 to 6
- stiffness: float32 [16, 16, 8192], P(None, None, ('gx', 'gy')), may hold values from -1.5 to 1.5
- elem_cell: int32 [8192], P(('gx', 'gy')), may hold values from 0 to 8191, as said below
- group_column: int32 [32768], P(('gx', 'gy')), may hold values from 0 to 32767, as said below
- group_inverse: bfloat16 [2048, 128, 128], P(('gx', 'gy')), may hold values from 0 to 0.875
Outputs:
- state_out: float32 [4, 8192, 16, 128], P(None, ('gx', 'gy'))
The draws below stay inside these ranges and needn't reach their ends.
Inputs may be any that keep to these rules, and one draw needn't show every extreme that they name: `elem_cell`: device i * 4 + j (index i along gx, j along gy) holds in its 256 slots, in some order, exactly the cells with x from i * 16 to (i + 1) * 16 - 1 and y from j * 16 to (j + 1) * 16 - 1; every cell is held once. `group_column`: every column is named once. Column c lies on device c // 1024, slot p on device p // 1024; the 1024 slots of each device name exactly 32 columns of each device.
All inputs are finite; a program needn't handle non-finite values.
Results may differ from the reference program's by a relative error of at most 0.0031.
Values may be sent and summed in bfloat16 or wider, within the bound.
No kernel may reach another device: no remote copies, remote signals or barrier semaphores. Data moves between devices by JAX's collectives and lax.ppermute only.
A program may use at most 128 MiB of HBM per device.

```python
import math
import jax
import jax.numpy as jnp
from jax import lax

LEV = 128
NF = 4
NP = 16
GROUP_COLS = 16
EXD = 16
EYD = 16
COL_DEV = 1024
EX = 128
EY = 64
NELEM = 8192
NCOL = 32768
GROUPS = 2048
N_GX = 8
N_GY = 4


def draw_elem_cell(key, part):
    devices = N_GX * N_GY
    per_device = EXD * EYD
    keys = jax.random.split(key, devices)
    orders = jax.vmap(lambda single: jax.random.permutation(single, per_device))(keys).astype(jnp.int32)
    device_ids = jnp.arange(devices, dtype=jnp.int32)[:, None]
    cell_x = device_ids // N_GY * EXD + orders // EYD
    cell_y = device_ids % N_GY * EYD + orders % EYD
    return (cell_x * EY + cell_y).reshape(-1).astype(jnp.int32)


def draw_group_column(key, part):
    devices = N_GX * N_GY
    per_peer = COL_DEV // devices
    first_key, second_key = jax.random.split(key)
    chosen = jax.vmap(lambda single: jax.random.permutation(single, COL_DEV))(jax.random.split(first_key, devices)).astype(jnp.int32)
    slot_draw = jax.vmap(lambda single: jax.random.permutation(single, COL_DEV))(jax.random.split(second_key, devices)).astype(jnp.int32)
    source = slot_draw // per_peer
    within = slot_draw % per_peer
    dest_ids = jnp.arange(devices, dtype=jnp.int32)[:, None]
    local_index = chosen[source, dest_ids * per_peer + within]
    return (source * COL_DEV + local_index).reshape(-1).astype(jnp.int32)


def draw_group_inverse(key, part):
    first_key, second_key = jax.random.split(key)
    length_scale = jnp.exp(jax.random.uniform(first_key, (GROUPS, 1, 1), jnp.float32, 0.0, math.log(16.0)))
    factor = jax.random.uniform(second_key, (GROUPS, LEV, LEV), jnp.float32, 0.5, 1.5)
    levels_row = jnp.arange(LEV, dtype=jnp.float32)[:, None]
    levels_col = jnp.arange(LEV, dtype=jnp.float32)[None, :]
    distance = jnp.abs(levels_row - levels_col)[None, :, :]
    values = factor * jnp.exp(-distance / length_scale) / (1.0 + 2.0 * length_scale)
    return values.astype(jnp.bfloat16)


def block_scale(key, shape, cuts, least, top_value):
    factor_of, own = 1.0, jax.random.fold_in(key, 6)
    for dim, shards_of in cuts:
        draws = jnp.exp(jax.random.uniform(jax.random.fold_in(own, dim), (shards_of,), jnp.float32, least / len(cuts), top_value / len(cuts)))
        factor_of = factor_of * jnp.repeat(draws, shape[dim] // shards_of).reshape([-1 if axis == dim else 1 for axis in range(len(shape))])
    return factor_of


def bell_draw(key, extent, deviation, most, shards=(), kind=jnp.bfloat16):
    loudness = block_scale(key, extent, shards, -0.22, 0.18) if shards else 1.0
    values = jax.random.normal(key, extent, jnp.float32) * deviation * loudness
    return jnp.minimum(jnp.maximum(values, -most), most).astype(kind)


def setup_inputs(seed: int = 0) -> dict:
    splits = jax.random.split(jax.random.key(seed), 6)
    state_in = bell_draw(splits[0], (NF, NELEM, NP, LEV), 1.0, 6.0, ((1, 32),), jnp.float32)
    stiffness = bell_draw(splits[1], (NP, NP, NELEM), NP ** -0.5, 1.5, ((2, 32),), jnp.float32)
    elem_cell = draw_elem_cell(jax.random.fold_in(splits[5], 71), 0)
    group_column = draw_group_column(jax.random.fold_in(splits[5], 71), 0)
    group_inverse = draw_group_inverse(jax.random.fold_in(splits[5], 71), 0)
    return dict(state_in=state_in, stiffness=stiffness, elem_cell=elem_cell, group_column=group_column, group_inverse=group_inverse)


exact_mode = lax.Precision.HIGHEST

def lagrange_value(node_index, position, gll_nodes):
    running = 1.0
    for other_index in range(4):
        if other_index != node_index:
            running = running * (position - gll_nodes[other_index]) / (gll_nodes[node_index] - gll_nodes[other_index])
    return running

def half_tables():
    gll_nodes = [-1.0, -1.0 / math.sqrt(5.0), 1.0 / math.sqrt(5.0), 1.0]
    halves = [[0.0] * 4, [0.0] * 4]
    for half_index, bounds in enumerate(((-1.0, 0.0), (0.0, 1.0))):
        lower_end, upper_end = bounds
        centre_point = 0.5 * (lower_end + upper_end)
        offset_gauss = 0.5 * (upper_end - lower_end) / math.sqrt(3.0)
        for node_index in range(4):
            first_value = lagrange_value(node_index, centre_point - offset_gauss, gll_nodes)
            second_value = lagrange_value(node_index, centre_point + offset_gauss, gll_nodes)
            halves[half_index][node_index] = 0.5 * (upper_end - lower_end) * (first_value + second_value)
    product = [[sum((halves[row_index][k_index] * halves[col_index][k_index] for k_index in range(4))) for col_index in range(2)] for row_index in range(2)]
    determinant = product[0][0] * product[1][1] - product[0][1] * product[1][0]
    inverse = [[product[1][1] / determinant, -product[0][1] / determinant], [-product[1][0] / determinant, product[0][0] / determinant]]
    spread = [[sum((halves[k_index][node_index] * inverse[k_index][col_index] for k_index in range(2))) for col_index in range(2)] for node_index in range(4)]
    return (jnp.asarray(halves, jnp.float32), jnp.asarray(spread, jnp.float32))

def assemble(element_grid):
    from_west = jnp.roll(element_grid[:, :, 3], 1, axis=0)
    from_east = jnp.roll(element_grid[:, :, 0], -1, axis=0)
    across = element_grid.at[:, :, 0].add(from_west).at[:, :, 3].add(from_east)
    from_south = jnp.roll(across[:, :, :, 3], 1, axis=1)
    from_north = jnp.roll(across[:, :, :, 0], -1, axis=1)
    summed = across.at[:, :, :, 0].add(from_south).at[:, :, :, 3].add(from_north)
    sharing = jnp.array([2.0, 1.0, 1.0, 2.0], jnp.float32)
    return summed / (sharing[:, None] * sharing[None, :])[:, :, None]

def reference(state_in, stiffness, elem_cell, group_column, group_inverse):
    halves, spread = half_tables()
    slot_of_cell = jnp.zeros((NELEM,), jnp.int32).at[elem_cell].set(jnp.arange(NELEM, dtype=jnp.int32))
    column_of_slot = jnp.zeros((NCOL,), jnp.int32).at[group_column].set(jnp.arange(NCOL, dtype=jnp.int32))
    inverse_wide = group_inverse.astype(jnp.float32)

    def one_field(one_state):
        local_term = jnp.einsum('nme,eml->enl', stiffness, one_state, precision=exact_mode)
        combined = one_state + local_term
        element_grid = combined[slot_of_cell].reshape(EX, EY, 4, 4, LEV)
        dynamics = assemble(element_grid)
        columns = jnp.einsum('ia,jb,xyabl->xyijl', halves, halves, dynamics, precision=exact_mode).astype(jnp.bfloat16)
        columns = columns.reshape(NELEM, 4, LEV)[elem_cell].reshape(NCOL, LEV)
        physics = columns[group_column].reshape(GROUPS, GROUP_COLS, LEV).astype(jnp.float32)
        smoothed = jnp.einsum('gkl,gjl->gjk', inverse_wide, physics, precision=exact_mode)
        tendency = (smoothed - physics).astype(jnp.bfloat16).reshape(NCOL, LEV)
        returned = tendency[column_of_slot]
        back_grid = returned.reshape(NELEM, 2, 2, LEV)[slot_of_cell].astype(jnp.float32)
        on_nodes = jnp.einsum('ai,bj,eijl->eabl', spread, spread, back_grid, precision=exact_mode)
        updated = dynamics + assemble(on_nodes.reshape(EX, EY, 4, 4, LEV))
        return updated.reshape(NELEM, 16, LEV)[elem_cell]
    return lax.map(one_field, state_in)
```

```python
import functools
import math

import jax
import jax.numpy as jnp
import numpy as np
from jax import lax
from jax.experimental import pallas as pl
from jax.experimental.pallas import tpu as pltpu
from jax.sharding import PartitionSpec as P

GROUP_COLS = 16
EXD = 16
EYD = 16
NP = 16
F32 = jnp.float32
BF16 = jnp.bfloat16
I32 = jnp.int32
MB = 1024 * 1024


def lagrange_value(node_index, position, gll_nodes):
    running = 1.0
    for other_index in range(4):
        if other_index != node_index:
            running = (
                running
                * (position - gll_nodes[other_index])
                / (gll_nodes[node_index] - gll_nodes[other_index])
            )
    return running


def half_tables():
    gll_nodes = [-1.0, -1.0 / math.sqrt(5.0), 1.0 / math.sqrt(5.0), 1.0]
    halves = np.zeros((2, 4))
    for half_index, (lower_end, upper_end) in enumerate(((-1.0, 0.0), (0.0, 1.0))):
        centre = 0.5 * (lower_end + upper_end)
        offset = 0.5 * (upper_end - lower_end) / math.sqrt(3.0)
        for node in range(4):
            first = lagrange_value(node, centre - offset, gll_nodes)
            second = lagrange_value(node, centre + offset, gll_nodes)
            halves[half_index, node] = 0.5 * (upper_end - lower_end) * (first + second)
    product = halves @ halves.T
    determinant = product[0, 0] * product[1, 1] - product[0, 1] * product[1, 0]
    inverse = (
        np.array([[product[1, 1], -product[0, 1]], [-product[1, 0], product[0, 0]]]) / determinant
    )
    spread = halves.T @ inverse
    return halves.astype(np.float32), spread.astype(np.float32)


HALVES, SPREAD = half_tables()
ONE_D = np.array([0.5, 1.0, 1.0, 0.5])


def shift_down(n):
    return np.eye(n, k=-1)


def local_pass(n):
    table = np.einsum("ab,xy->axby", np.eye(4), np.eye(n))
    table[0, :, 3, :] += shift_down(n)
    table[3, :, 0, :] += shift_down(n).T
    return table


def constant_tables():
    h = HALVES.astype(np.float64)
    s = SPREAD.astype(np.float64)
    w = ONE_D
    eye = np.eye(EXD)
    line = local_pass(EYD)
    col_x = []
    for a in (0, 3):
        col_x.append(
            np.einsum("i,jb,b,byez->ijyez", h[:, a] * w[a], h, w, line).reshape(4 * EYD, 4 * EYD)
        )
    col_y = np.zeros((EXD, 2, 2, EYD, 2, 4, EXD))
    for side, (b, y) in enumerate(((0, 0), (3, EYD - 1))):
        col_y[:, :, :, y, side] = np.einsum("ia,j,xz->xijaz", h * w, h[:, b] * w[b], eye)
    col_y = col_y.reshape(EXD * 4 * EYD, 2 * 4 * EXD)
    nodes = np.einsum("ai,bj,yz->abyijz", s, s, np.eye(EYD))
    across = np.zeros((4, 4, EYD, 3, 2, 2, EYD))
    across[:, :, :, 1] = nodes
    across[0, :, :, 0] = nodes[3]
    across[3, :, :, 2] = nodes[0]
    full = np.einsum("byez,aezdijt->abydijt", line, across)
    full = full * w[:, None, None, None, None, None, None] * w[:, None, None, None, None, None]
    final = full.reshape(NP * EYD, 3 * 4 * EYD)
    along = local_pass(EXD)
    lines = np.zeros((2, 4, EXD, EXD, 2, 2, EYD))
    corner_col = np.zeros((2, 4, EXD, 2, 2, 2, EYD))
    corner_pt = np.zeros((2, 4, EXD, 2, 4, EYD))
    for side, (b, y) in enumerate(((0, 0), (3, EYD - 1))):
        lines[side, :, :, :, :, :, y] = np.einsum("axcz,ci,j->axzij", along, s, s[b])
        corner_col[side, 0, 0, 0, :, :, y] = np.outer(s[3], s[b])
        corner_col[side, 3, EXD - 1, 1, :, :, y] = np.outer(s[0], s[b])
        corner_pt[side, 0, 0, 0, b, y] = 1.0
        corner_pt[side, 3, EXD - 1, 1, b, y] = 1.0
    lines = lines.reshape(2 * 4 * EXD, EXD * 4 * EYD)
    corner_col = corner_col.reshape(2 * 4 * EXD, 2 * 4 * EYD)
    corner_pt = corner_pt.reshape(2 * 4 * EXD, 2 * 4 * EYD)
    border = np.zeros((4, EYD, NP, 128))
    order = full.transpose(2, 0, 1, 3, 4, 5, 6).reshape(EYD, NP, 3, 4 * EYD)
    west, east = hi_lo_arrays(order[:, :, 0]), hi_lo_arrays(order[:, :, 2])
    border[0] = np.concatenate(west, axis=-1)
    border[1] = np.concatenate(east, axis=-1)
    for side, b in enumerate((0, 3)):
        for a in range(4):
            for x in range(EXD):
                border[2 + side, x, 4 * a + b, 16 * a + x] = w[a] * w[b]
    return dict(
        col_x=np.concatenate(col_x, axis=0),
        col_y=col_y,
        final=order.reshape(EYD * NP, 3 * 4 * EYD),
        lines=lines,
        corner_col=corner_col,
        corner_pt=corner_pt,
        border=border.reshape(4 * EYD * NP, 128),
    )


def hi_lo_arrays(table):
    hi = np.asarray(table, np.float32).astype(jnp.bfloat16)
    lo = (np.asarray(table, np.float32) - hi.astype(np.float32)).astype(jnp.bfloat16)
    return hi, lo


def hi_lo(table):
    return jnp.asarray(np.concatenate(hi_lo_arrays(table), axis=1))


TABLES = constant_tables()


def dot(left, right):
    return jnp.dot(left, right, preferred_element_type=F32)


def dot_nt(left, right):
    return lax.dot_general(left, right, (((1,), (1,)), ((), ())), preferred_element_type=F32)


def dot_twice(table, right):
    return dot(table, jnp.concatenate([right, right], axis=0))


def split(values):
    hi = values.astype(BF16)
    return hi, (values - hi.astype(F32)).astype(BF16)


def iota(shape, dim):
    return lax.broadcasted_iota(I32, shape, dim)


def one_hot(condition):
    return jnp.where(condition, 1.0, 0.0).astype(BF16)


def as_columns(row, start):
    piece = row[:, start : start + 128].astype(F32)
    return jnp.transpose(jnp.broadcast_to(piece, (128, 128))).astype(I32)


def tile_number(cell, span_y):
    shift = span_y.bit_length() - 1
    assert span_y == 1 << shift
    return ((cell >> shift) & (EXD - 1)) * EYD + (cell & (EYD - 1))


VMEM = pl.BlockSpec(memory_space=pltpu.VMEM)
SMEM = pl.BlockSpec(memory_space=pltpu.SMEM)
ANY = pl.BlockSpec(memory_space=pl.ANY)


def params(mib):
    return pltpu.CompilerParams(vmem_limit_bytes=mib * MB)


def cost(flops, moved):
    return pl.CostEstimate(flops=int(flops), bytes_accessed=int(moved), transcendentals=0)


def request_kernel(devices, per_peer, group_ref, wanted_ref, q_ref):
    columns_dev = devices * per_peer
    shift = columns_dev.bit_length() - 1
    group = group_ref[...]
    source = group >> shift
    local = group & (columns_dev - 1)
    of_source = source == iota((devices, columns_dev), 0)
    marks = one_hot(of_source)
    upper = one_hot(iota((128, 128), 0) <= iota((128, 128), 1))
    before = jnp.zeros((devices, 1), F32)
    ranks = []
    for start in range(0, columns_dev, 128):
        piece = marks[:, start : start + 128]
        counts = dot(piece, upper) + before
        ranks.append(counts)
        before = counts[:, 127:128]
    counts = jnp.concatenate(ranks, axis=1)
    rank = jnp.sum(jnp.where(of_source, counts, 0.0), axis=0, keepdims=True).astype(I32) - 1
    q_ref[...] = source * per_peer + rank
    of_rank = one_hot(rank == iota((128, columns_dev), 0))
    high = jnp.where(of_source, (local >> 5).astype(F32), 0.0).astype(BF16)
    low = jnp.where(of_source, (local & 31).astype(F32), 0.0).astype(BF16)
    wanted = (dot_nt(high, of_rank) * 32.0 + dot_nt(low, of_rank)).astype(I32)
    wanted_ref[...] = jnp.broadcast_to(wanted[:, None, :], (devices, 8, 128))


def requests(group, devices):
    columns_dev = group.shape[1]
    return pl.pallas_call(
        functools.partial(request_kernel, devices, columns_dev // devices),
        out_shape=(
            jax.ShapeDtypeStruct((devices, 8, 128), I32),
            jax.ShapeDtypeStruct((1, columns_dev), I32),
        ),
        in_specs=[VMEM],
        out_specs=(VMEM,) * 2,
        compiler_params=params(16),
        cost_estimate=cost(2e7, 2e5),
        name="requests",
    )(group)


def operator_masks(rows):
    row, col = iota((rows, 256), 0), iota((rows, 256), 1)
    same_elem = one_hot((row & 15) == (col >> 4))
    row, col = iota((256, 256), 0), iota((256, 256), 1)
    tiling = one_hot((row & 15) == (col & 15))
    return tiling, same_elem


def operator_block(ktt, nodes, tiling, same_elem):
    parts = []
    column = iota((16, 256), 1) >> 4
    for part in split(ktt):
        part = part.astype(F32)
        stacked = jnp.concatenate(
            [jnp.where(column == n, part, 0.0).astype(BF16) for n in nodes], axis=0
        )
        parts.append(dot(stacked, tiling).astype(BF16) * same_elem)
    return parts


def apply_operator(operator, hi, lo):
    k_hi, k_lo = operator
    return dot(k_hi, hi) + dot(k_lo, hi) + dot(k_hi, lo)


def shifted(values, step):
    rows = values.shape[0]
    moved = pltpu.roll(values, step % rows, 0)
    free = 0 if step > 0 else rows - 1
    return jnp.where(iota(values.shape, 0) == free, 0.0, moved)


CHUNKS = 8


def front_kernel(
    fields,
    span_y,
    cell_smem,
    cell_ref,
    stiff_ref,
    state_ref,
    hi_ref,
    lo_ref,
    ktt_ref,
    slot_ref,
    west_ref,
    east_ref,
    south_ref,
    north_ref,
    buffer,
    sems,
):
    elements = cell_ref.shape[1]
    levels = state_ref.shape[3]
    per = elements // CHUNKS

    def copy(chunk):
        return pltpu.make_async_copy(
            state_ref.at[:, pl.ds(chunk * per, per)], buffer.at[chunk], sems.at[chunk]
        )

    for chunk in range(CHUNKS):
        copy(chunk).start()

    tile = tile_number(cell_ref[...], span_y)
    marks = one_hot(tile == iota((elements, elements), 0))
    pick = iota((64, elements), 0)
    kind = pick >> 4
    place = pick & 15
    edge_tile = jnp.where(
        kind == 0,
        place,
        jnp.where(
            kind == 1,
            place + (EXD - 1) * EYD,
            jnp.where(kind == 2, place * EYD, place * EYD + EYD - 1),
        ),
    )
    marks = jnp.concatenate([marks, one_hot(tile == edge_tile)], axis=0)
    stiff = stiff_ref[...]
    row = iota(stiff.shape, 0)
    stiff = stiff + jnp.where((row >> 4) == (row & 15), 1.0, 0.0)
    k_hi, k_lo = split(stiff)
    ktt = dot_nt(marks, k_hi) + dot_nt(marks, k_lo)
    ktt_ref[...] = ktt[0:elements]
    tiling, same_elem = operator_masks(64)
    nodes = ((0, 1, 2, 3), (12, 13, 14, 15), (0, 4, 8, 12), (3, 7, 11, 15))
    operators = [
        operator_block(
            ktt[elements + 16 * k : elements + 16 * k + 16], nodes[k], tiling, same_elem
        )
        for k in range(4)
    ]

    for chunk in range(CHUNKS):
        copy(chunk).wait()

        def place_slots(i, _, chunk=chunk):
            for u in range(4):
                k = i * 4 + u
                slot = chunk * per + k
                where = tile_number(cell_smem[slot], span_y)
                slot_ref[0, where] = slot
                for f in range(fields):
                    hi, lo = split(buffer[chunk, f, k])
                    hi_ref[where, :, f * levels : (f + 1) * levels] = hi
                    lo_ref[where, :, f * levels : (f + 1) * levels] = lo
            return 0

        lax.fori_loop(0, per // 4, place_slots, 0)

    for kind in range(4):
        if kind < 2:
            first = (0, (EXD - 1) * EYD)[kind]
            hi, lo = (
                part[first : first + EYD].reshape(EYD * NP, fields * levels)
                for part in (hi_ref, lo_ref)
            )
        else:
            y = (0, EYD - 1)[kind - 2]
            hi, lo = (
                jnp.concatenate([part[x * EYD + y] for x in range(EXD)], axis=0)
                for part in (hi_ref, lo_ref)
            )
        line = apply_operator(operators[kind], hi, lo)
        if kind == 0:
            west_ref[...] = line.astype(BF16)
        elif kind == 1:
            east_ref[...] = line.astype(BF16)
        else:
            first, last = line[0:16], line[48:64]
            out = (south_ref, north_ref)[kind - 2]
            out[0:16] = first + shifted(last, 1)
            out[16:48] = line[16:48]
            out[48:64] = last + shifted(first, -1)


def front(cell, stiff, state, span_y):
    fields, elements, _, levels = state.shape
    width = fields * levels
    return pl.pallas_call(
        functools.partial(front_kernel, fields, span_y),
        out_shape=(
            jax.ShapeDtypeStruct((elements, NP, width), BF16),
            jax.ShapeDtypeStruct((elements, NP, width), BF16),
            jax.ShapeDtypeStruct((elements, 256), F32),
            jax.ShapeDtypeStruct((1, elements), I32),
            jax.ShapeDtypeStruct((64, width), BF16),
            jax.ShapeDtypeStruct((64, width), BF16),
            jax.ShapeDtypeStruct((64, width), F32),
            jax.ShapeDtypeStruct((64, width), F32),
        ),
        in_specs=[SMEM, VMEM, VMEM, ANY],
        out_specs=(VMEM, VMEM, VMEM, SMEM, VMEM, VMEM, VMEM, VMEM),
        scratch_shapes=[
            pltpu.VMEM((CHUNKS, fields, elements // CHUNKS, NP, levels), F32),
            pltpu.SemaphoreType.DMA((CHUNKS,)),
        ],
        compiler_params=params(FRONT_LIMIT),
        cost_estimate=cost(8e8, 2e7),
        name="front",
    )(cell, cell.reshape(1, elements), stiff, state)


FRONT_LIMIT = 48


def row_kernel(emit_columns, *refs):
    ktt_ref, hi_ref, lo_ref = refs[:3]
    refs = refs[3:]
    if not emit_columns:
        hx_west, hx_east, hy_south, hy_north = refs[:4]
        refs = refs[4:]
    out_ref, held, before = refs[:3]
    width = held.shape[1]
    if not emit_columns:
        turned = refs[3]
        levels = turned.shape[2]
        fields = width // levels
    tiling, same_elem = operator_masks(256)

    def emit(row, next_first):
        nodes = [held[16 * n : 16 * n + 16] for n in range(NP)]
        for b in range(4):
            nodes[b] = nodes[b] + before[16 * b : 16 * b + 16]
            if next_first is not None:
                nodes[12 + b] = nodes[12 + b] + next_first[b]
        if emit_columns:
            along = [
                [
                    sum(float(HALVES[i, a] * ONE_D[a]) * nodes[4 * a + b] for a in range(4))
                    for b in range(4)
                ]
                for i in range(2)
            ]
            for i in range(2):
                for j in range(2):
                    out_ref[pl.ds(pl.multiple_of(row * 64 + (2 * i + j) * 16, 16), 16)] = sum(
                        float(HALVES[j, b] * ONE_D[b]) * along[i][b] for b in range(4)
                    )
        else:
            for a in range(4):
                at_row = pl.ds(16 * a + row, 1)
                for b in range(4):
                    n = 4 * a + b
                    values = nodes[n]
                    if b == 0:
                        values = values + jnp.where(
                            iota(values.shape, 0) == 0, hy_south[at_row], 0.0
                        )
                    if b == 3:
                        values = values + jnp.where(
                            iota(values.shape, 0) == 15, hy_north[at_row], 0.0
                        )
                    values = values * float(ONE_D[a] * ONE_D[b])
                    for f in range(fields):
                        turned[f, 16 * n : 16 * n + 16] = values[:, f * levels : (f + 1) * levels]
            for y in range(EYD):
                for f in range(fields):
                    out_ref[row * EYD + y, :, f * levels : (f + 1) * levels] = turned[
                        f, pl.ds(y, NP, stride=16)
                    ]

    before[...] = jnp.zeros_like(before)

    def one_row(row, _):
        operator = operator_block(
            ktt_ref[pl.ds(pl.multiple_of(row * 16, 16), 16)], range(NP), tiling, same_elem
        )
        at = pl.ds(pl.multiple_of(row * EYD, EYD), EYD)
        points = apply_operator(
            operator,
            hi_ref[at].reshape(EYD * NP, width),
            lo_ref[at].reshape(EYD * NP, width),
        )
        nodes = [points[16 * n : 16 * n + 16] for n in range(NP)]
        if not emit_columns:
            low = jnp.where(row == 0, 1.0, 0.0)
            high = jnp.where(row == EXD - 1, 1.0, 0.0)
            for b in range(4):
                rows = slice(16 * b, 16 * b + 16)
                nodes[b] = nodes[b] + hx_west[rows].astype(F32) * low
                nodes[12 + b] = nodes[12 + b] + hx_east[rows].astype(F32) * high
        for a in range(4):
            first, last = nodes[4 * a], nodes[4 * a + 3]
            nodes[4 * a] = first + shifted(last, 1)
            nodes[4 * a + 3] = last + shifted(first, -1)

        @pl.when(row > 0)
        def _():
            emit(row - 1, nodes[0:4])
            before[...] = held[192:256]

        for n in range(NP):
            held[16 * n : 16 * n + 16] = nodes[n]
        return 0

    lax.fori_loop(0, EXD, one_row, 0)
    emit(EXD - 1, None)


def rows_call(emit_columns, ktt, hi, lo, levels, halos=()):
    elements, _, width = hi.shape
    out = (
        jax.ShapeDtypeStruct((4 * elements, width), F32)
        if emit_columns
        else jax.ShapeDtypeStruct((elements, NP, width), F32)
    )
    scratch = [pltpu.VMEM((256, width), F32), pltpu.VMEM((64, width), F32)]
    if not emit_columns:
        scratch.append(pltpu.VMEM((width // levels, 256, levels), F32))
    return pl.pallas_call(
        functools.partial(row_kernel, emit_columns),
        out_shape=out,
        in_specs=[VMEM] * (3 + len(halos)),
        out_specs=VMEM,
        scratch_shapes=scratch,
        compiler_params=params(16),
        cost_estimate=cost(4e9, 2e7),
        name="column_rows" if emit_columns else "dynamics_rows",
    )(ktt, hi, lo, *halos)


def message_kernel(twice, west_ref, east_ref, south_ref, north_ref, table, to_south, to_north):
    both = jnp.concatenate([west_ref[...], east_ref[...]], axis=0)
    add = dot_twice(table[...], both) if twice else dot(table[...], both)
    to_south[...] = (south_ref[...] + add[0:64]).astype(BF16)
    to_north[...] = (north_ref[...] + add[64:128]).astype(BF16)


def messages(west, east, south, north, table):
    width = west.shape[1]
    return pl.pallas_call(
        functools.partial(message_kernel, table.shape[1] > 128),
        out_shape=(jax.ShapeDtypeStruct((64, width), BF16),) * 2,
        in_specs=[VMEM] * 5,
        out_specs=(VMEM,) * 2,
        compiler_params=params(16),
        cost_estimate=cost(4e7, 6e5),
        name="line_messages",
    )(west, east, south, north, table)


def ring(axis, step):
    count = lax.axis_size(axis)
    return [(i, (i + step) % count) for i in range(count)]


def exchange(axis, to_low, to_high):
    from_low = lax.ppermute(to_high, axis, ring(axis, 1))
    from_high = lax.ppermute(to_low, axis, ring(axis, -1))
    return from_low, from_high


def send_kernel(
    devices,
    span_y,
    columns_ref,
    west_ref,
    east_ref,
    south_ref,
    north_ref,
    table_ref,
    requested_ref,
    cell_ref,
    out_ref,
    place_ref,
    rounded,
):
    count = columns_ref.shape[0]
    per_peer = count // devices
    requested = requested_ref[:, 0, :]
    spread_out = one_hot((iota((128, count), 1) & (per_peer - 1)) == iota((128, count), 0))
    own = (iota((devices, count), 1) // per_peer) == iota((devices, count), 0)
    wide = dot((requested >> 5).astype(F32).astype(BF16), spread_out) * 32.0 + dot(
        (requested & 31).astype(F32).astype(BF16), spread_out
    )
    requested = jnp.sum(jnp.where(own, wide, 0.0), axis=0, keepdims=True).astype(I32)
    elements = cell_ref.shape[1]
    marks = one_hot((requested >> 2) == iota((elements, count), 0))
    tile_row = tile_number(cell_ref[...], span_y).astype(F32)
    tile_row = jnp.broadcast_to(tile_row, (8, elements)).astype(BF16)
    tile = dot(tile_row, marks)[0:1].astype(I32)
    place = (tile >> 4) * 64 + (requested & 3) * 16 + (tile & 15)
    place_ref[...] = place

    lines = jnp.concatenate([south_ref[...], north_ref[...]], axis=0)
    west = dot_twice(table_ref[count : count + 64, 0:128], west_ref[...])
    east = dot_twice(table_ref[count + 64 : count + 128, 0:128], east_ref[...])
    for start in range(0, count, 128):
        rows = slice(start, start + 128)
        values = columns_ref[rows] + dot_twice(table_ref[rows], lines)
        if start == 0:
            values = values + jnp.concatenate([west, jnp.zeros_like(west)], axis=0)
        if start == count - 128:
            values = values + jnp.concatenate([jnp.zeros_like(east), east], axis=0)
        rounded[rows] = values.astype(BF16)
    for start in range(0, count, 128):
        column = as_columns(place, start)
        pick = jnp.concatenate(
            [one_hot(column == iota((128, 128), 1) + other) for other in range(0, count, 128)],
            axis=1,
        )
        out_ref[start : start + 128] = dot(pick, rounded[...]).astype(BF16)


def send_columns(columns, halos, requested, cell, devices, span_y):
    count, width = columns.shape
    extra = np.concatenate(hi_lo_arrays(TABLES["col_x"]), axis=1)
    table = np.concatenate(hi_lo_arrays(TABLES["col_y"]), axis=1)
    table = np.concatenate([table, np.pad(extra, ((0, 0), (0, 128)))], axis=0)
    return pl.pallas_call(
        functools.partial(send_kernel, devices, span_y),
        out_shape=(
            jax.ShapeDtypeStruct((count, width), BF16),
            jax.ShapeDtypeStruct((1, count), I32),
        ),
        in_specs=[VMEM] * 8,
        out_specs=(VMEM,) * 2,
        scratch_shapes=[pltpu.VMEM((count, width), BF16)],
        compiler_params=params(16),
        cost_estimate=cost(2e9, 5e6),
        name="send_columns",
    )(columns, *halos, jnp.asarray(table), requested, cell)


def physics_kernel(fields, incoming_ref, q_ref, inverse_ref, out_ref, tendency):
    count, width = incoming_ref.shape
    levels = width // fields
    q = q_ref[...]
    for start in range(0, count, 128):
        column = as_columns(q, start)
        pick = jnp.concatenate(
            [one_hot(column == iota((128, 128), 1) + other) for other in range(0, count, 128)],
            axis=1,
        )
        physics = dot(pick, incoming_ref[...])
        for group in range(128 // GROUP_COLS):
            rows = physics[group * GROUP_COLS : (group + 1) * GROUP_COLS]
            stacked = jnp.concatenate(
                [rows[:, f * levels : (f + 1) * levels] for f in range(fields)], axis=0
            )
            inverse = inverse_ref[start // GROUP_COLS + group]
            result = dot_nt(stacked.astype(BF16), inverse) - stacked
            where = start + group * GROUP_COLS
            tendency[where : where + GROUP_COLS] = jnp.concatenate(
                [result[f * GROUP_COLS : (f + 1) * GROUP_COLS] for f in range(fields)], axis=1
            ).astype(BF16)
    for start in range(0, count, 128):
        pick = one_hot(q == iota((128, count), 0) + start)
        out_ref[start : start + 128] = dot(pick, tendency[...]).astype(BF16)


def physics_step(incoming, q, inverse, fields):
    count, width = incoming.shape
    return pl.pallas_call(
        functools.partial(physics_kernel, fields),
        out_shape=jax.ShapeDtypeStruct((count, width), BF16),
        in_specs=[VMEM] * 3,
        out_specs=VMEM,
        scratch_shapes=[pltpu.VMEM((count, width), BF16)],
        compiler_params=params(16),
        cost_estimate=cost(3e9, 5e6),
        name="physics",
    )(incoming, q, inverse)


def unpack_kernel(
    received_ref, place_ref, lines_table, back_ref, west_ref, east_ref, south_ref, north_ref
):
    count = received_ref.shape[0]
    place = place_ref[...]
    for start in range(0, count, 128):
        pick = one_hot(place == iota((128, count), 0) + start)
        back_ref[start : start + 128] = dot(pick, received_ref[...]).astype(BF16)
    west_ref[...] = back_ref[0:64]
    east_ref[...] = back_ref[count - 64 : count]
    lines = dot(lines_table[:, 0:count], back_ref[...]) + dot(
        lines_table[:, count : 2 * count], back_ref[...]
    )
    south_ref[...] = lines[0:64]
    north_ref[...] = lines[64:128]


def unpack(received, place):
    count, width = received.shape
    return pl.pallas_call(
        unpack_kernel,
        out_shape=(
            jax.ShapeDtypeStruct((count, width), BF16),
            jax.ShapeDtypeStruct((64, width), BF16),
            jax.ShapeDtypeStruct((64, width), BF16),
            jax.ShapeDtypeStruct((64, width), F32),
            jax.ShapeDtypeStruct((64, width), F32),
        ),
        in_specs=[VMEM] * 3,
        out_specs=(VMEM,) * 5,
        compiler_params=params(16),
        cost_estimate=cost(2e9, 4e6),
        name="unpack",
    )(received, place, hi_lo(TABLES["lines"]))


def inner_kernel(
    fields, span_y, cell_smem, dynamics_ref, back_ref, table_ref, out_ref, border_ref, total, buffer, sems
):
    elements, _, width = dynamics_ref.shape
    levels = width // fields
    count = back_ref.shape[0]
    depth = 192

    def near_sum(row, first, rows, skip):
        near = back_ref[pl.ds(first, rows)]
        sums = dot(table_ref[:, skip : skip + rows], near)
        sums = sums + dot(table_ref[:, depth + skip : depth + skip + rows], near)
        at = pl.ds(row * EYD, EYD)
        total[at] = dynamics_ref[at] + sums.reshape(EYD, NP, width)

    near_sum(0, 0, 128, 64)
    near_sum(EXD - 1, count - 128, 128, 0)

    def middle(row, _):
        near_sum(row, pl.multiple_of(row * 64 - 64, 64), 192, 0)
        return 0

    lax.fori_loop(1, EXD - 1, middle, 0)
    for kind in range(4):
        for k in range(16):
            tile = (k, (EXD - 1) * EYD + k, k * EYD, k * EYD + EYD - 1)[kind]
            for f in range(fields):
                border_ref[kind, f, k] = total[tile, :, f * levels : (f + 1) * levels]
    per = elements // CHUNKS

    def copy(chunk):
        return pltpu.make_async_copy(
            buffer.at[chunk], out_ref.at[:, pl.ds(chunk * per, per)], sems.at[chunk]
        )

    for chunk in range(CHUNKS):

        def take_slots(i, _, chunk=chunk):
            for u in range(4):
                k = i * 4 + u
                tile = tile_number(cell_smem[chunk * per + k], span_y)
                for f in range(fields):
                    buffer[chunk, f, k] = total[tile, :, f * levels : (f + 1) * levels]
            return 0

        lax.fori_loop(0, per // 4, take_slots, 0)
        copy(chunk).start()
    for chunk in range(CHUNKS):
        copy(chunk).wait()


def inner_sum(cell, dynamics, back, fields, span_y):
    elements, _, width = dynamics.shape
    levels = width // fields
    return pl.pallas_call(
        functools.partial(inner_kernel, fields, span_y),
        out_shape=(
            jax.ShapeDtypeStruct((fields, elements, NP, levels), F32),
            jax.ShapeDtypeStruct((4, fields, 16, NP, levels), F32),
        ),
        in_specs=[SMEM, VMEM, VMEM, VMEM],
        out_specs=(ANY, VMEM),
        scratch_shapes=[
            pltpu.VMEM((elements, NP, width), F32),
            pltpu.VMEM((CHUNKS, fields, elements // CHUNKS, NP, levels), F32),
            pltpu.SemaphoreType.DMA((CHUNKS,)),
        ],
        compiler_params=params(32),
        cost_estimate=cost(2e9, 2e7),
        name="inner_sum",
    )(cell, dynamics, back, hi_lo(TABLES["final"]))


def border_kernel(
    fields, slot_ref, west_ref, east_ref, south_ref, north_ref, border_ref, table_ref, _, out_ref, buffer, sem
):
    width = west_ref.shape[1]
    levels = width // fields
    adds = []
    for kind, ref in enumerate((west_ref, east_ref, south_ref, north_ref)):
        table = table_ref[kind * 256 : kind * 256 + 256]
        if kind < 2:
            add = dot_twice(table, ref[...])
        else:
            add = dot(table[:, 0:64], ref[...])
        adds.append(add.reshape(16, NP, width))
    for kind in range(4):
        for k in range(16):
            if kind >= 2 and k in (0, 15):
                continue
            add = adds[kind][k]
            if kind < 2 and k in (0, 15):
                add = add + adds[2 if k == 0 else 3][0 if kind == 0 else 15]
            for f in range(fields):
                buffer[kind, f, k] = border_ref[kind, f, k] + add[:, f * levels : (f + 1) * levels]
            tile = (k, (EXD - 1) * EYD + k, k * EYD, k * EYD + EYD - 1)[kind]
            pltpu.make_async_copy(
                buffer.at[kind, :, k], out_ref.at[:, slot_ref[0, tile]], sem.at[kind]
            ).start()
    for kind in range(4):
        part = buffer.at[kind] if kind < 2 else buffer.at[kind, :, 1:15]
        pltpu.make_async_copy(part, part, sem.at[kind]).wait()


def border_sum(slot, halos, border, out):
    fields, levels = out.shape[0], out.shape[3]
    table = jnp.asarray(TABLES["border"].astype(np.float32).astype(jnp.bfloat16))
    return pl.pallas_call(
        functools.partial(border_kernel, fields),
        out_shape=jax.ShapeDtypeStruct(out.shape, F32),
        in_specs=[SMEM] + [VMEM] * 6 + [ANY],
        out_specs=ANY,
        scratch_shapes=[
            pltpu.VMEM((4, fields, 16, NP, levels), F32),
            pltpu.SemaphoreType.DMA((4,)),
        ],
        input_output_aliases={7: 0},
        compiler_params=params(16),
        cost_estimate=cost(2e8, 4e6),
        name="border_sum",
    )(slot, *halos, border, table, out)


def regroup(blocks):
    return lax.all_to_all(blocks, ("gx", "gy"), split_axis=0, concat_axis=0, tiled=True)


def per_device(state_in, stiffness, elem_cell, group_column, group_inverse):
    fields, elements, _, levels = state_in.shape
    devices = lax.axis_size("gx") * lax.axis_size("gy")
    columns_dev = 4 * elements
    span_y = EYD * lax.axis_size("gy")

    wanted, q = requests(group_column.reshape(1, columns_dev), devices)
    requested = regroup(wanted)
    hi, lo, ktt, slot, to_west, to_east, south, north = front(
        elem_cell, stiffness.reshape(NP * NP, elements), state_in, span_y
    )
    hx = exchange("gx", to_west, to_east)
    columns = rows_call(True, ktt, hi, lo, levels)
    corner = jnp.asarray(TABLES["corner_pt"].astype(np.float32).astype(jnp.bfloat16))
    hy = exchange("gy", *messages(*hx, south, north, corner))

    outgoing, place = send_columns(
        columns, (*hx, *hy), requested, elem_cell.reshape(1, elements), devices, span_y
    )
    incoming = regroup(outgoing)
    halos = (*hx, hy[0].astype(F32), hy[1].astype(F32))
    dynamics = rows_call(False, ktt, hi, lo, levels, halos)
    incoming, dynamics = lax.optimization_barrier((incoming, dynamics))
    received = regroup(physics_step(incoming, q, group_inverse, fields))

    back, west, east, south, north = unpack(received, place)
    bx = exchange("gx", west, east)
    by = exchange("gy", *messages(*bx, south, north, hi_lo(TABLES["corner_col"])))
    inner, border = inner_sum(elem_cell, dynamics, back, fields, span_y)
    return border_sum(slot, (*bx, *by), border, inner)


def solution(mesh):
    placed = (
        P(None, ("gx", "gy"), None, None),
        P(None, None, ("gx", "gy")),
        P(("gx", "gy")),
        P(("gx", "gy")),
        P(("gx", "gy"), None, None),
    )
    return jax.shard_map(
        per_device,
        mesh=mesh,
        in_specs=placed,
        out_specs=P(None, ("gx", "gy"), None, None),
        check_vma=False,
    )
```

```python
import functools
import math

import jax
import jax.numpy as jnp
import numpy as np
from jax import lax
from jax.experimental import pallas as pl
from jax.experimental.pallas import tpu as pltpu
from jax.sharding import PartitionSpec as P

GROUP_COLS = 16
EXD = 16
EYD = 16
NP = 16
F32 = jnp.float32
BF16 = jnp.bfloat16
I32 = jnp.int32
MB = 1024 * 1024


def lagrange_value(node_index, position, gll_nodes):
    running = 1.0
    for other_index in range(4):
        if other_index != node_index:
            running = (
                running
                * (position - gll_nodes[other_index])
                / (gll_nodes[node_index] - gll_nodes[other_index])
            )
    return running


def half_tables():
    gll_nodes = [-1.0, -1.0 / math.sqrt(5.0), 1.0 / math.sqrt(5.0), 1.0]
    halves = np.zeros((2, 4))
    for half_index, (lower_end, upper_end) in enumerate(((-1.0, 0.0), (0.0, 1.0))):
        centre = 0.5 * (lower_end + upper_end)
        offset = 0.5 * (upper_end - lower_end) / math.sqrt(3.0)
        for node in range(4):
            first = lagrange_value(node, centre - offset, gll_nodes)
            second = lagrange_value(node, centre + offset, gll_nodes)
            halves[half_index, node] = 0.5 * (upper_end - lower_end) * (first + second)
    product = halves @ halves.T
    determinant = product[0, 0] * product[1, 1] - product[0, 1] * product[1, 0]
    inverse = (
        np.array([[product[1, 1], -product[0, 1]], [-product[1, 0], product[0, 0]]]) / determinant
    )
    spread = halves.T @ inverse
    return halves.astype(np.float32), spread.astype(np.float32)


HALVES, SPREAD = half_tables()
ONE_D = np.array([0.5, 1.0, 1.0, 0.5])


def shift_down(n):
    return np.eye(n, k=-1)


def local_pass(n):
    table = np.einsum("ab,xy->axby", np.eye(4), np.eye(n))
    table[0, :, 3, :] += shift_down(n)
    table[3, :, 0, :] += shift_down(n).T
    return table


def constant_tables():
    h = HALVES.astype(np.float64)
    s = SPREAD.astype(np.float64)
    w = ONE_D
    eye = np.eye(EXD)
    line = local_pass(EYD)
    col_x = []
    for a in (0, 3):
        col_x.append(
            np.einsum("i,jb,b,byez->ijyez", h[:, a] * w[a], h, w, line).reshape(4 * EYD, 4 * EYD)
        )
    col_y = np.zeros((EXD, 2, 2, EYD, 2, 4, EXD))
    for side, (b, y) in enumerate(((0, 0), (3, EYD - 1))):
        col_y[:, :, :, y, side] = np.einsum("ia,j,xz->xijaz", h * w, h[:, b] * w[b], eye)
    col_y = col_y.reshape(EXD * 4 * EYD, 2 * 4 * EXD)
    nodes = np.einsum("ai,bj,yz->abyijz", s, s, np.eye(EYD))
    across = np.zeros((4, 4, EYD, 3, 2, 2, EYD))
    across[:, :, :, 1] = nodes
    across[0, :, :, 0] = nodes[3]
    across[3, :, :, 2] = nodes[0]
    full = np.einsum("byez,aezdijt->abydijt", line, across)
    full = full * w[:, None, None, None, None, None, None] * w[:, None, None, None, None, None]
    final = full.reshape(NP * EYD, 3 * 4 * EYD)
    along = local_pass(EXD)
    lines = np.zeros((2, 4, EXD, EXD, 2, 2, EYD))
    corner_col = np.zeros((2, 4, EXD, 2, 2, 2, EYD))
    corner_pt = np.zeros((2, 4, EXD, 2, 4, EYD))
    for side, (b, y) in enumerate(((0, 0), (3, EYD - 1))):
        lines[side, :, :, :, :, :, y] = np.einsum("axcz,ci,j->axzij", along, s, s[b])
        corner_col[side, 0, 0, 0, :, :, y] = np.outer(s[3], s[b])
        corner_col[side, 3, EXD - 1, 1, :, :, y] = np.outer(s[0], s[b])
        corner_pt[side, 0, 0, 0, b, y] = 1.0
        corner_pt[side, 3, EXD - 1, 1, b, y] = 1.0
    lines = lines.reshape(2 * 4 * EXD, EXD * 4 * EYD)
    corner_col = corner_col.reshape(2 * 4 * EXD, 2 * 4 * EYD)
    corner_pt = corner_pt.reshape(2 * 4 * EXD, 2 * 4 * EYD)
    border = np.zeros((4, EYD, NP, 128))
    order = full.transpose(2, 0, 1, 3, 4, 5, 6).reshape(EYD, NP, 3, 4 * EYD)
    west, east = hi_lo_arrays(order[:, :, 0]), hi_lo_arrays(order[:, :, 2])
    border[0] = np.concatenate(west, axis=-1)
    border[1] = np.concatenate(east, axis=-1)
    for side, b in enumerate((0, 3)):
        for a in range(4):
            for x in range(EXD):
                border[2 + side, x, 4 * a + b, 16 * a + x] = w[a] * w[b]
    return dict(
        col_x=np.concatenate(col_x, axis=0),
        col_y=col_y,
        final=order.reshape(EYD * NP, 3 * 4 * EYD),
        lines=lines,
        corner_col=corner_col,
        corner_pt=corner_pt,
        border=border.reshape(4 * EYD * NP, 128),
    )


def hi_lo_arrays(table):
    hi = np.asarray(table, np.float32).astype(jnp.bfloat16)
    lo = (np.asarray(table, np.float32) - hi.astype(np.float32)).astype(jnp.bfloat16)
    return hi, lo


def hi_lo(table):
    return jnp.asarray(np.concatenate(hi_lo_arrays(table), axis=1))


TABLES = constant_tables()


def dot(left, right):
    return jnp.dot(left, right, preferred_element_type=F32)


def dot_nt(left, right):
    return lax.dot_general(left, right, (((1,), (1,)), ((), ())), preferred_element_type=F32)


def dot_twice(table, right):
    return dot(table, jnp.concatenate([right, right], axis=0))


def split(values):
    hi = values.astype(BF16)
    return hi, (values - hi.astype(F32)).astype(BF16)


def iota(shape, dim):
    return lax.broadcasted_iota(I32, shape, dim)


def one_hot(condition):
    return jnp.where(condition, 1.0, 0.0).astype(BF16)


def as_columns(row, start):
    piece = row[:, start : start + 128].astype(F32)
    return jnp.transpose(jnp.broadcast_to(piece, (128, 128))).astype(I32)


def tile_number(cell, span_y):
    shift = span_y.bit_length() - 1
    assert span_y == 1 << shift
    return ((cell >> shift) & (EXD - 1)) * EYD + (cell & (EYD - 1))


VMEM = pl.BlockSpec(memory_space=pltpu.VMEM)
SMEM = pl.BlockSpec(memory_space=pltpu.SMEM)
ANY = pl.BlockSpec(memory_space=pl.ANY)


def params(mib):
    return pltpu.CompilerParams(vmem_limit_bytes=mib * MB)


def cost(flops, moved):
    return pl.CostEstimate(flops=int(flops), bytes_accessed=int(moved), transcendentals=0)


def column_requests(devices, per_peer, group):
    columns_dev = devices * per_peer
    shift = columns_dev.bit_length() - 1
    source = group >> shift
    local = group & (columns_dev - 1)
    of_source = source == iota((devices, columns_dev), 0)
    marks = one_hot(of_source)
    upper = one_hot(iota((128, 128), 0) <= iota((128, 128), 1))
    before = jnp.zeros((devices, 1), F32)
    ranks = []
    for start in range(0, columns_dev, 128):
        piece = marks[:, start : start + 128]
        counts = dot(piece, upper) + before
        ranks.append(counts)
        before = counts[:, 127:128]
    counts = jnp.concatenate(ranks, axis=1)
    rank = jnp.sum(jnp.where(of_source, counts, 0.0), axis=0, keepdims=True).astype(I32) - 1
    of_rank = one_hot(rank == iota((128, columns_dev), 0))
    high = jnp.where(of_source, (local >> 5).astype(F32), 0.0).astype(BF16)
    low = jnp.where(of_source, (local & 31).astype(F32), 0.0).astype(BF16)
    wanted = dot_nt(high, of_rank) * 32.0 + dot_nt(low, of_rank)
    return wanted, source * per_peer + rank


def diagonal(sizes, step_x, step_y):
    count_x, count_y = sizes
    x = lax.rem(lax.axis_index("gx") + step_x + count_x, count_x)
    y = lax.rem(lax.axis_index("gy") + step_y + count_y, count_y)
    return x * count_y + y


CHUNKS = 8


def state_copy(state_ref, raw, sems, chunk):
    per = raw.shape[2]
    return pltpu.make_async_copy(
        state_ref.at[:, pl.ds(chunk * per, per)], raw.at[chunk], sems.at[chunk]
    )


def tile_operators(span_y, cell, stiff):
    elements = cell.shape[1]
    marks = one_hot(tile_number(cell, span_y) == iota((elements, elements), 0))
    row = iota(stiff.shape, 0)
    stiff = stiff + jnp.where((row >> 4) == (row & 15), 1.0, 0.0)
    hi, lo = split(stiff)
    return dot_nt(marks, hi), dot_nt(marks, lo)


def place_operators(parts, operators):
    row, col = iota((256, 256), 0), iota((256, 256), 1)
    same_elem = one_hot((row & 15) == (col >> 4))
    tiling = one_hot((row & 15) == (col & 15))
    column = iota((EYD, 256), 1) >> 4
    for x in range(EXD):
        stacked = jnp.concatenate(
            [
                jnp.where(column == n, part[x * EYD : (x + 1) * EYD], 0.0).astype(BF16)
                for part in parts
                for n in range(NP)
            ],
            axis=0,
        )
        placed = dot(stacked, tiling).astype(BF16)
        operators[x, 0:256] = placed[0:256] * same_elem
        operators[x, 256:512] = placed[256:512] * same_elem


def place_states(span_y, cell_smem, state_ref, raw, sems, hi_ref, lo_ref):
    fields, per, _, levels = raw.shape[1:]
    for chunk in range(CHUNKS):
        state_copy(state_ref, raw, sems, chunk).wait()

        def place_slots(i, _, chunk=chunk):
            for u in range(4):
                k = i * 4 + u
                where = tile_number(cell_smem[chunk * per + k], span_y)
                for f in range(fields):
                    hi, lo = split(raw[chunk, f, k])
                    hi_ref[where, :, f * levels : (f + 1) * levels] = hi
                    lo_ref[where, :, f * levels : (f + 1) * levels] = lo
            return 0

        lax.fori_loop(0, per // 4, place_slots, 0)


def row_points(row, operators, hi_ref, lo_ref):
    width = hi_ref.shape[2]
    at = pl.ds(pl.multiple_of(row * EYD, EYD), EYD)
    hi = hi_ref[at].reshape(EYD * NP, width)
    lo = lo_ref[at].reshape(EYD * NP, width)
    both = dot(operators[row], hi)
    return both[0:256] + both[256:512] + dot(operators[row, 0:256], lo)


def shifted(values, step):
    rows = values.shape[0]
    moved = pltpu.roll(values, step % rows, 0)
    free = 0 if step > 0 else rows - 1
    return jnp.where(iota(values.shape, 0) == free, 0.0, moved)


def sum_along_y(nodes):
    for a in range(4):
        first, last = nodes[4 * a], nodes[4 * a + 3]
        nodes[4 * a] = first + shifted(last, 1)
        nodes[4 * a + 3] = last + shifted(first, -1)


def held_nodes(held, before, next_first):
    nodes = [held[16 * n : 16 * n + 16] for n in range(NP)]
    for b in range(4):
        nodes[b] = nodes[b] + before[16 * b : 16 * b + 16]
        if next_first is not None:
            nodes[12 + b] = nodes[12 + b] + next_first[b]
    return nodes


def front_kernel(
    sizes,
    span_y,
    cell_smem,
    cell_ref,
    group_ref,
    stiff_ref,
    state_ref,
    columns_out,
    blocks_ref,
    q_ref,
    x_one,
    x_two,
    y_one,
    y_two,
    raw,
    sems,
    hi_ref,
    lo_ref,
    operators,
    held,
    before,
    lines,
    ends,
    columns,
    out_sem,
):
    devices = sizes[0] * sizes[1]
    width = held.shape[1]
    for chunk in range(CHUNKS):
        state_copy(state_ref, raw, sems, chunk).start()
    place_operators(tile_operators(span_y, cell_ref[...], stiff_ref[...]), operators)
    wanted, q_ref[...] = column_requests(
        devices, group_ref.shape[1] // devices, group_ref[...]
    )
    blocks_ref[...] = jnp.broadcast_to(wanted[:, None, :], (devices, 8, 128))
    place_states(span_y, cell_smem, state_ref, raw, sems, hi_ref, lo_ref)
    before[...] = jnp.zeros_like(before)
    held[...] = jnp.zeros_like(held)

    def emit(row, next_first):
        nodes = held_nodes(held, before, next_first)
        along = [
            [
                sum(float(HALVES[i, a] * ONE_D[a]) * nodes[4 * a + b] for a in range(4))
                for b in range(4)
            ]
            for i in range(2)
        ]
        for i in range(2):
            for j in range(2):
                columns[pl.ds(pl.multiple_of(row * 64 + (2 * i + j) * 16, 16), 16)] = sum(
                    float(HALVES[j, b] * ONE_D[b]) * along[i][b] for b in range(4)
                )

    def one_row(row, _):
        points = row_points(row, operators, hi_ref, lo_ref)

        ends[0, jnp.minimum(row, 1)] = points[0:64]
        ends[1, jnp.maximum(row - EXD + 2, 0)] = points[192:256]
        nodes = [points[16 * n : 16 * n + 16] for n in range(NP)]
        for a in range(4):
            lines[0, pl.ds(16 * a + row, 1)] = nodes[4 * a][0:1]
            lines[1, pl.ds(16 * a + row, 1)] = nodes[4 * a + 3][15:16]
        sum_along_y(nodes)
        emit(jnp.maximum(row - 1, 0), nodes[0:4])
        before[...] = held[192:256]
        for n in range(NP):
            held[16 * n : 16 * n + 16] = nodes[n]
        return 0

    def send(part):
        rows = pl.ds(part * (columns.shape[0] // 2), columns.shape[0] // 2)
        return pltpu.make_async_copy(columns.at[rows], columns_out.at[rows], out_sem.at[part])

    lax.fori_loop(0, EXD // 2 + 2, one_row, 0, unroll=2)
    send(0).start()
    lax.fori_loop(EXD // 2 + 2, EXD, one_row, 0, unroll=2)
    emit(EXD - 1, None)
    send(1).start()
    whole = []
    for side in range(2):
        first, last = lines[side, 0:16], lines[side, 48:64]
        whole.append(
            jnp.concatenate(
                [first + shifted(last, 1), lines[side, 16:48], last + shifted(first, -1)], axis=0
            )
        )
    for axis, low, high, one, two in (
        ("gx", ends[0, 0], ends[1, 1], x_one, x_two),
        ("gy", whole[0], whole[1], y_one, y_two),
    ):
        first, second = by_parity(axis, low, high)
        one[...] = first.astype(BF16)
        two[...] = second.astype(BF16)
    for step_x, row in ((-1, 0), (1, 3 * 16 + 15)):
        for step_y, side in ((-1, 0), (1, 1)):
            block = diagonal(sizes, step_x, step_y)
            point = lines[side, row : row + 1]
            for f in range(width // 128):
                blocks_ref[block, 1 + f : 2 + f] = point[:, f * 128 : (f + 1) * 128]
    send(0).wait()
    send(1).wait()


def state_scratch(fields, elements, levels):
    width = fields * levels
    return [
        pltpu.VMEM((CHUNKS, fields, elements // CHUNKS, NP, levels), F32),
        pltpu.SemaphoreType.DMA((CHUNKS,)),
        pltpu.VMEM((elements, NP, width), BF16),
        pltpu.VMEM((elements, NP, width), BF16),
        pltpu.VMEM((EXD, 512, 256), BF16),
        pltpu.VMEM((256, width), F32),
        pltpu.VMEM((64, width), F32),
    ]


FRONT_LIMIT = 56


def front(cell, group, stiff, state, sizes):
    fields, elements, _, levels = state.shape
    width = fields * levels
    devices = sizes[0] * sizes[1]
    line = jax.ShapeDtypeStruct((64, width), BF16)
    return pl.pallas_call(
        functools.partial(front_kernel, sizes, EYD * sizes[1]),
        out_shape=(
            jax.ShapeDtypeStruct((4 * elements, width), F32),
            jax.ShapeDtypeStruct((devices, 8, 128), F32),
            jax.ShapeDtypeStruct((1, 4 * elements), I32),
            line,
            line,
            line,
            line,
        ),
        in_specs=[SMEM, VMEM, VMEM, VMEM, ANY],
        out_specs=(ANY,) + (VMEM,) * 6,
        scratch_shapes=state_scratch(fields, elements, levels)
        + [
            pltpu.VMEM((2, 64, width), F32),
            pltpu.VMEM((2, 2, 64, width), F32),
            pltpu.VMEM((4 * elements, width), F32),
            pltpu.SemaphoreType.DMA((2,)),
        ],
        compiler_params=params(FRONT_LIMIT),
        cost_estimate=cost(4e9, 2e7),
        name="front",
    )(cell, cell.reshape(1, elements), group, stiff, state)


def dynamics_kernel(
    span_y,
    cell_smem,
    cell_ref,
    stiff_ref,
    state_ref,
    hx_one,
    hx_two,
    hy_south,
    hy_north,
    out_ref,
    raw,
    sems,
    hi_ref,
    lo_ref,
    operators,
    held,
    before,
    turned,
    hx,
    rows_out,
    out_sems,
):
    hx[0], hx[1] = from_neighbours("gx", hx_one[...].astype(F32), hx_two[...].astype(F32))
    fields, _, levels = turned.shape
    for chunk in range(CHUNKS):
        state_copy(state_ref, raw, sems, chunk).start()
    place_operators(tile_operators(span_y, cell_ref[...], stiff_ref[...]), operators)
    place_states(span_y, cell_smem, state_ref, raw, sems, hi_ref, lo_ref)
    before[...] = jnp.zeros_like(before)
    held[...] = jnp.zeros_like(held)

    def emit(row, next_first):
        nodes = held_nodes(held, before, next_first)
        for a in range(4):
            at_row = pl.ds(16 * a + row, 1)
            for b in range(4):
                n = 4 * a + b
                values = nodes[n]
                if b == 0:
                    values = values + jnp.where(iota(values.shape, 0) == 0, hy_south[at_row], 0.0)
                if b == 3:
                    values = values + jnp.where(iota(values.shape, 0) == 15, hy_north[at_row], 0.0)
                values = values * float(ONE_D[a] * ONE_D[b])
                for f in range(fields):
                    turned[f, 16 * n : 16 * n + 16] = values[:, f * levels : (f + 1) * levels]
        slot = row & 1
        for y in range(EYD):
            for f in range(fields):
                rows_out[slot, y, :, f * levels : (f + 1) * levels] = turned[
                    f, pl.ds(y, NP, stride=16)
                ]

    def copy_out(row):
        slot = row & 1
        return pltpu.make_async_copy(
            rows_out.at[slot], out_ref.at[pl.ds(row * EYD, EYD)], out_sems.at[slot]
        )

    def one_row(row, _):
        points = row_points(row, operators, hi_ref, lo_ref)
        nodes = [points[16 * n : 16 * n + 16] for n in range(NP)]
        low = jnp.where(row == 0, 1.0, 0.0)
        high = jnp.where(row == EXD - 1, 1.0, 0.0)
        for b in range(4):
            rows = slice(16 * b, 16 * b + 16)
            nodes[b] = nodes[b] + hx[0, rows] * low
            nodes[12 + b] = nodes[12 + b] + hx[1, rows] * high
        sum_along_y(nodes)

        @pl.when(row >= 3)
        def _():
            copy_out(row - 3).wait()

        @pl.when(row >= 1)
        def _():
            emit(row - 1, nodes[0:4])
            copy_out(row - 1).start()

        before[...] = held[192:256]
        for n in range(NP):
            held[16 * n : 16 * n + 16] = nodes[n]
        return 0

    lax.fori_loop(0, EXD, one_row, 0)
    copy_out(EXD - 3).wait()
    emit(EXD - 1, None)
    copy_out(EXD - 1).start()
    copy_out(EXD - 2).wait()
    copy_out(EXD - 1).wait()


def dynamics_rows(cell, stiff, state, span_y, halos):
    fields, elements, _, levels = state.shape
    width = fields * levels
    return pl.pallas_call(
        functools.partial(dynamics_kernel, span_y),
        out_shape=jax.ShapeDtypeStruct((elements, NP, width), F32),
        in_specs=[SMEM, VMEM, VMEM, ANY] + [VMEM] * 4,
        out_specs=ANY,
        scratch_shapes=state_scratch(fields, elements, levels)
        + [
            pltpu.VMEM((fields, 256, levels), F32),
            pltpu.VMEM((2, 64, width), F32),
            pltpu.VMEM((2, EYD, NP, width), F32),
            pltpu.SemaphoreType.DMA((2,)),
        ],
        compiler_params=params(DYN_LIMIT),
        cost_estimate=cost(4e9, 2e7),
        name="dynamics_rows",
    )(cell, cell.reshape(1, elements), stiff, state, *halos)


def message_kernel(x_one, x_two, south_ref, north_ref, table, y_one, y_two):
    both = jnp.concatenate(from_neighbours("gx", x_one[...], x_two[...]), axis=0)
    add = dot_twice(table[...], both)
    one, two = by_parity("gy", south_ref[...] + add[0:64], north_ref[...] + add[64:128])
    y_one[...] = one.astype(BF16)
    y_two[...] = two.astype(BF16)


def messages(one, two, south, north, table):
    width = one.shape[1]
    return pl.pallas_call(
        message_kernel,
        out_shape=(jax.ShapeDtypeStruct((64, width), BF16),) * 2,
        in_specs=[VMEM] * 5,
        out_specs=(VMEM,) * 2,
        compiler_params=params(16),
        cost_estimate=cost(4e7, 6e5),
        name="line_messages",
    )(one, two, south, north, table)


def pairs(axis, first):
    count = lax.axis_size(axis)
    low = range(0 if first else 1, count, 2)
    return [(i, (i + 1) % count) for i in low] + [((i + 1) % count, i) for i in low]


def exchange(axis, one, two):
    return (
        lax.ppermute(one, axis, pairs(axis, True)),
        lax.ppermute(two, axis, pairs(axis, False)),
    )


def by_parity(axis, to_low, to_high):
    even = (lax.axis_index(axis) & 1) == 0
    return jnp.where(even, to_high, to_low), jnp.where(even, to_low, to_high)


def from_neighbours(axis, one, two):
    even = (lax.axis_index(axis) & 1) == 0
    return jnp.where(even, two, one), jnp.where(even, one, two)


def send_kernel(
    sizes,
    span_y,
    columns_hbm,
    table_hbm,
    x_one,
    x_two,
    y_one,
    y_two,
    blocks_ref,
    cell_ref,
    out_ref,
    place_ref,
    whole_south,
    whole_north,
    columns_ref,
    table_ref,
    rounded,
    pick,
    sems,
):
    count, width = columns_ref.shape
    devices = sizes[0] * sizes[1]
    per_peer = count // devices
    table_copy = pltpu.make_async_copy(table_hbm, table_ref, sems.at[0])
    table_copy.start()
    copy = pltpu.make_async_copy(columns_hbm, columns_ref, sems.at[1])
    copy.start()
    requested = blocks_ref[:, 0, :].astype(I32)
    spread_out = one_hot((iota((128, count), 1) & (per_peer - 1)) == iota((128, count), 0))
    shift = per_peer.bit_length() - 1
    own = (iota((devices, count), 1) >> shift) == iota((devices, count), 0)
    wide = dot((requested >> 5).astype(F32).astype(BF16), spread_out) * 32.0 + dot(
        (requested & 31).astype(F32).astype(BF16), spread_out
    )
    requested = jnp.sum(jnp.where(own, wide, 0.0), axis=0, keepdims=True).astype(I32)
    elements = cell_ref.shape[1]
    marks = one_hot((requested >> 2) == iota((elements, count), 0))
    tile_row = tile_number(cell_ref[...], span_y).astype(F32)
    tile_row = jnp.broadcast_to(tile_row, (8, elements)).astype(BF16)
    tile = dot(tile_row, marks)[0:1].astype(I32)
    place = (tile >> 4) * 64 + (requested & 3) * 16 + (tile & 15)
    place_ref[...] = place
    for start in range(0, count, 128):
        column = as_columns(place, start)
        for other in range(0, count, 128):
            pick[start : start + 128, other : other + 128] = one_hot(
                column == iota((128, 128), 1) + other
            )

    south, north = from_neighbours("gy", y_one[...].astype(F32), y_two[...].astype(F32))
    for ref, line, step_y in ((whole_south, south, -1), (whole_north, north, 1)):
        ref[...] = line
        for step_x, row in ((-1, 0), (1, 63)):
            block = diagonal(sizes, step_x, step_y)
            for f in range(width // 128):
                ref[row : row + 1, f * 128 : (f + 1) * 128] += blocks_ref[block, 1 + f : 2 + f]
    lines = jnp.concatenate([whole_south[...], whole_north[...]], axis=0).astype(BF16)
    west, east = from_neighbours("gx", x_one[...], x_two[...])
    table_copy.wait()
    west = dot_twice(table_ref[count : count + 64, 0:128], west)
    east = dot_twice(table_ref[count + 64 : count + 128, 0:128], east)
    add = dot_twice(table_ref[0:count], lines)
    copy.wait()
    rounded[...] = (columns_ref[...] + add).astype(BF16)
    rounded[0:64] = (columns_ref[0:64] + add[0:64] + west).astype(BF16)
    rounded[count - 64 : count] = (
        columns_ref[count - 64 : count] + add[count - 64 : count] + east
    ).astype(BF16)
    out_ref[...] = dot(pick[...], rounded[...]).astype(BF16)


def send_columns(columns, halos, blocks, cell, sizes):
    count, width = columns.shape
    extra = np.concatenate(hi_lo_arrays(TABLES["col_x"]), axis=1)
    table = np.concatenate(hi_lo_arrays(TABLES["col_y"]), axis=1)
    table = np.concatenate([table, np.pad(extra, ((0, 0), (0, 128)))], axis=0)
    return pl.pallas_call(
        functools.partial(send_kernel, sizes, EYD * sizes[1]),
        out_shape=(
            jax.ShapeDtypeStruct((count, width), BF16),
            jax.ShapeDtypeStruct((1, count), I32),
            jax.ShapeDtypeStruct((64, width), F32),
            jax.ShapeDtypeStruct((64, width), F32),
        ),
        in_specs=[ANY, ANY] + [VMEM] * 6,
        out_specs=(VMEM,) * 4,
        scratch_shapes=[
            pltpu.VMEM((count, width), F32),
            pltpu.VMEM(table.shape, BF16),
            pltpu.VMEM((count, width), BF16),
            pltpu.VMEM((count, count), BF16),
            pltpu.SemaphoreType.DMA((2,)),
        ],
        compiler_params=params(SEND_LIMIT),
        cost_estimate=cost(2e9, 5e6),
        name="send_columns",
    )(columns, jnp.asarray(table), *halos, blocks, cell)


SEND_LIMIT = 60
DYN_LIMIT = 56


def physics_kernel(
    fields, incoming_ref, q_ref, inverse_hbm, out_ref, inverse, pick, physics, tendency, sem
):
    count, width = incoming_ref.shape
    levels = width // fields
    copy = pltpu.make_async_copy(inverse_hbm, inverse, sem)
    copy.start()
    q = q_ref[...]
    for start in range(0, count, 128):
        column = as_columns(q, start)
        for other in range(0, count, 128):
            pick[start : start + 128, other : other + 128] = one_hot(
                column == iota((128, 128), 1) + other
            )
    physics[...] = dot(pick[...], incoming_ref[...])
    copy.wait()
    for start in range(0, count, 128):
        pick[start : start + 128] = one_hot(q == iota((128, count), 0) + start)
    for group in range(count // GROUP_COLS):
        at = slice(group * GROUP_COLS, (group + 1) * GROUP_COLS)
        stacked = jnp.concatenate(
            [physics[at, f * levels : (f + 1) * levels] for f in range(fields)], axis=0
        )
        result = dot_nt(stacked.astype(BF16), inverse[group]) - stacked
        tendency[at] = jnp.concatenate(
            [result[f * GROUP_COLS : (f + 1) * GROUP_COLS] for f in range(fields)], axis=1
        ).astype(BF16)
    out_ref[...] = dot(pick[...], tendency[...]).astype(BF16)


def physics_step(incoming, q, inverse, fields):
    count, width = incoming.shape
    return pl.pallas_call(
        functools.partial(physics_kernel, fields),
        out_shape=jax.ShapeDtypeStruct((count, width), BF16),
        in_specs=[VMEM, VMEM, ANY],
        out_specs=VMEM,
        scratch_shapes=[
            pltpu.VMEM(inverse.shape, BF16),
            pltpu.VMEM((count, count), BF16),
            pltpu.VMEM((count, width), F32),
            pltpu.VMEM((count, width), BF16),
            pltpu.SemaphoreType.DMA,
        ],
        compiler_params=params(PHYSICS_LIMIT),
        cost_estimate=cost(3e9, 5e6),
        name="physics",
    )(incoming, q, inverse)


PHYSICS_LIMIT = 16


def unpack_kernel(
    received_ref,
    place_ref,
    lines_table,
    back_ref,
    x_one,
    x_two,
    south_ref,
    north_ref,
    pick,
):
    count = received_ref.shape[0]
    place = place_ref[...]
    for start in range(0, count, 128):
        pick[start : start + 128] = one_hot(place == iota((128, count), 0) + start)
    back_ref[...] = dot(pick[...], received_ref[...]).astype(BF16)
    x_one[...], x_two[...] = by_parity("gx", back_ref[0:64], back_ref[count - 64 : count])
    lines = dot(lines_table[...], back_ref[...])
    south_ref[...] = lines[0:64] + lines[128:192]
    north_ref[...] = lines[64:128] + lines[192:256]


def unpack(received, place):
    count, width = received.shape
    table = jnp.asarray(np.concatenate(hi_lo_arrays(TABLES["lines"]), axis=0))
    return pl.pallas_call(
        unpack_kernel,
        out_shape=(
            jax.ShapeDtypeStruct((count, width), BF16),
            jax.ShapeDtypeStruct((64, width), BF16),
            jax.ShapeDtypeStruct((64, width), BF16),
            jax.ShapeDtypeStruct((64, width), F32),
            jax.ShapeDtypeStruct((64, width), F32),
        ),
        in_specs=[VMEM] * 3,
        out_specs=(VMEM,) * 5,
        scratch_shapes=[pltpu.VMEM((count, count), BF16)],
        compiler_params=params(16),
        cost_estimate=cost(2e9, 4e6),
        name="unpack",
    )(received, place, table)


def inner_kernel(
    span_y,
    cell_smem,
    dynamics_ref,
    back_ref,
    table_ref,
    out_ref,
    border_ref,
    slot_ref,
    total,
    buffer,
    sems,
):
    elements, _, width = total.shape
    fields, levels = buffer.shape[1], buffer.shape[4]
    count = back_ref.shape[0]

    def near_sum(row, first, rows, skip):
        near = back_ref[pl.ds(first, rows)]
        both = dot(table_ref[:, skip : skip + rows], near)
        at = pl.ds(row * EYD, 2 * EYD)
        sums = both[0:512] + both[512:1024]
        total[at] = dynamics_ref[at] + sums.reshape(2 * EYD, NP, width)

    near_sum(0, 0, 192, 64)
    near_sum(EXD - 2, count - 192, 192, 0)

    def middle(pair, _):
        near_sum(pair * 2, pl.multiple_of(pair * 128 - 64, 64), 256, 0)
        return 0

    lax.fori_loop(1, EXD // 2 - 1, middle, 0, unroll=2)
    for kind in range(4):
        for k in range(16):
            tile = (k, (EXD - 1) * EYD + k, k * EYD, k * EYD + EYD - 1)[kind]
            for f in range(fields):
                border_ref[kind, f, k] = total[tile, :, f * levels : (f + 1) * levels]
    per = elements // CHUNKS

    def copy(chunk):
        return pltpu.make_async_copy(
            buffer.at[chunk], out_ref.at[:, pl.ds(chunk * per, per)], sems.at[chunk]
        )

    for chunk in range(CHUNKS):

        def take_slots(i, _, chunk=chunk):
            for u in range(4):
                k = i * 4 + u
                tile = tile_number(cell_smem[chunk * per + k], span_y)
                slot_ref[0, tile] = chunk * per + k
                for f in range(fields):
                    buffer[chunk, f, k] = total[tile, :, f * levels : (f + 1) * levels]
            return 0

        lax.fori_loop(0, per // 4, take_slots, 0)
        copy(chunk).start()
    for chunk in range(CHUNKS):
        copy(chunk).wait()


def inner_sum(cell, dynamics, back, fields, span_y):
    elements, _, width = dynamics.shape
    levels = width // fields
    one = TABLES["final"].reshape(EYD * NP, 3, 64)
    two = np.zeros((2, EYD * NP, 4, 64))
    two[0, :, 0:3] = one
    two[1, :, 1:4] = one
    table = np.concatenate(hi_lo_arrays(two.reshape(2 * EYD * NP, 256)), axis=0)
    return pl.pallas_call(
        functools.partial(inner_kernel, span_y),
        out_shape=(
            jax.ShapeDtypeStruct((fields, elements, NP, levels), F32),
            jax.ShapeDtypeStruct((4, fields, 16, NP, levels), F32),
            jax.ShapeDtypeStruct((1, elements), I32),
        ),
        in_specs=[SMEM, VMEM, VMEM, VMEM],
        out_specs=(ANY, VMEM, SMEM),
        scratch_shapes=[
            pltpu.VMEM((elements, NP, width), F32),
            pltpu.VMEM((CHUNKS, fields, elements // CHUNKS, NP, levels), F32),
            pltpu.SemaphoreType.DMA((CHUNKS,)),
        ],
        compiler_params=params(32),
        cost_estimate=cost(2e9, 2e7),
        name="inner_sum",
    )(cell, dynamics, back, jnp.asarray(table))


def border_kernel(
    fields, slot_ref, x_one, x_two, y_one, y_two, border_ref, table_ref, _, out_ref, buffer, sem
):
    width = x_one.shape[1]
    levels = width // fields
    adds = []
    halos = from_neighbours("gx", x_one[...], x_two[...])
    halos = halos + from_neighbours("gy", y_one[...], y_two[...])
    for kind, halo in enumerate(halos):
        table = table_ref[kind * 256 : kind * 256 + 256]
        if kind < 2:
            add = dot_twice(table, halo)
        else:
            add = dot(table[:, 0:64], halo)
        adds.append(add.reshape(16, NP, width))
    for kind in range(4):
        for k in range(16):
            if kind >= 2 and k in (0, 15):
                continue
            add = adds[kind][k]
            if kind < 2 and k in (0, 15):
                add = add + adds[2 if k == 0 else 3][0 if kind == 0 else 15]
            for f in range(fields):
                buffer[kind, f, k] = border_ref[kind, f, k] + add[:, f * levels : (f + 1) * levels]
            tile = (k, (EXD - 1) * EYD + k, k * EYD, k * EYD + EYD - 1)[kind]
            pltpu.make_async_copy(
                buffer.at[kind, :, k], out_ref.at[:, slot_ref[0, tile]], sem.at[kind]
            ).start()
    for kind in range(4):
        part = buffer.at[kind] if kind < 2 else buffer.at[kind, :, 1:15]
        pltpu.make_async_copy(part, part, sem.at[kind]).wait()


def border_sum(slot, halos, border, out):
    fields, levels = out.shape[0], out.shape[3]
    table = jnp.asarray(TABLES["border"].astype(np.float32).astype(jnp.bfloat16))
    return pl.pallas_call(
        functools.partial(border_kernel, fields),
        out_shape=jax.ShapeDtypeStruct(out.shape, F32),
        in_specs=[SMEM] + [VMEM] * 6 + [ANY],
        out_specs=ANY,
        scratch_shapes=[
            pltpu.VMEM((4, fields, 16, NP, levels), F32),
            pltpu.SemaphoreType.DMA((4,)),
        ],
        input_output_aliases={7: 0},
        compiler_params=params(16),
        cost_estimate=cost(2e8, 4e6),
        name="border_sum",
    )(slot, *halos, border, table, out)


def regroup(blocks):
    return lax.all_to_all(blocks, ("gx", "gy"), split_axis=0, concat_axis=0, tiled=True)


def per_device(state_in, stiffness, elem_cell, group_column, group_inverse):
    fields, elements = state_in.shape[:2]
    sizes = (lax.axis_size("gx"), lax.axis_size("gy"))
    columns_dev = 4 * elements
    span_y = EYD * sizes[1]
    stiff = stiffness.reshape(NP * NP, elements)

    columns, blocks, q, x_one, x_two, y_one, y_two = front(
        elem_cell, group_column.reshape(1, columns_dev), stiff, state_in, sizes
    )
    hx = exchange("gx", x_one, x_two)
    hy = exchange("gy", y_one, y_two)
    blocks = regroup(blocks)

    outgoing, place, south, north = send_columns(
        columns, (*hx, *hy), blocks, elem_cell.reshape(1, elements), sizes
    )
    incoming = regroup(outgoing)
    dynamics = dynamics_rows(elem_cell, stiff, state_in, span_y, (*hx, south, north))
    incoming, dynamics = lax.optimization_barrier((incoming, dynamics))
    received = regroup(physics_step(incoming, q, group_inverse, fields))

    back, x_one, x_two, south, north = unpack(received, place)
    bx = exchange("gx", x_one, x_two)
    by = exchange("gy", *messages(*bx, south, north, hi_lo(TABLES["corner_col"])))
    inner, border, slot = inner_sum(elem_cell, dynamics, back, fields, span_y)
    return border_sum(slot, (*bx, *by), border, inner)


def solution(mesh):
    placed = (
        P(None, ("gx", "gy"), None, None),
        P(None, None, ("gx", "gy")),
        P(("gx", "gy")),
        P(("gx", "gy")),
        P(("gx", "gy"), None, None),
    )
    return jax.shard_map(
        per_device,
        mesh=mesh,
        in_specs=placed,
        out_specs=P(None, ("gx", "gy"), None, None),
        check_vma=False,
    )
```

```python
import functools
import math

import jax
import jax.numpy as jnp
import numpy as np
from jax import lax
from jax.experimental import pallas as pl
from jax.experimental.pallas import tpu as pltpu
from jax.sharding import PartitionSpec as P

GROUP_COLS = 16
EXD = 16
EYD = 16
NP = 16
F32 = jnp.float32
BF16 = jnp.bfloat16
I32 = jnp.int32
MB = 1024 * 1024


def lagrange_value(node_index, position, gll_nodes):
    running = 1.0
    for other_index in range(4):
        if other_index != node_index:
            running = (
                running
                * (position - gll_nodes[other_index])
                / (gll_nodes[node_index] - gll_nodes[other_index])
            )
    return running


def half_tables():
    gll_nodes = [-1.0, -1.0 / math.sqrt(5.0), 1.0 / math.sqrt(5.0), 1.0]
    halves = np.zeros((2, 4))
    for half_index, (lower_end, upper_end) in enumerate(((-1.0, 0.0), (0.0, 1.0))):
        centre = 0.5 * (lower_end + upper_end)
        offset = 0.5 * (upper_end - lower_end) / math.sqrt(3.0)
        for node in range(4):
            first = lagrange_value(node, centre - offset, gll_nodes)
            second = lagrange_value(node, centre + offset, gll_nodes)
            halves[half_index, node] = 0.5 * (upper_end - lower_end) * (first + second)
    product = halves @ halves.T
    determinant = product[0, 0] * product[1, 1] - product[0, 1] * product[1, 0]
    inverse = (
        np.array([[product[1, 1], -product[0, 1]], [-product[1, 0], product[0, 0]]]) / determinant
    )
    spread = halves.T @ inverse
    return halves.astype(np.float32), spread.astype(np.float32)


HALVES, SPREAD = half_tables()
ONE_D = np.array([0.5, 1.0, 1.0, 0.5])


def shift_down(n):
    return np.eye(n, k=-1)


def local_pass(n):
    table = np.einsum("ab,xy->axby", np.eye(4), np.eye(n))
    table[0, :, 3, :] += shift_down(n)
    table[3, :, 0, :] += shift_down(n).T
    return table


def constant_tables():
    h = HALVES.astype(np.float64)
    s = SPREAD.astype(np.float64)
    w = ONE_D
    eye = np.eye(EXD)
    line = local_pass(EYD)
    col_x = []
    for a in (0, 3):
        col_x.append(
            np.einsum("i,jb,b,byez->ijyez", h[:, a] * w[a], h, w, line).reshape(4 * EYD, 4 * EYD)
        )
    col_y = np.zeros((EXD, 2, 2, EYD, 2, 4, EXD))
    for side, (b, y) in enumerate(((0, 0), (3, EYD - 1))):
        col_y[:, :, :, y, side] = np.einsum("ia,j,xz->xijaz", h * w, h[:, b] * w[b], eye)
    col_y = col_y.reshape(EXD * 4 * EYD, 2 * 4 * EXD)
    nodes = np.einsum("ai,bj,yz->abyijz", s, s, np.eye(EYD))
    across = np.zeros((4, 4, EYD, 3, 2, 2, EYD))
    across[:, :, :, 1] = nodes
    across[0, :, :, 0] = nodes[3]
    across[3, :, :, 2] = nodes[0]
    full = np.einsum("byez,aezdijt->abydijt", line, across)
    full = full * w[:, None, None, None, None, None, None] * w[:, None, None, None, None, None]
    final = full.reshape(NP * EYD, 3 * 4 * EYD)
    along = local_pass(EXD)
    lines = np.zeros((2, 4, EXD, EXD, 2, 2, EYD))
    corner_col = np.zeros((2, 4, EXD, 2, 2, 2, EYD))
    corner_pt = np.zeros((2, 4, EXD, 2, 4, EYD))
    for side, (b, y) in enumerate(((0, 0), (3, EYD - 1))):
        lines[side, :, :, :, :, :, y] = np.einsum("axcz,ci,j->axzij", along, s, s[b])
        corner_col[side, 0, 0, 0, :, :, y] = np.outer(s[3], s[b])
        corner_col[side, 3, EXD - 1, 1, :, :, y] = np.outer(s[0], s[b])
        corner_pt[side, 0, 0, 0, b, y] = 1.0
        corner_pt[side, 3, EXD - 1, 1, b, y] = 1.0
    lines = lines.reshape(2 * 4 * EXD, EXD * 4 * EYD)
    corner_col = corner_col.reshape(2 * 4 * EXD, 2 * 4 * EYD)
    corner_pt = corner_pt.reshape(2 * 4 * EXD, 2 * 4 * EYD)
    border = np.zeros((4, EYD, NP, 128))
    order = full.transpose(2, 0, 1, 3, 4, 5, 6).reshape(EYD, NP, 3, 4 * EYD)
    west, east = hi_lo_arrays(order[:, :, 0]), hi_lo_arrays(order[:, :, 2])
    border[0] = np.concatenate(west, axis=-1)
    border[1] = np.concatenate(east, axis=-1)
    for side, b in enumerate((0, 3)):
        for a in range(4):
            for x in range(EXD):
                border[2 + side, x, 4 * a + b, 16 * a + x] = w[a] * w[b]
    return dict(
        col_x=np.concatenate(col_x, axis=0),
        col_y=col_y,
        final=order.reshape(EYD * NP, 3 * 4 * EYD),
        lines=lines,
        corner_col=corner_col,
        corner_pt=corner_pt,
        border=border.reshape(4 * EYD * NP, 128),
    )


def hi_lo_arrays(table):
    hi = np.asarray(table, np.float32).astype(jnp.bfloat16)
    lo = (np.asarray(table, np.float32) - hi.astype(np.float32)).astype(jnp.bfloat16)
    return hi, lo


def hi_lo(table):
    return jnp.asarray(np.concatenate(hi_lo_arrays(table), axis=1))


TABLES = constant_tables()


def dot(left, right):
    return jnp.dot(left, right, preferred_element_type=F32)


def dot_nt(left, right):
    return lax.dot_general(left, right, (((1,), (1,)), ((), ())), preferred_element_type=F32)


def dot_twice(table, right):
    return dot(table, jnp.concatenate([right, right], axis=0))


def split(values):
    hi = values.astype(BF16)
    return hi, (values - hi.astype(F32)).astype(BF16)


def iota(shape, dim):
    return lax.broadcasted_iota(I32, shape, dim)


def one_hot(condition):
    return jnp.where(condition, 1.0, 0.0).astype(BF16)


def as_columns(row, start):
    piece = row[:, start : start + 128].astype(F32)
    return jnp.transpose(jnp.broadcast_to(piece, (128, 128))).astype(I32)


def tile_number(cell, span_y):
    shift = span_y.bit_length() - 1
    assert span_y == 1 << shift
    return ((cell >> shift) & (EXD - 1)) * EYD + (cell & (EYD - 1))


VMEM = pl.BlockSpec(memory_space=pltpu.VMEM)
SMEM = pl.BlockSpec(memory_space=pltpu.SMEM)
ANY = pl.BlockSpec(memory_space=pl.ANY)


def params(mib):
    return pltpu.CompilerParams(vmem_limit_bytes=mib * MB)


def cost(flops, moved):
    return pl.CostEstimate(flops=int(flops), bytes_accessed=int(moved), transcendentals=0)


def column_requests(devices, per_peer, group):
    columns_dev = devices * per_peer
    shift = columns_dev.bit_length() - 1
    source = group >> shift
    local = group & (columns_dev - 1)
    of_source = source == iota((devices, columns_dev), 0)
    marks = one_hot(of_source)
    upper = one_hot(iota((128, 128), 0) <= iota((128, 128), 1))
    before = jnp.zeros((devices, 1), F32)
    ranks = []
    for start in range(0, columns_dev, 128):
        piece = marks[:, start : start + 128]
        counts = dot(piece, upper) + before
        ranks.append(counts)
        before = counts[:, 127:128]
    counts = jnp.concatenate(ranks, axis=1)
    rank = jnp.sum(jnp.where(of_source, counts, 0.0), axis=0, keepdims=True).astype(I32) - 1
    of_rank = one_hot(rank == iota((128, columns_dev), 0))
    high = jnp.where(of_source, (local >> 5).astype(F32), 0.0).astype(BF16)
    low = jnp.where(of_source, (local & 31).astype(F32), 0.0).astype(BF16)
    wanted = dot_nt(high, of_rank) * 32.0 + dot_nt(low, of_rank)
    return wanted, source * per_peer + rank


def diagonal(sizes, step_x, step_y):
    count_x, count_y = sizes
    x = lax.rem(lax.axis_index("gx") + step_x + count_x, count_x)
    y = lax.rem(lax.axis_index("gy") + step_y + count_y, count_y)
    return x * count_y + y


CHUNKS = 8


def state_copy(state_ref, raw, sems, chunk):
    per = raw.shape[2]
    return pltpu.make_async_copy(
        state_ref.at[:, pl.ds(chunk * per, per)], raw.at[chunk], sems.at[chunk]
    )


def tile_operators(span_y, cell, stiff):
    elements = cell.shape[1]
    marks = one_hot(tile_number(cell, span_y) == iota((elements, elements), 0))
    row = iota(stiff.shape, 0)
    stiff = stiff + jnp.where((row >> 4) == (row & 15), 1.0, 0.0)
    hi, lo = split(stiff)
    return dot_nt(marks, hi), dot_nt(marks, lo)


def place_operators(parts, operators):
    row, col = iota((256, 256), 0), iota((256, 256), 1)
    same_elem = one_hot((row & 15) == (col >> 4))
    tiling = one_hot((row & 15) == (col & 15))
    column = iota((EYD, 256), 1) >> 4
    for x in range(EXD):
        stacked = jnp.concatenate(
            [
                jnp.where(column == n, part[x * EYD : (x + 1) * EYD], 0.0).astype(BF16)
                for part in parts
                for n in range(NP)
            ],
            axis=0,
        )
        placed = dot(stacked, tiling).astype(BF16)
        operators[x, 0:256] = placed[0:256] * same_elem
        operators[x, 256:512] = placed[256:512] * same_elem


def place_states(span_y, cell_smem, state_ref, raw, sems, hi_ref, lo_ref):
    fields, per, _, levels = raw.shape[1:]
    for chunk in range(CHUNKS):
        state_copy(state_ref, raw, sems, chunk).wait()

        def place_slots(i, _, chunk=chunk):
            for u in range(4):
                k = i * 4 + u
                where = tile_number(cell_smem[chunk * per + k], span_y)
                for f in range(fields):
                    hi, lo = split(raw[chunk, f, k])
                    hi_ref[where, :, f * levels : (f + 1) * levels] = hi
                    lo_ref[where, :, f * levels : (f + 1) * levels] = lo
            return 0

        lax.fori_loop(0, per // 4, place_slots, 0)


def row_points(row, operators, hi_ref, lo_ref):
    width = hi_ref.shape[2]
    at = pl.ds(pl.multiple_of(row * EYD, EYD), EYD)
    hi = hi_ref[at].reshape(EYD * NP, width)
    lo = lo_ref[at].reshape(EYD * NP, width)
    both = dot(operators[row], hi)
    return both[0:256] + both[256:512] + dot(operators[row, 0:256], lo)


def shifted(values, step):
    rows = values.shape[0]
    moved = pltpu.roll(values, step % rows, 0)
    free = 0 if step > 0 else rows - 1
    return jnp.where(iota(values.shape, 0) == free, 0.0, moved)


def sum_along_y(nodes):
    for a in range(4):
        first, last = nodes[4 * a], nodes[4 * a + 3]
        nodes[4 * a] = first + shifted(last, 1)
        nodes[4 * a + 3] = last + shifted(first, -1)


def held_nodes(held, before, next_first):
    nodes = [held[16 * n : 16 * n + 16] for n in range(NP)]
    for b in range(4):
        nodes[b] = nodes[b] + before[16 * b : 16 * b + 16]
        if next_first is not None:
            nodes[12 + b] = nodes[12 + b] + next_first[b]
    return nodes


def front_kernel(
    sizes,
    span_y,
    cell_smem,
    cell_ref,
    group_ref,
    stiff_ref,
    state_ref,
    columns_out,
    blocks_ref,
    q_ref,
    x_one,
    x_two,
    y_one,
    y_two,
    raw,
    sems,
    hi_ref,
    lo_ref,
    operators,
    held,
    before,
    lines,
    ends,
    columns,
    out_sem,
):
    devices = sizes[0] * sizes[1]
    width = held.shape[1]
    for chunk in range(CHUNKS):
        state_copy(state_ref, raw, sems, chunk).start()
    place_operators(tile_operators(span_y, cell_ref[...], stiff_ref[...]), operators)
    wanted, q_ref[...] = column_requests(
        devices, group_ref.shape[1] // devices, group_ref[...]
    )
    blocks_ref[...] = jnp.broadcast_to(wanted[:, None, :], (devices, 8, 128))
    place_states(span_y, cell_smem, state_ref, raw, sems, hi_ref, lo_ref)
    before[...] = jnp.zeros_like(before)
    held[...] = jnp.zeros_like(held)

    def emit(row, next_first):
        nodes = held_nodes(held, before, next_first)
        along = [
            [
                sum(float(HALVES[i, a] * ONE_D[a]) * nodes[4 * a + b] for a in range(4))
                for b in range(4)
            ]
            for i in range(2)
        ]
        for i in range(2):
            for j in range(2):
                columns[pl.ds(pl.multiple_of(row * 64 + (2 * i + j) * 16, 16), 16)] = sum(
                    float(HALVES[j, b] * ONE_D[b]) * along[i][b] for b in range(4)
                )

    def one_row(row, _):
        points = row_points(row, operators, hi_ref, lo_ref)

        ends[0, jnp.minimum(row, 1)] = points[0:64]
        ends[1, jnp.maximum(row - EXD + 2, 0)] = points[192:256]
        nodes = [points[16 * n : 16 * n + 16] for n in range(NP)]
        for a in range(4):
            lines[0, pl.ds(16 * a + row, 1)] = nodes[4 * a][0:1]
            lines[1, pl.ds(16 * a + row, 1)] = nodes[4 * a + 3][15:16]
        sum_along_y(nodes)
        emit(jnp.maximum(row - 1, 0), nodes[0:4])
        before[...] = held[192:256]
        for n in range(NP):
            held[16 * n : 16 * n + 16] = nodes[n]
        return 0

    def send(part):
        rows = pl.ds(part * (columns.shape[0] // 2), columns.shape[0] // 2)
        return pltpu.make_async_copy(columns.at[rows], columns_out.at[rows], out_sem.at[part])

    lax.fori_loop(0, EXD // 2 + 2, one_row, 0, unroll=2)
    send(0).start()
    lax.fori_loop(EXD // 2 + 2, EXD, one_row, 0, unroll=2)
    emit(EXD - 1, None)
    send(1).start()
    whole = []
    for side in range(2):
        first, last = lines[side, 0:16], lines[side, 48:64]
        whole.append(
            jnp.concatenate(
                [first + shifted(last, 1), lines[side, 16:48], last + shifted(first, -1)], axis=0
            )
        )
    for axis, low, high, one, two in (
        ("gx", ends[0, 0], ends[1, 1], x_one, x_two),
        ("gy", whole[0], whole[1], y_one, y_two),
    ):
        first, second = by_parity(axis, low, high)
        one[...] = first.astype(BF16)
        two[...] = second.astype(BF16)
    for step_x, row in ((-1, 0), (1, 3 * 16 + 15)):
        for step_y, side in ((-1, 0), (1, 1)):
            block = diagonal(sizes, step_x, step_y)
            point = lines[side, row : row + 1]
            for f in range(width // 128):
                blocks_ref[block, 1 + f : 2 + f] = point[:, f * 128 : (f + 1) * 128]
    send(0).wait()
    send(1).wait()


def state_scratch(fields, elements, levels):
    width = fields * levels
    return [
        pltpu.VMEM((CHUNKS, fields, elements // CHUNKS, NP, levels), F32),
        pltpu.SemaphoreType.DMA((CHUNKS,)),
        pltpu.VMEM((elements, NP, width), BF16),
        pltpu.VMEM((elements, NP, width), BF16),
        pltpu.VMEM((EXD, 512, 256), BF16),
        pltpu.VMEM((256, width), F32),
        pltpu.VMEM((64, width), F32),
    ]


FRONT_LIMIT = 56


def front(cell, group, stiff, state, sizes):
    fields, elements, _, levels = state.shape
    width = fields * levels
    devices = sizes[0] * sizes[1]
    line = jax.ShapeDtypeStruct((64, width), BF16)
    return pl.pallas_call(
        functools.partial(front_kernel, sizes, EYD * sizes[1]),
        out_shape=(
            jax.ShapeDtypeStruct((4 * elements, width), F32),
            jax.ShapeDtypeStruct((devices, 8, 128), F32),
            jax.ShapeDtypeStruct((1, 4 * elements), I32),
            line,
            line,
            line,
            line,
        ),
        in_specs=[SMEM, VMEM, VMEM, VMEM, ANY],
        out_specs=(ANY,) + (VMEM,) * 6,
        scratch_shapes=state_scratch(fields, elements, levels)
        + [
            pltpu.VMEM((2, 64, width), F32),
            pltpu.VMEM((2, 2, 64, width), F32),
            pltpu.VMEM((4 * elements, width), F32),
            pltpu.SemaphoreType.DMA((2,)),
        ],
        compiler_params=params(FRONT_LIMIT),
        cost_estimate=cost(4e9, 2e7),
        name="front",
    )(cell, cell.reshape(1, elements), group, stiff, state)


def dynamics_kernel(
    span_y,
    cell_smem,
    cell_ref,
    stiff_ref,
    state_ref,
    hx_one,
    hx_two,
    hy_south,
    hy_north,
    out_ref,
    raw,
    sems,
    hi_ref,
    lo_ref,
    operators,
    held,
    before,
    turned,
    hx,
    rows_out,
    out_sems,
):
    hx[0], hx[1] = from_neighbours("gx", hx_one[...].astype(F32), hx_two[...].astype(F32))
    fields, _, levels = turned.shape
    for chunk in range(CHUNKS):
        state_copy(state_ref, raw, sems, chunk).start()
    place_operators(tile_operators(span_y, cell_ref[...], stiff_ref[...]), operators)
    place_states(span_y, cell_smem, state_ref, raw, sems, hi_ref, lo_ref)
    before[...] = jnp.zeros_like(before)
    held[...] = jnp.zeros_like(held)

    def emit(row, next_first):
        nodes = held_nodes(held, before, next_first)
        for a in range(4):
            at_row = pl.ds(16 * a + row, 1)
            for b in range(4):
                n = 4 * a + b
                values = nodes[n]
                if b == 0:
                    values = values + jnp.where(iota(values.shape, 0) == 0, hy_south[at_row], 0.0)
                if b == 3:
                    values = values + jnp.where(iota(values.shape, 0) == 15, hy_north[at_row], 0.0)
                values = values * float(ONE_D[a] * ONE_D[b])
                for f in range(fields):
                    turned[f, 16 * n : 16 * n + 16] = values[:, f * levels : (f + 1) * levels]
        slot = row & 1
        for y in range(EYD):
            for f in range(fields):
                rows_out[slot, y, :, f * levels : (f + 1) * levels] = turned[
                    f, pl.ds(y, NP, stride=16)
                ]

    def copy_out(row):
        slot = row & 1
        return pltpu.make_async_copy(
            rows_out.at[slot], out_ref.at[pl.ds(row * EYD, EYD)], out_sems.at[slot]
        )

    def one_row(row, _):
        points = row_points(row, operators, hi_ref, lo_ref)
        nodes = [points[16 * n : 16 * n + 16] for n in range(NP)]
        low = jnp.where(row == 0, 1.0, 0.0)
        high = jnp.where(row == EXD - 1, 1.0, 0.0)
        for b in range(4):
            rows = slice(16 * b, 16 * b + 16)
            nodes[b] = nodes[b] + hx[0, rows] * low
            nodes[12 + b] = nodes[12 + b] + hx[1, rows] * high
        sum_along_y(nodes)

        @pl.when(row >= 3)
        def _():
            copy_out(row - 3).wait()

        @pl.when(row >= 1)
        def _():
            emit(row - 1, nodes[0:4])
            copy_out(row - 1).start()

        before[...] = held[192:256]
        for n in range(NP):
            held[16 * n : 16 * n + 16] = nodes[n]
        return 0

    lax.fori_loop(0, EXD, one_row, 0)
    copy_out(EXD - 3).wait()
    emit(EXD - 1, None)
    copy_out(EXD - 1).start()
    copy_out(EXD - 2).wait()
    copy_out(EXD - 1).wait()


def dynamics_rows(cell, stiff, state, span_y, halos):
    fields, elements, _, levels = state.shape
    width = fields * levels
    return pl.pallas_call(
        functools.partial(dynamics_kernel, span_y),
        out_shape=jax.ShapeDtypeStruct((elements, NP, width), F32),
        in_specs=[SMEM, VMEM, VMEM, ANY] + [VMEM] * 4,
        out_specs=ANY,
        scratch_shapes=state_scratch(fields, elements, levels)
        + [
            pltpu.VMEM((fields, 256, levels), F32),
            pltpu.VMEM((2, 64, width), F32),
            pltpu.VMEM((2, EYD, NP, width), F32),
            pltpu.SemaphoreType.DMA((2,)),
        ],
        compiler_params=params(DYN_LIMIT),
        cost_estimate=cost(4e9, 2e7),
        name="dynamics_rows",
    )(cell, cell.reshape(1, elements), stiff, state, *halos)


def message_kernel(x_one, x_two, south_ref, north_ref, table, y_one, y_two):
    both = jnp.concatenate(from_neighbours("gx", x_one[...], x_two[...]), axis=0)
    add = dot_twice(table[...], both)
    one, two = by_parity("gy", south_ref[...] + add[0:64], north_ref[...] + add[64:128])
    y_one[...] = one.astype(BF16)
    y_two[...] = two.astype(BF16)


def messages(one, two, south, north, table):
    width = one.shape[1]
    return pl.pallas_call(
        message_kernel,
        out_shape=(jax.ShapeDtypeStruct((64, width), BF16),) * 2,
        in_specs=[VMEM] * 5,
        out_specs=(VMEM,) * 2,
        compiler_params=params(16),
        cost_estimate=cost(4e7, 6e5),
        name="line_messages",
    )(one, two, south, north, table)


def pairs(axis, first):
    count = lax.axis_size(axis)
    low = range(0 if first else 1, count, 2)
    return [(i, (i + 1) % count) for i in low] + [((i + 1) % count, i) for i in low]


def exchange(axis, one, two):
    return (
        lax.ppermute(one, axis, pairs(axis, True)),
        lax.ppermute(two, axis, pairs(axis, False)),
    )


def by_parity(axis, to_low, to_high):
    even = (lax.axis_index(axis) & 1) == 0
    return jnp.where(even, to_high, to_low), jnp.where(even, to_low, to_high)


def from_neighbours(axis, one, two):
    even = (lax.axis_index(axis) & 1) == 0
    return jnp.where(even, two, one), jnp.where(even, one, two)


def send_kernel(
    sizes,
    span_y,
    columns_hbm,
    table_hbm,
    x_one,
    x_two,
    y_one,
    y_two,
    blocks_ref,
    cell_ref,
    out_ref,
    place_ref,
    whole_south,
    whole_north,
    columns_ref,
    table_ref,
    rounded,
    pick,
    sems,
):
    count, width = columns_ref.shape
    devices = sizes[0] * sizes[1]
    per_peer = count // devices
    table_copy = pltpu.make_async_copy(table_hbm, table_ref, sems.at[0])
    table_copy.start()
    copy = pltpu.make_async_copy(columns_hbm, columns_ref, sems.at[1])
    copy.start()
    requested = blocks_ref[:, 0, :].astype(I32)
    spread_out = one_hot((iota((128, count), 1) & (per_peer - 1)) == iota((128, count), 0))
    shift = per_peer.bit_length() - 1
    own = (iota((devices, count), 1) >> shift) == iota((devices, count), 0)
    wide = dot((requested >> 5).astype(F32).astype(BF16), spread_out) * 32.0 + dot(
        (requested & 31).astype(F32).astype(BF16), spread_out
    )
    requested = jnp.sum(jnp.where(own, wide, 0.0), axis=0, keepdims=True).astype(I32)
    elements = cell_ref.shape[1]
    marks = one_hot((requested >> 2) == iota((elements, count), 0))
    tile_row = tile_number(cell_ref[...], span_y).astype(F32)
    tile_row = jnp.broadcast_to(tile_row, (8, elements)).astype(BF16)
    tile = dot(tile_row, marks)[0:1].astype(I32)
    place = (tile >> 4) * 64 + (requested & 3) * 16 + (tile & 15)
    place_ref[...] = place
    for start in range(0, count, 128):
        column = as_columns(place, start)
        for other in range(0, count, 128):
            pick[start : start + 128, other : other + 128] = one_hot(
                column == iota((128, 128), 1) + other
            )

    south, north = from_neighbours("gy", y_one[...].astype(F32), y_two[...].astype(F32))
    for ref, line, step_y in ((whole_south, south, -1), (whole_north, north, 1)):
        ref[...] = line
        for step_x, row in ((-1, 0), (1, 63)):
            block = diagonal(sizes, step_x, step_y)
            for f in range(width // 128):
                ref[row : row + 1, f * 128 : (f + 1) * 128] += blocks_ref[block, 1 + f : 2 + f]
    lines = jnp.concatenate([whole_south[...], whole_north[...]], axis=0).astype(BF16)
    west, east = from_neighbours("gx", x_one[...], x_two[...])
    table_copy.wait()
    west = dot_twice(table_ref[count : count + 64, 0:128], west)
    east = dot_twice(table_ref[count + 64 : count + 128, 0:128], east)
    add = dot_twice(table_ref[0:count], lines)
    copy.wait()
    rounded[...] = (columns_ref[...] + add).astype(BF16)
    rounded[0:64] = (columns_ref[0:64] + add[0:64] + west).astype(BF16)
    rounded[count - 64 : count] = (
        columns_ref[count - 64 : count] + add[count - 64 : count] + east
    ).astype(BF16)
    out_ref[...] = dot(pick[...], rounded[...]).astype(BF16)


def send_columns(columns, halos, blocks, cell, sizes):
    count, width = columns.shape
    extra = np.concatenate(hi_lo_arrays(TABLES["col_x"]), axis=1)
    table = np.concatenate(hi_lo_arrays(TABLES["col_y"]), axis=1)
    table = np.concatenate([table, np.pad(extra, ((0, 0), (0, 128)))], axis=0)
    return pl.pallas_call(
        functools.partial(send_kernel, sizes, EYD * sizes[1]),
        out_shape=(
            jax.ShapeDtypeStruct((count, width), BF16),
            jax.ShapeDtypeStruct((1, count), I32),
            jax.ShapeDtypeStruct((64, width), F32),
            jax.ShapeDtypeStruct((64, width), F32),
        ),
        in_specs=[ANY, ANY] + [VMEM] * 6,
        out_specs=(VMEM,) * 4,
        scratch_shapes=[
            pltpu.VMEM((count, width), F32),
            pltpu.VMEM(table.shape, BF16),
            pltpu.VMEM((count, width), BF16),
            pltpu.VMEM((count, count), BF16),
            pltpu.SemaphoreType.DMA((2,)),
        ],
        compiler_params=params(SEND_LIMIT),
        cost_estimate=cost(2e9, 5e6),
        name="send_columns",
    )(columns, jnp.asarray(table), *halos, blocks, cell)


SEND_LIMIT = 60
DYN_LIMIT = 56


def physics_kernel(
    fields, incoming_ref, q_ref, inverse_hbm, out_ref, inverse, tendency, sem
):
    count, width = incoming_ref.shape
    levels = width // fields
    copy = pltpu.make_async_copy(inverse_hbm, inverse, sem)
    copy.start()
    q = q_ref[...]
    size = count // PARTS
    for part in range(PARTS):
        pick = []
        for start in range(part * size, (part + 1) * size, 128):
            column = as_columns(q, start)
            pick.append(
                jnp.concatenate(
                    [
                        one_hot(column == iota((128, 128), 1) + other)
                        for other in range(0, count, 128)
                    ],
                    axis=1,
                )
            )
        physics = dot(jnp.concatenate(pick, axis=0), incoming_ref[...])
        if part == 0:
            copy.wait()
        for group in range(size // GROUP_COLS):
            rows = physics[group * GROUP_COLS : (group + 1) * GROUP_COLS]
            stacked = jnp.concatenate(
                [rows[:, f * levels : (f + 1) * levels] for f in range(fields)], axis=0
            )
            whole = part * (size // GROUP_COLS) + group
            result = dot_nt(stacked.astype(BF16), inverse[whole]) - stacked
            tendency[whole * GROUP_COLS : (whole + 1) * GROUP_COLS] = jnp.concatenate(
                [result[f * GROUP_COLS : (f + 1) * GROUP_COLS] for f in range(fields)], axis=1
            ).astype(BF16)
    for start in range(0, count, size):
        pick = one_hot(q == iota((size, count), 0) + start)
        out_ref[start : start + size] = dot(pick, tendency[...]).astype(BF16)


def physics_step(incoming, q, inverse, fields):
    count, width = incoming.shape
    return pl.pallas_call(
        functools.partial(physics_kernel, fields),
        out_shape=jax.ShapeDtypeStruct((count, width), BF16),
        in_specs=[VMEM, VMEM, ANY],
        out_specs=VMEM,
        scratch_shapes=[
            pltpu.VMEM(inverse.shape, BF16),
            pltpu.VMEM((count, width), BF16),
            pltpu.SemaphoreType.DMA,
        ],
        compiler_params=params(PHYSICS_LIMIT),
        cost_estimate=cost(3e9, 5e6),
        name="physics",
    )(incoming, q, inverse)


PHYSICS_LIMIT = 16
PARTS = 2


def unpack_kernel(
    received_ref,
    place_ref,
    lines_table,
    back_ref,
    x_one,
    x_two,
    south_ref,
    north_ref,
    pick,
):
    count = received_ref.shape[0]
    place = place_ref[...]
    for start in range(0, count, 128):
        pick[start : start + 128] = one_hot(place == iota((128, count), 0) + start)
    back_ref[...] = dot(pick[...], received_ref[...]).astype(BF16)
    x_one[...], x_two[...] = by_parity("gx", back_ref[0:64], back_ref[count - 64 : count])
    lines = dot(lines_table[...], back_ref[...])
    south_ref[...] = lines[0:64] + lines[128:192]
    north_ref[...] = lines[64:128] + lines[192:256]


def unpack(received, place):
    count, width = received.shape
    table = jnp.asarray(np.concatenate(hi_lo_arrays(TABLES["lines"]), axis=0))
    return pl.pallas_call(
        unpack_kernel,
        out_shape=(
            jax.ShapeDtypeStruct((count, width), BF16),
            jax.ShapeDtypeStruct((64, width), BF16),
            jax.ShapeDtypeStruct((64, width), BF16),
            jax.ShapeDtypeStruct((64, width), F32),
            jax.ShapeDtypeStruct((64, width), F32),
        ),
        in_specs=[VMEM] * 3,
        out_specs=(VMEM,) * 5,
        scratch_shapes=[pltpu.VMEM((count, count), BF16)],
        compiler_params=params(16),
        cost_estimate=cost(2e9, 4e6),
        name="unpack",
    )(received, place, table)


def inner_kernel(dynamics_ref, back_ref, table_ref, total):
    width = total.shape[2]
    count = back_ref.shape[0]

    def near_sum(row, first, rows, skip):
        near = back_ref[pl.ds(first, rows)]
        both = dot(table_ref[:, skip : skip + rows], near)
        at = pl.ds(row * EYD, 2 * EYD)
        sums = both[0:512] + both[512:1024]
        total[at] = dynamics_ref[at] + sums.reshape(2 * EYD, NP, width)

    near_sum(0, 0, 192, 64)
    near_sum(EXD - 2, count - 192, 192, 0)

    def middle(pair, _):
        near_sum(pair * 2, pl.multiple_of(pair * 128 - 64, 64), 256, 0)
        return 0

    lax.fori_loop(1, EXD // 2 - 1, middle, 0, unroll=2)


def inner_sum(dynamics, back):
    one = TABLES["final"].reshape(EYD * NP, 3, 64)
    two = np.zeros((2, EYD * NP, 4, 64))
    two[0, :, 0:3] = one
    two[1, :, 1:4] = one
    table = np.concatenate(hi_lo_arrays(two.reshape(2 * EYD * NP, 256)), axis=0)
    return pl.pallas_call(
        inner_kernel,
        out_shape=jax.ShapeDtypeStruct(dynamics.shape, F32),
        in_specs=[VMEM] * 3,
        out_specs=VMEM,
        input_output_aliases={0: 0},
        compiler_params=params(16),
        cost_estimate=cost(4e9, 2e7),
        name="inner_sum",
    )(dynamics, back, jnp.asarray(table))


def to_slots_kernel(span_y, cell_smem, total, out_ref, slot_ref, buffer, sems):
    elements, _, width = total.shape
    fields, levels = buffer.shape[1], buffer.shape[4]
    per = elements // CHUNKS

    def copy(chunk):
        return pltpu.make_async_copy(
            buffer.at[chunk], out_ref.at[:, pl.ds(chunk * per, per)], sems.at[chunk]
        )

    for chunk in range(CHUNKS):

        def take_slots(i, _, chunk=chunk):
            for u in range(4):
                k = i * 4 + u
                tile = tile_number(cell_smem[chunk * per + k], span_y)
                slot_ref[0, tile] = chunk * per + k
                for f in range(fields):
                    buffer[chunk, f, k] = total[tile, :, f * levels : (f + 1) * levels]
            return 0

        lax.fori_loop(0, per // 4, take_slots, 0)
        copy(chunk).start()
    for chunk in range(CHUNKS):
        copy(chunk).wait()


def to_slots(cell, total, fields, span_y):
    elements, _, width = total.shape
    levels = width // fields
    return pl.pallas_call(
        functools.partial(to_slots_kernel, span_y),
        out_shape=(
            jax.ShapeDtypeStruct((fields, elements, NP, levels), F32),
            jax.ShapeDtypeStruct((1, elements), I32),
        ),
        in_specs=[SMEM, VMEM],
        out_specs=(ANY, SMEM),
        scratch_shapes=[
            pltpu.VMEM((CHUNKS, fields, elements // CHUNKS, NP, levels), F32),
            pltpu.SemaphoreType.DMA((CHUNKS,)),
        ],
        compiler_params=params(16),
        cost_estimate=cost(4e9, 2e7),
        name="to_slots",
    )(cell, total)


def border_kernel(
    fields, slot_ref, x_one, x_two, y_one, y_two, total_ref, table_ref, _, out_ref, buffer, sem
):
    width = x_one.shape[1]
    levels = width // fields
    halos = from_neighbours("gx", x_one[...], x_two[...])
    halos = halos + from_neighbours("gy", y_one[...], y_two[...])
    adds = []
    for kind, halo in enumerate(halos):
        table = table_ref[kind * 256 : kind * 256 + 256]
        if kind < 2:
            add = dot_twice(table, halo)
        else:
            add = dot(table[:, 0:64], halo)
        adds.append(add.reshape(16, NP, width))
    for kind in range(4):
        for k in range(16):
            if kind >= 2 and k in (0, 15):
                continue
            tile = (k, (EXD - 1) * EYD + k, k * EYD, k * EYD + EYD - 1)[kind]
            whole = total_ref[tile] + adds[kind][k]
            if kind < 2 and k in (0, 15):
                whole = whole + adds[2 if k == 0 else 3][0 if kind == 0 else 15]
            for f in range(fields):
                buffer[kind, f, k] = whole[:, f * levels : (f + 1) * levels]
            pltpu.make_async_copy(
                buffer.at[kind, :, k], out_ref.at[:, slot_ref[0, tile]], sem.at[kind]
            ).start()
    for kind in range(4):
        part = buffer.at[kind] if kind < 2 else buffer.at[kind, :, 1:15]
        pltpu.make_async_copy(part, part, sem.at[kind]).wait()


def border_sum(slot, halos, total, out):
    fields, levels = out.shape[0], out.shape[3]
    table = jnp.asarray(TABLES["border"].astype(np.float32).astype(jnp.bfloat16))
    return pl.pallas_call(
        functools.partial(border_kernel, fields),
        out_shape=jax.ShapeDtypeStruct(out.shape, F32),
        in_specs=[SMEM] + [VMEM] * 6 + [ANY],
        out_specs=ANY,
        scratch_shapes=[
            pltpu.VMEM((4, fields, 16, NP, levels), F32),
            pltpu.SemaphoreType.DMA((4,)),
        ],
        input_output_aliases={7: 0},
        compiler_params=params(16),
        cost_estimate=cost(2e8, 4e6),
        name="border_sum",
    )(slot, *halos, total, table, out)


def regroup(blocks):
    return lax.all_to_all(blocks, ("gx", "gy"), split_axis=0, concat_axis=0, tiled=True)


def per_device(state_in, stiffness, elem_cell, group_column, group_inverse):
    fields, elements = state_in.shape[:2]
    sizes = (lax.axis_size("gx"), lax.axis_size("gy"))
    columns_dev = 4 * elements
    span_y = EYD * sizes[1]
    stiff = stiffness.reshape(NP * NP, elements)

    columns, blocks, q, x_one, x_two, y_one, y_two = front(
        elem_cell, group_column.reshape(1, columns_dev), stiff, state_in, sizes
    )
    hx = exchange("gx", x_one, x_two)
    hy = exchange("gy", y_one, y_two)
    blocks = regroup(blocks)

    outgoing, place, south, north = send_columns(
        columns, (*hx, *hy), blocks, elem_cell.reshape(1, elements), sizes
    )
    incoming = regroup(outgoing)
    dynamics = dynamics_rows(elem_cell, stiff, state_in, span_y, (*hx, south, north))
    incoming, dynamics = lax.optimization_barrier((incoming, dynamics))
    received = regroup(physics_step(incoming, q, group_inverse, fields))

    back, x_one, x_two, south, north = unpack(received, place)
    bx = exchange("gx", x_one, x_two)
    by = exchange("gy", *messages(*bx, south, north, hi_lo(TABLES["corner_col"])))
    total = inner_sum(dynamics, back)
    inner, slot = to_slots(elem_cell, total, fields, span_y)
    return border_sum(slot, (*bx, *by), total, inner)


def solution(mesh):
    placed = (
        P(None, ("gx", "gy"), None, None),
        P(None, None, ("gx", "gy")),
        P(("gx", "gy")),
        P(("gx", "gy")),
        P(("gx", "gy"), None, None),
    )
    return jax.shard_map(
        per_device,
        mesh=mesh,
        in_specs=placed,
        out_specs=P(None, ("gx", "gy"), None, None),
        check_vma=False,
    )
```

```python
import functools
import math

import jax
import jax.numpy as jnp
import numpy as np
from jax import lax
from jax.experimental import pallas as pl
from jax.experimental.pallas import tpu as pltpu
from jax.sharding import PartitionSpec as P

GROUP_COLS = 16
EXD = 16
EYD = 16
NP = 16
F32 = jnp.float32
BF16 = jnp.bfloat16
I32 = jnp.int32
MB = 1024 * 1024


def lagrange_value(node_index, position, gll_nodes):
    running = 1.0
    for other_index in range(4):
        if other_index != node_index:
            running = (
                running
                * (position - gll_nodes[other_index])
                / (gll_nodes[node_index] - gll_nodes[other_index])
            )
    return running


def half_tables():
    gll_nodes = [-1.0, -1.0 / math.sqrt(5.0), 1.0 / math.sqrt(5.0), 1.0]
    halves = np.zeros((2, 4))
    for half_index, (lower_end, upper_end) in enumerate(((-1.0, 0.0), (0.0, 1.0))):
        centre = 0.5 * (lower_end + upper_end)
        offset = 0.5 * (upper_end - lower_end) / math.sqrt(3.0)
        for node in range(4):
            first = lagrange_value(node, centre - offset, gll_nodes)
            second = lagrange_value(node, centre + offset, gll_nodes)
            halves[half_index, node] = 0.5 * (upper_end - lower_end) * (first + second)
    product = halves @ halves.T
    determinant = product[0, 0] * product[1, 1] - product[0, 1] * product[1, 0]
    inverse = (
        np.array([[product[1, 1], -product[0, 1]], [-product[1, 0], product[0, 0]]]) / determinant
    )
    spread = halves.T @ inverse
    return halves.astype(np.float32), spread.astype(np.float32)


HALVES, SPREAD = half_tables()
ONE_D = np.array([0.5, 1.0, 1.0, 0.5])


def shift_down(n):
    return np.eye(n, k=-1)


def local_pass(n):
    table = np.einsum("ab,xy->axby", np.eye(4), np.eye(n))
    table[0, :, 3, :] += shift_down(n)
    table[3, :, 0, :] += shift_down(n).T
    return table


def constant_tables():
    h = HALVES.astype(np.float64)
    s = SPREAD.astype(np.float64)
    w = ONE_D
    eye = np.eye(EXD)
    line = local_pass(EYD)
    col_y = np.zeros((EXD, 2, 2, EYD, 2, 2, EXD))
    for side, (b, y) in enumerate(((0, 0), (3, EYD - 1))):
        col_y[:, :, :, y, side] = np.einsum("j,ik,xz->xijkz", h[:, b] * w[b], np.eye(2), eye)
    col_y = col_y.reshape(EXD * 4 * EYD, 2 * 2 * EXD)
    nodes = np.einsum("ai,bj,yz->abyijz", s, s, np.eye(EYD))
    across = np.zeros((4, 4, EYD, 3, 2, 2, EYD))
    across[:, :, :, 1] = nodes
    across[0, :, :, 0] = nodes[3]
    across[3, :, :, 2] = nodes[0]
    full = np.einsum("byez,aezdijt->abydijt", line, across)
    full = full * w[:, None, None, None, None, None, None] * w[:, None, None, None, None, None]
    final = full.reshape(NP * EYD, 3 * 4 * EYD)
    along = local_pass(EXD)
    lines = np.zeros((2, 4, EXD, EXD, 2, 2, EYD))
    corner_pt = np.zeros((2, 4, EXD, 2, 4, EYD))
    for side, (b, y) in enumerate(((0, 0), (3, EYD - 1))):
        lines[side, :, :, :, :, :, y] = np.einsum("axcz,ci,j->axzij", along, s, s[b])
        corner_pt[side, 0, 0, 0, b, y] = 1.0
        corner_pt[side, 3, EXD - 1, 1, b, y] = 1.0
    lines = lines.reshape(2 * 4 * EXD, EXD * 4 * EYD)
    corner_pt = corner_pt.reshape(2 * 4 * EXD, 2 * 4 * EYD)
    border = np.zeros((4, EYD, NP, 64))
    order = full.transpose(2, 0, 1, 3, 4, 5, 6).reshape(EYD, NP, 3, 4 * EYD)
    for kind, a in enumerate((0, 3)):
        border[kind, :, 4 * a : 4 * a + 4] = np.einsum("b,byez->ybez", w[a] * w, line).reshape(
            EYD, 4, 4 * EYD
        )
    for side, b in enumerate((0, 3)):
        for a in range(4):
            for x in range(EXD):
                border[2 + side, x, 4 * a + b, 16 * a + x] = w[a] * w[b]
    return dict(
        col_y=col_y,
        final=order.reshape(EYD * NP, 3 * 4 * EYD),
        lines=lines,
        corner_pt=corner_pt,
        border=border.reshape(4 * EYD * NP, 64),
    )


def hi_lo_arrays(table):
    hi = np.asarray(table, np.float32).astype(jnp.bfloat16)
    lo = (np.asarray(table, np.float32) - hi.astype(np.float32)).astype(jnp.bfloat16)
    return hi, lo


def hi_lo(table):
    return jnp.asarray(np.concatenate(hi_lo_arrays(table), axis=1))


TABLES = constant_tables()


def bf16_table(name):
    return jnp.asarray(TABLES[name].astype(np.float32).astype(jnp.bfloat16))


def dot(left, right):
    return jnp.dot(left, right, preferred_element_type=F32)


def dot_nt(left, right):
    return lax.dot_general(left, right, (((1,), (1,)), ((), ())), preferred_element_type=F32)


def dot_twice(table, right):
    return dot(table, jnp.concatenate([right, right], axis=0))


def split(values):
    hi = values.astype(BF16)
    return hi, (values - hi.astype(F32)).astype(BF16)


def iota(shape, dim):
    return lax.broadcasted_iota(I32, shape, dim)


def one_hot(condition):
    return jnp.where(condition, 1.0, 0.0).astype(BF16)


def as_columns(row, start):
    piece = row[:, start : start + 128].astype(F32)
    return jnp.transpose(jnp.broadcast_to(piece, (128, 128))).astype(I32)


def tile_number(cell, span_y):
    shift = span_y.bit_length() - 1
    assert span_y == 1 << shift
    return ((cell >> shift) & (EXD - 1)) * EYD + (cell & (EYD - 1))


VMEM = pl.BlockSpec(memory_space=pltpu.VMEM)
SMEM = pl.BlockSpec(memory_space=pltpu.SMEM)
ANY = pl.BlockSpec(memory_space=pl.ANY)


def params(mib):
    return pltpu.CompilerParams(vmem_limit_bytes=mib * MB)


def cost(flops, moved):
    return pl.CostEstimate(flops=int(flops), bytes_accessed=int(moved), transcendentals=0)


def column_requests(devices, per_peer, group):
    columns_dev = devices * per_peer
    shift = columns_dev.bit_length() - 1
    source = group >> shift
    local = group & (columns_dev - 1)
    of_source = source == iota((devices, columns_dev), 0)
    marks = one_hot(of_source)
    upper = one_hot(iota((128, 128), 0) <= iota((128, 128), 1))
    before = jnp.zeros((devices, 1), F32)
    ranks = []
    for start in range(0, columns_dev, 128):
        piece = marks[:, start : start + 128]
        counts = dot(piece, upper) + before
        ranks.append(counts)
        before = counts[:, 127:128]
    counts = jnp.concatenate(ranks, axis=1)
    rank = jnp.sum(jnp.where(of_source, counts, 0.0), axis=0, keepdims=True).astype(I32) - 1
    of_rank = one_hot(rank == iota((128, columns_dev), 0))
    high = jnp.where(of_source, (local >> 5).astype(F32), 0.0).astype(BF16)
    low = jnp.where(of_source, (local & 31).astype(F32), 0.0).astype(BF16)
    return dot_nt(high, of_rank), dot_nt(low, of_rank), source * per_peer + rank


def diagonal(sizes, step_x, step_y):
    count_x, count_y = sizes
    x = lax.rem(lax.axis_index("gx") + step_x + count_x, count_x)
    y = lax.rem(lax.axis_index("gy") + step_y + count_y, count_y)
    return x * count_y + y


CHUNKS = 8


def state_copy(state_ref, raw, sems, chunk):
    per = raw.shape[2]
    return pltpu.make_async_copy(
        state_ref.at[:, pl.ds(chunk * per, per)], raw.at[chunk], sems.at[chunk]
    )


def tile_operators(span_y, cell, stiff):
    elements = cell.shape[1]
    marks = one_hot(tile_number(cell, span_y) == iota((elements, elements), 0))
    row = iota(stiff.shape, 0)
    stiff = stiff + jnp.where((row >> 4) == (row & 15), 1.0, 0.0)
    hi, lo = split(stiff)
    return dot_nt(marks, hi), dot_nt(marks, lo)


def place_operators(parts, operators):
    row, col = iota((256, 256), 0), iota((256, 256), 1)
    same_elem = one_hot((row & 15) == (col >> 4))
    tiling = one_hot((row & 15) == (col & 15))
    column = iota((EYD, 256), 1) >> 4
    for x in range(EXD):
        stacked = jnp.concatenate(
            [
                jnp.where(column == n, part[x * EYD : (x + 1) * EYD], 0.0).astype(BF16)
                for part in parts
                for n in range(NP)
            ],
            axis=0,
        )
        placed = dot(stacked, tiling).astype(BF16)
        operators[x, 0:256] = placed[0:256] * same_elem
        operators[x, 256:512] = placed[256:512] * same_elem


def place_states(span_y, cell_smem, state_ref, raw, sems, hi_ref, lo_ref):
    fields, per, _, levels = raw.shape[1:]
    for chunk in range(CHUNKS):
        state_copy(state_ref, raw, sems, chunk).wait()

        def place_slots(i, _, chunk=chunk):
            for u in range(4):
                k = i * 4 + u
                where = tile_number(cell_smem[chunk * per + k], span_y)
                for f in range(fields):
                    hi, lo = split(raw[chunk, f, k])
                    hi_ref[where, :, f * levels : (f + 1) * levels] = hi
                    lo_ref[where, :, f * levels : (f + 1) * levels] = lo
            return 0

        lax.fori_loop(0, per // 4, place_slots, 0)


def row_points(row, operators, hi_ref, lo_ref):
    width = hi_ref.shape[2]
    at = pl.ds(pl.multiple_of(row * EYD, EYD), EYD)
    hi = hi_ref[at].reshape(EYD * NP, width)
    lo = lo_ref[at].reshape(EYD * NP, width)
    both = dot(operators[row], hi)
    return both[0:256] + both[256:512] + dot(operators[row, 0:256], lo)


def shifted(values, step):
    rows = values.shape[0]
    moved = pltpu.roll(values, step % rows, 0)
    free = 0 if step > 0 else rows - 1
    return jnp.where(iota(values.shape, 0) == free, 0.0, moved)


def sum_along_y(nodes):
    for a in range(4):
        first, last = nodes[4 * a], nodes[4 * a + 3]
        nodes[4 * a] = first + shifted(last, 1)
        nodes[4 * a + 3] = last + shifted(first, -1)


def summed_line(line):
    first, last = line[0:16], line[48:64]
    return jnp.concatenate(
        [first + shifted(last, 1), line[16:48], last + shifted(first, -1)], axis=0
    )


def averaged(line):
    line = summed_line(line)
    return jnp.concatenate(
        [
            sum(
                float(HALVES[i, a] * ONE_D[a]) * line[16 * a : 16 * a + 16] for a in range(4)
            )
            for i in range(2)
        ],
        axis=0,
    )


def held_nodes(held, before, next_first):
    nodes = [held[16 * n : 16 * n + 16] for n in range(NP)]
    for b in range(4):
        nodes[b] = nodes[b] + before[16 * b : 16 * b + 16]
        if next_first is not None:
            nodes[12 + b] = nodes[12 + b] + next_first[b]
    return nodes


def front_kernel(
    sizes,
    span_y,
    cell_smem,
    cell_ref,
    group_ref,
    stiff_ref,
    state_ref,
    columns_out,
    blocks_out,
    q_ref,
    x_one,
    x_two,
    y_one,
    y_two,
    raw,
    sems,
    hi_ref,
    lo_ref,
    operators,
    held,
    before,
    lines,
    ends,
    columns,
    blocks_ref,
    out_sem,
):
    devices = sizes[0] * sizes[1]
    width = held.shape[1]
    for chunk in range(CHUNKS):
        state_copy(state_ref, raw, sems, chunk).start()
    place_operators(tile_operators(span_y, cell_ref[...], stiff_ref[...]), operators)
    high, low, q_ref[...] = column_requests(
        devices, group_ref.shape[1] // devices, group_ref[...]
    )
    first = iota((devices, 8, 128), 1) == 0
    blocks_ref[...] = jnp.where(first, high[:, None, :], low[:, None, :])
    place_states(span_y, cell_smem, state_ref, raw, sems, hi_ref, lo_ref)
    before[...] = jnp.zeros_like(before)
    held[...] = jnp.zeros_like(held)

    def emit(row, next_first):
        nodes = held_nodes(held, before, next_first)
        along = [
            [
                sum(float(HALVES[i, a] * ONE_D[a]) * nodes[4 * a + b] for a in range(4))
                for b in range(4)
            ]
            for i in range(2)
        ]
        for i in range(2):
            for j in range(2):
                columns[pl.ds(pl.multiple_of(row * 64 + (2 * i + j) * 16, 16), 16)] = sum(
                    float(HALVES[j, b] * ONE_D[b]) * along[i][b] for b in range(4)
                )

    def one_row(row, _):
        points = row_points(row, operators, hi_ref, lo_ref)

        ends[0, jnp.minimum(row, 1)] = points[0:64]
        ends[1, jnp.maximum(row - EXD + 2, 0)] = points[192:256]
        nodes = [points[16 * n : 16 * n + 16] for n in range(NP)]
        for a in range(4):
            lines[0, pl.ds(16 * a + row, 1)] = nodes[4 * a][0:1]
            lines[1, pl.ds(16 * a + row, 1)] = nodes[4 * a + 3][15:16]
        sum_along_y(nodes)
        emit(jnp.maximum(row - 1, 0), nodes[0:4])
        before[...] = held[192:256]
        for n in range(NP):
            held[16 * n : 16 * n + 16] = nodes[n]
        return 0

    def send(part):
        rows = pl.ds(part * (columns.shape[0] // 2), columns.shape[0] // 2)
        return pltpu.make_async_copy(columns.at[rows], columns_out.at[rows], out_sem.at[part])

    lax.fori_loop(0, EXD // 2 + 2, one_row, 0, unroll=2)
    send(0).start()
    lax.fori_loop(EXD // 2 + 2, EXD, one_row, 0, unroll=2)
    emit(EXD - 1, None)
    send(1).start()
    for axis, low, high, one, two in (
        ("gx", ends[0, 0], ends[1, 1], x_one, x_two),
        ("gy", lines[0], lines[1], y_one, y_two),
    ):
        first, second = by_parity(axis, averaged(low), averaged(high))
        one[...] = first.astype(BF16)
        two[...] = second.astype(BF16)
    for step_x, row in ((-1, 0), (1, 3 * 16 + 15)):
        for step_y, side in ((-1, 0), (1, 1)):
            block = diagonal(sizes, step_x, step_y)
            point = lines[side, row : row + 1]
            for f in range(width // 128):
                blocks_ref[block, 2 + f : 3 + f] = point[:, f * 128 : (f + 1) * 128]
    blocks_out[...] = blocks_ref[...].astype(BF16)
    send(0).wait()
    send(1).wait()


def state_scratch(fields, elements, levels):
    width = fields * levels
    return [
        pltpu.VMEM((CHUNKS, fields, elements // CHUNKS, NP, levels), F32),
        pltpu.SemaphoreType.DMA((CHUNKS,)),
        pltpu.VMEM((elements, NP, width), BF16),
        pltpu.VMEM((elements, NP, width), BF16),
        pltpu.VMEM((EXD, 512, 256), BF16),
        pltpu.VMEM((256, width), F32),
        pltpu.VMEM((64, width), F32),
    ]


FRONT_LIMIT = 56


def front(cell, group, stiff, state, sizes):
    fields, elements, _, levels = state.shape
    width = fields * levels
    devices = sizes[0] * sizes[1]
    line = jax.ShapeDtypeStruct((32, width), BF16)
    return pl.pallas_call(
        functools.partial(front_kernel, sizes, EYD * sizes[1]),
        out_shape=(
            jax.ShapeDtypeStruct((4 * elements, width), F32),
            jax.ShapeDtypeStruct((devices, 8, 128), BF16),
            jax.ShapeDtypeStruct((1, 4 * elements), I32),
            line,
            line,
            line,
            line,
        ),
        in_specs=[SMEM, VMEM, VMEM, VMEM, ANY],
        out_specs=(ANY,) + (VMEM,) * 6,
        scratch_shapes=state_scratch(fields, elements, levels)
        + [
            pltpu.VMEM((2, 64, width), F32),
            pltpu.VMEM((2, 2, 64, width), F32),
            pltpu.VMEM((4 * elements, width), F32),
            pltpu.VMEM((devices, 8, 128), F32),
            pltpu.SemaphoreType.DMA((2,)),
        ],
        compiler_params=params(FRONT_LIMIT),
        cost_estimate=cost(4e9, 2e7),
        name="front",
    )(cell, cell.reshape(1, elements), group, stiff, state)


def dynamics_kernel(
    span_y,
    cell_smem,
    cell_ref,
    stiff_ref,
    state_ref,
    out_ref,
    lines_ref,
    raw,
    sems,
    hi_ref,
    lo_ref,
    operators,
    held,
    before,
    turned,
    ends,
    rows_out,
    out_sems,
):
    fields, _, levels = turned.shape
    for chunk in range(CHUNKS):
        state_copy(state_ref, raw, sems, chunk).start()
    place_operators(tile_operators(span_y, cell_ref[...], stiff_ref[...]), operators)
    place_states(span_y, cell_smem, state_ref, raw, sems, hi_ref, lo_ref)
    before[...] = jnp.zeros_like(before)
    held[...] = jnp.zeros_like(held)

    def emit(row, next_first):
        nodes = held_nodes(held, before, next_first)
        for n in range(NP):
            values = nodes[n] * float(ONE_D[n // 4] * ONE_D[n % 4])
            for f in range(fields):
                turned[f, 16 * n : 16 * n + 16] = values[:, f * levels : (f + 1) * levels]
        slot = row & 1
        for y in range(EYD):
            for f in range(fields):
                rows_out[slot, y, :, f * levels : (f + 1) * levels] = turned[
                    f, pl.ds(y, NP, stride=16)
                ]

    def copy_out(row):
        slot = row & 1
        return pltpu.make_async_copy(
            rows_out.at[slot], out_ref.at[pl.ds(row * EYD, EYD)], out_sems.at[slot]
        )

    def one_row(row, _):
        points = row_points(row, operators, hi_ref, lo_ref)
        nodes = [points[16 * n : 16 * n + 16] for n in range(NP)]
        ends[0, jnp.minimum(row, 1)] = points[0:64]
        ends[1, jnp.maximum(row - EXD + 2, 0)] = points[192:256]
        for a in range(4):
            lines_ref[2, pl.ds(16 * a + row, 1)] = nodes[4 * a][0:1]
            lines_ref[3, pl.ds(16 * a + row, 1)] = nodes[4 * a + 3][15:16]
        sum_along_y(nodes)

        @pl.when(row >= 3)
        def _():
            copy_out(row - 3).wait()

        @pl.when(row >= 1)
        def _():
            emit(row - 1, nodes[0:4])
            copy_out(row - 1).start()

        before[...] = held[192:256]
        for n in range(NP):
            held[16 * n : 16 * n + 16] = nodes[n]
        return 0

    lax.fori_loop(0, EXD, one_row, 0)
    copy_out(EXD - 3).wait()
    emit(EXD - 1, None)
    copy_out(EXD - 1).start()
    lines_ref[0] = ends[0, 0]
    lines_ref[1] = ends[1, 1]
    lines_ref[2] = summed_line(lines_ref[2])
    lines_ref[3] = summed_line(lines_ref[3])
    copy_out(EXD - 2).wait()
    copy_out(EXD - 1).wait()


def dynamics_rows(cell, stiff, state, span_y):
    fields, elements, _, levels = state.shape
    width = fields * levels
    return pl.pallas_call(
        functools.partial(dynamics_kernel, span_y),
        out_shape=(
            jax.ShapeDtypeStruct((elements, NP, width), F32),
            jax.ShapeDtypeStruct((4, 64, width), F32),
        ),
        in_specs=[SMEM, VMEM, VMEM, ANY],
        out_specs=(ANY, VMEM),
        scratch_shapes=state_scratch(fields, elements, levels)
        + [
            pltpu.VMEM((fields, 256, levels), F32),
            pltpu.VMEM((2, 2, 64, width), F32),
            pltpu.VMEM((2, EYD, NP, width), F32),
            pltpu.SemaphoreType.DMA((2,)),
        ],
        compiler_params=params(DYN_LIMIT),
        cost_estimate=cost(4e9, 2e7),
        name="dynamics_rows",
    )(cell, cell.reshape(1, elements), stiff, state)


def message_kernel(x_two, x_one, south_ref, north_ref, table, y_one, y_two):
    both = jnp.concatenate(from_neighbours("gx", x_one[...], x_two[...]), axis=0)
    add = dot(table[...], both)
    one, two = by_parity("gy", south_ref[...] + add[0:64], north_ref[...] + add[64:128])
    y_one[...] = one.astype(BF16)
    y_two[...] = two.astype(BF16)


def messages(one, two, south, north, table):
    width = one.shape[1]
    return pl.pallas_call(
        message_kernel,
        out_shape=(jax.ShapeDtypeStruct((64, width), BF16),) * 2,
        in_specs=[VMEM] * 5,
        out_specs=(VMEM,) * 2,
        compiler_params=params(16),
        cost_estimate=cost(4e7, 6e5),
        name="line_messages",
    )(two, one, south, north, table)


def pairs(axis, first):
    count = lax.axis_size(axis)
    low = range(0 if first else 1, count, 2)
    return [(i, (i + 1) % count) for i in low] + [((i + 1) % count, i) for i in low]


def exchange(axis, one, two):
    second = lax.ppermute(two, axis, pairs(axis, False))
    return lax.ppermute(one, axis, pairs(axis, True)), second


def by_parity(axis, to_low, to_high):
    even = (lax.axis_index(axis) & 1) == 0
    return jnp.where(even, to_high, to_low), jnp.where(even, to_low, to_high)


def from_neighbours(axis, one, two):
    even = (lax.axis_index(axis) & 1) == 0
    return jnp.where(even, two, one), jnp.where(even, one, two)


def send_kernel(
    sizes,
    span_y,
    columns_hbm,
    table_hbm,
    y_two,
    x_two,
    y_one,
    x_one,
    blocks_in,
    cell_ref,
    out_ref,
    place_ref,
    columns_ref,
    table_ref,
    lines_ref,
    blocks_ref,
    rounded,
    pick,
    sems,
):
    count, width = columns_ref.shape
    devices = sizes[0] * sizes[1]
    per_peer = count // devices
    table_copy = pltpu.make_async_copy(table_hbm, table_ref, sems.at[0])
    table_copy.start()
    copy = pltpu.make_async_copy(columns_hbm, columns_ref, sems.at[1])
    copy.start()
    blocks_ref[...] = blocks_in[...].astype(F32)
    spread_out = one_hot((iota((128, count), 1) & (per_peer - 1)) == iota((128, count), 0))
    shift = per_peer.bit_length() - 1
    own = (iota((devices, count), 1) >> shift) == iota((devices, count), 0)
    wide = dot(blocks_ref[:, 0, :].astype(BF16), spread_out) * 32.0 + dot(
        blocks_ref[:, 1, :].astype(BF16), spread_out
    )
    requested = jnp.sum(jnp.where(own, wide, 0.0), axis=0, keepdims=True).astype(I32)
    elements = cell_ref.shape[1]
    marks = one_hot((requested >> 2) == iota((elements, count), 0))
    tile_row = tile_number(cell_ref[...], span_y).astype(F32)
    tile_row = jnp.broadcast_to(tile_row, (8, elements)).astype(BF16)
    tile = dot(tile_row, marks)[0:1].astype(I32)
    place = (tile >> 4) * 64 + (requested & 3) * 16 + (tile & 15)
    place_ref[...] = place
    for start in range(0, count, 128):
        column = as_columns(place, start)
        for other in range(0, count, 128):
            pick[start : start + 128, other : other + 128] = one_hot(
                column == iota((128, 128), 1) + other
            )

    lines_ref[0], lines_ref[1] = from_neighbours(
        "gy", y_one[...].astype(F32), y_two[...].astype(F32)
    )
    for side, step_y in enumerate((-1, 1)):
        for step_x, a, x in ((-1, 0, 0), (1, 3, EXD - 1)):
            block = diagonal(sizes, step_x, step_y)
            for i in range(2):
                weight = float(HALVES[i, a] * ONE_D[a])
                for f in range(width // 128):
                    lines_ref[side, 16 * i + x : 16 * i + x + 1, f * 128 : (f + 1) * 128] += (
                        weight * blocks_ref[block, 2 + f : 3 + f]
                    )
    lines = jnp.concatenate([lines_ref[0], lines_ref[1]], axis=0).astype(BF16)
    west, east = from_neighbours("gx", x_one[...].astype(F32), x_two[...].astype(F32))
    west, east = (
        jnp.concatenate([float(HALVES[i, a] * ONE_D[a]) * line for i in range(2)], axis=0)
        for line, a in ((west, 0), (east, 3))
    )
    table_copy.wait()
    add = dot_twice(table_ref[...], lines)
    copy.wait()
    rounded[...] = (columns_ref[...] + add).astype(BF16)
    rounded[0:64] = (columns_ref[0:64] + add[0:64] + west).astype(BF16)
    rounded[count - 64 : count] = (
        columns_ref[count - 64 : count] + add[count - 64 : count] + east
    ).astype(BF16)
    out_ref[...] = dot(pick[...], rounded[...]).astype(BF16)


def send_columns(columns, halos, blocks, cell, sizes):
    count, width = columns.shape
    table = np.concatenate(hi_lo_arrays(TABLES["col_y"]), axis=1)
    return pl.pallas_call(
        functools.partial(send_kernel, sizes, EYD * sizes[1]),
        out_shape=(
            jax.ShapeDtypeStruct((count, width), BF16),
            jax.ShapeDtypeStruct((1, count), I32),
        ),
        in_specs=[ANY, ANY] + [VMEM] * 6,
        out_specs=(VMEM,) * 2,
        scratch_shapes=[
            pltpu.VMEM((count, width), F32),
            pltpu.VMEM(table.shape, BF16),
            pltpu.VMEM((2, 32, width), F32),
            pltpu.VMEM(blocks.shape, F32),
            pltpu.VMEM((count, width), BF16),
            pltpu.VMEM((count, count), BF16),
            pltpu.SemaphoreType.DMA((2,)),
        ],
        compiler_params=params(SEND_LIMIT),
        cost_estimate=cost(2e9, 5e6),
        name="send_columns",
    )(columns, jnp.asarray(table), halos[3], halos[1], halos[2], halos[0], blocks, cell)


SEND_LIMIT = 60
DYN_LIMIT = 56


def physics_kernel(
    fields, incoming_ref, q_ref, inverse_hbm, out_ref, inverse, tendency, sem
):
    count, width = incoming_ref.shape
    levels = width // fields
    copy = pltpu.make_async_copy(inverse_hbm, inverse, sem)
    copy.start()
    q = q_ref[...]
    size = count // PARTS
    for part in range(PARTS):
        pick = []
        for start in range(part * size, (part + 1) * size, 128):
            column = as_columns(q, start)
            pick.append(
                jnp.concatenate(
                    [
                        one_hot(column == iota((128, 128), 1) + other)
                        for other in range(0, count, 128)
                    ],
                    axis=1,
                )
            )
        physics = dot(jnp.concatenate(pick, axis=0), incoming_ref[...])
        if part == 0:
            copy.wait()
        for group in range(size // GROUP_COLS):
            rows = physics[group * GROUP_COLS : (group + 1) * GROUP_COLS]
            stacked = jnp.concatenate(
                [rows[:, f * levels : (f + 1) * levels] for f in range(fields)], axis=0
            )
            whole = part * (size // GROUP_COLS) + group
            result = dot_nt(stacked.astype(BF16), inverse[whole]) - stacked
            tendency[whole * GROUP_COLS : (whole + 1) * GROUP_COLS] = jnp.concatenate(
                [result[f * GROUP_COLS : (f + 1) * GROUP_COLS] for f in range(fields)], axis=1
            ).astype(BF16)
    for start in range(0, count, size):
        pick = one_hot(q == iota((size, count), 0) + start)
        out_ref[start : start + size] = dot(pick, tendency[...]).astype(BF16)


def physics_step(incoming, q, inverse, fields):
    count, width = incoming.shape
    return pl.pallas_call(
        functools.partial(physics_kernel, fields),
        out_shape=jax.ShapeDtypeStruct((count, width), BF16),
        in_specs=[VMEM, VMEM, ANY],
        out_specs=VMEM,
        scratch_shapes=[
            pltpu.VMEM(inverse.shape, BF16),
            pltpu.VMEM((count, width), BF16),
            pltpu.SemaphoreType.DMA,
        ],
        compiler_params=params(PHYSICS_LIMIT),
        cost_estimate=cost(3e9, 5e6),
        name="physics",
    )(incoming, q, inverse)


PHYSICS_LIMIT = 16
PARTS = 2


def unpack_kernel(
    received_ref,
    place_ref,
    own_lines,
    lines_table,
    back_ref,
    x_one,
    x_two,
    south_ref,
    north_ref,
    pick,
):
    count = received_ref.shape[0]
    place = place_ref[...]
    for start in range(0, count, 128):
        pick[start : start + 128] = one_hot(place == iota((128, count), 0) + start)
    back_ref[...] = dot(pick[...], received_ref[...]).astype(BF16)
    ends = []
    for kind, (first, a) in enumerate(((0, 0), (count - 64, 3))):
        rows = back_ref[first : first + 64].astype(F32)
        half = [
            sum(float(SPREAD[a, i]) * rows[32 * i + 16 * j : 32 * i + 16 * j + 16] for i in range(2))
            for j in range(2)
        ]
        nodes = [sum(float(SPREAD[b, j]) * half[j] for j in range(2)) for b in range(4)]
        ends.append(own_lines[kind] + jnp.concatenate(nodes, axis=0))
    one, two = by_parity("gx", *ends)
    x_one[...] = one.astype(BF16)
    x_two[...] = two.astype(BF16)
    lines = dot(lines_table[...], back_ref[...])
    south_ref[...] = own_lines[2] + lines[0:64] + lines[128:192]
    north_ref[...] = own_lines[3] + lines[64:128] + lines[192:256]


def unpack(received, place, own_lines):
    count, width = received.shape
    table = jnp.asarray(np.concatenate(hi_lo_arrays(TABLES["lines"]), axis=0))
    return pl.pallas_call(
        unpack_kernel,
        out_shape=(
            jax.ShapeDtypeStruct((count, width), BF16),
            jax.ShapeDtypeStruct((64, width), BF16),
            jax.ShapeDtypeStruct((64, width), BF16),
            jax.ShapeDtypeStruct((64, width), F32),
            jax.ShapeDtypeStruct((64, width), F32),
        ),
        in_specs=[VMEM] * 4,
        out_specs=(VMEM,) * 5,
        scratch_shapes=[pltpu.VMEM((count, count), BF16)],
        compiler_params=params(16),
        cost_estimate=cost(2e9, 4e6),
        name="unpack",
    )(received, place, own_lines, table)


def inner_kernel(dynamics_ref, back_ref, table_ref, total):
    width = total.shape[2]
    count = back_ref.shape[0]

    def near_sum(row, first, rows, skip):
        near = back_ref[pl.ds(first, rows)]
        both = dot(table_ref[:, skip : skip + rows], near)
        at = pl.ds(row * EYD, 2 * EYD)
        sums = both[0:512] + both[512:1024]
        total[at] = dynamics_ref[at] + sums.reshape(2 * EYD, NP, width)

    near_sum(0, 0, 192, 64)
    near_sum(EXD - 2, count - 192, 192, 0)

    def middle(pair, _):
        near_sum(pair * 2, pl.multiple_of(pair * 128 - 64, 64), 256, 0)
        return 0

    lax.fori_loop(1, EXD // 2 - 1, middle, 0, unroll=2)


def inner_sum(dynamics, back):
    one = TABLES["final"].reshape(EYD * NP, 3, 64)
    two = np.zeros((2, EYD * NP, 4, 64))
    two[0, :, 0:3] = one
    two[1, :, 1:4] = one
    table = np.concatenate(hi_lo_arrays(two.reshape(2 * EYD * NP, 256)), axis=0)
    return pl.pallas_call(
        inner_kernel,
        out_shape=jax.ShapeDtypeStruct(dynamics.shape, F32),
        in_specs=[VMEM] * 3,
        out_specs=VMEM,
        input_output_aliases={0: 0},
        compiler_params=params(16),
        cost_estimate=cost(4e9, 2e7),
        name="inner_sum",
    )(dynamics, back, jnp.asarray(table))


def to_slots_kernel(span_y, cell_smem, total, out_ref, slot_ref, buffer, sems):
    elements, _, width = total.shape
    fields, levels = buffer.shape[1], buffer.shape[4]
    per = elements // CHUNKS

    def copy(chunk):
        return pltpu.make_async_copy(
            buffer.at[chunk], out_ref.at[:, pl.ds(chunk * per, per)], sems.at[chunk]
        )

    for chunk in range(CHUNKS):

        def take_slots(i, _, chunk=chunk):
            for u in range(4):
                k = i * 4 + u
                tile = tile_number(cell_smem[chunk * per + k], span_y)
                slot_ref[0, tile] = chunk * per + k
                for f in range(fields):
                    buffer[chunk, f, k] = total[tile, :, f * levels : (f + 1) * levels]
            return 0

        lax.fori_loop(0, per // 4, take_slots, 0)
        copy(chunk).start()
    for chunk in range(CHUNKS):
        copy(chunk).wait()


def to_slots(cell, total, fields, span_y):
    elements, _, width = total.shape
    levels = width // fields
    return pl.pallas_call(
        functools.partial(to_slots_kernel, span_y),
        out_shape=(
            jax.ShapeDtypeStruct((fields, elements, NP, levels), F32),
            jax.ShapeDtypeStruct((1, elements), I32),
        ),
        in_specs=[SMEM, VMEM],
        out_specs=(ANY, SMEM),
        scratch_shapes=[
            pltpu.VMEM((CHUNKS, fields, elements // CHUNKS, NP, levels), F32),
            pltpu.SemaphoreType.DMA((CHUNKS,)),
        ],
        compiler_params=params(16),
        cost_estimate=cost(4e9, 2e7),
        name="to_slots",
    )(cell, total)


def border_kernel(
    fields, slot_ref, y_two, y_one, x_two, x_one, total_ref, table_ref, _, out_ref, buffer, sem
):
    width = x_one.shape[1]
    levels = width // fields
    halos = from_neighbours("gx", x_one[...], x_two[...])
    halos = halos + from_neighbours("gy", y_one[...], y_two[...])
    adds = []
    for kind, halo in enumerate(halos):
        table = table_ref[kind * 256 : kind * 256 + 256]
        adds.append(dot(table, halo).reshape(16, NP, width))
    for kind in range(4):
        for k in range(16):
            if kind >= 2 and k in (0, 15):
                continue
            tile = (k, (EXD - 1) * EYD + k, k * EYD, k * EYD + EYD - 1)[kind]
            whole = total_ref[tile] + adds[kind][k]
            if kind < 2 and k in (0, 15):
                whole = whole + adds[2 if k == 0 else 3][0 if kind == 0 else 15]
            for f in range(fields):
                buffer[kind, f, k] = whole[:, f * levels : (f + 1) * levels]
            pltpu.make_async_copy(
                buffer.at[kind, :, k], out_ref.at[:, slot_ref[0, tile]], sem.at[kind]
            ).start()
    for kind in range(4):
        part = buffer.at[kind] if kind < 2 else buffer.at[kind, :, 1:15]
        pltpu.make_async_copy(part, part, sem.at[kind]).wait()


def border_sum(slot, halos, total, out):
    fields, levels = out.shape[0], out.shape[3]
    table = jnp.asarray(TABLES["border"].astype(np.float32).astype(jnp.bfloat16))
    return pl.pallas_call(
        functools.partial(border_kernel, fields),
        out_shape=jax.ShapeDtypeStruct(out.shape, F32),
        in_specs=[SMEM] + [VMEM] * 6 + [ANY],
        out_specs=ANY,
        scratch_shapes=[
            pltpu.VMEM((4, fields, 16, NP, levels), F32),
            pltpu.SemaphoreType.DMA((4,)),
        ],
        input_output_aliases={7: 0},
        compiler_params=params(16),
        cost_estimate=cost(2e8, 4e6),
        name="border_sum",
    )(slot, *halos[::-1], total, table, out)


def regroup(blocks):
    return lax.all_to_all(blocks, ("gx", "gy"), split_axis=0, concat_axis=0, tiled=True)


def per_device(state_in, stiffness, elem_cell, group_column, group_inverse):
    fields, elements = state_in.shape[:2]
    sizes = (lax.axis_size("gx"), lax.axis_size("gy"))
    columns_dev = 4 * elements
    span_y = EYD * sizes[1]
    stiff = stiffness.reshape(NP * NP, elements)

    columns, blocks, q, x_one, x_two, y_one, y_two = front(
        elem_cell, group_column.reshape(1, columns_dev), stiff, state_in, sizes
    )
    hy = exchange("gy", y_one, y_two)
    hx = exchange("gx", x_one, x_two)
    blocks = regroup(blocks)

    outgoing, place = send_columns(
        columns, (*hx, *hy), blocks, elem_cell.reshape(1, elements), sizes
    )
    incoming = regroup(outgoing)
    dynamics, own_lines = dynamics_rows(elem_cell, stiff, state_in, span_y)
    incoming, dynamics, own_lines = lax.optimization_barrier((incoming, dynamics, own_lines))
    received = regroup(physics_step(incoming, q, group_inverse, fields))

    back, x_one, x_two, south, north = unpack(received, place, own_lines)
    bx = exchange("gx", x_one, x_two)
    by = exchange("gy", *messages(*bx, south, north, bf16_table("corner_pt")))
    total = inner_sum(dynamics, back)
    inner, slot = to_slots(elem_cell, total, fields, span_y)
    return border_sum(slot, (*bx, *by), total, inner)


def solution(mesh):
    placed = (
        P(None, ("gx", "gy"), None, None),
        P(None, None, ("gx", "gy")),
        P(("gx", "gy")),
        P(("gx", "gy")),
        P(("gx", "gy"), None, None),
    )
    return jax.shard_map(
        per_device,
        mesh=mesh,
        in_specs=placed,
        out_specs=P(None, ("gx", "gy"), None, None),
        check_vma=False,
    )
```

```python
import functools
import math

import jax
import jax.numpy as jnp
import numpy as np
from jax import lax
from jax.experimental import pallas as pl
from jax.experimental.pallas import tpu as pltpu
from jax.sharding import PartitionSpec as P

GROUP_COLS = 16
EXD = 16
EYD = 16
NP = 16
F32 = jnp.float32
BF16 = jnp.bfloat16
I32 = jnp.int32
MB = 1024 * 1024


def lagrange_value(node_index, position, gll_nodes):
    running = 1.0
    for other_index in range(4):
        if other_index != node_index:
            running = (
                running
                * (position - gll_nodes[other_index])
                / (gll_nodes[node_index] - gll_nodes[other_index])
            )
    return running


def half_tables():
    gll_nodes = [-1.0, -1.0 / math.sqrt(5.0), 1.0 / math.sqrt(5.0), 1.0]
    halves = np.zeros((2, 4))
    for half_index, (lower_end, upper_end) in enumerate(((-1.0, 0.0), (0.0, 1.0))):
        centre = 0.5 * (lower_end + upper_end)
        offset = 0.5 * (upper_end - lower_end) / math.sqrt(3.0)
        for node in range(4):
            first = lagrange_value(node, centre - offset, gll_nodes)
            second = lagrange_value(node, centre + offset, gll_nodes)
            halves[half_index, node] = 0.5 * (upper_end - lower_end) * (first + second)
    product = halves @ halves.T
    determinant = product[0, 0] * product[1, 1] - product[0, 1] * product[1, 0]
    inverse = (
        np.array([[product[1, 1], -product[0, 1]], [-product[1, 0], product[0, 0]]]) / determinant
    )
    spread = halves.T @ inverse
    return halves.astype(np.float32), spread.astype(np.float32)


HALVES, SPREAD = half_tables()
ONE_D = np.array([0.5, 1.0, 1.0, 0.5])


def shift_down(n):
    return np.eye(n, k=-1)


def local_pass(n):
    table = np.einsum("ab,xy->axby", np.eye(4), np.eye(n))
    table[0, :, 3, :] += shift_down(n)
    table[3, :, 0, :] += shift_down(n).T
    return table


def constant_tables():
    h = HALVES.astype(np.float64)
    s = SPREAD.astype(np.float64)
    w = ONE_D
    eye = np.eye(EXD)
    line = local_pass(EYD)
    col_y = np.zeros((EXD, 2, 2, EYD, 2, 2, EXD))
    for side, (b, y) in enumerate(((0, 0), (3, EYD - 1))):
        col_y[:, :, :, y, side] = np.einsum("j,ik,xz->xijkz", h[:, b] * w[b], np.eye(2), eye)
    col_y = col_y.reshape(EXD * 4 * EYD, 2 * 2 * EXD)
    nodes = np.einsum("ai,bj,yz->abyijz", s, s, np.eye(EYD))
    across = np.zeros((4, 4, EYD, 3, 2, 2, EYD))
    across[:, :, :, 1] = nodes
    across[0, :, :, 0] = nodes[3]
    across[3, :, :, 2] = nodes[0]
    full = np.einsum("byez,aezdijt->abydijt", line, across)
    full = full * w[:, None, None, None, None, None, None] * w[:, None, None, None, None, None]
    final = full.reshape(NP * EYD, 3 * 4 * EYD)
    along = local_pass(EXD)
    lines = np.zeros((2, 4, EXD, EXD, 2, 2, EYD))
    corner_pt = np.zeros((2, 4, EXD, 2, 4, EYD))
    for side, (b, y) in enumerate(((0, 0), (3, EYD - 1))):
        lines[side, :, :, :, :, :, y] = np.einsum("axcz,ci,j->axzij", along, s, s[b])
        corner_pt[side, 0, 0, 0, b, y] = 1.0
        corner_pt[side, 3, EXD - 1, 1, b, y] = 1.0
    lines = lines.reshape(2 * 4 * EXD, EXD * 4 * EYD)
    corner_pt = corner_pt.reshape(2 * 4 * EXD, 2 * 4 * EYD)
    border = np.zeros((4, EYD, NP, 64))
    order = full.transpose(2, 0, 1, 3, 4, 5, 6).reshape(EYD, NP, 3, 4 * EYD)
    for kind, a in enumerate((0, 3)):
        border[kind, :, 4 * a : 4 * a + 4] = np.einsum("b,byez->ybez", w[a] * w, line).reshape(
            EYD, 4, 4 * EYD
        )
    for side, b in enumerate((0, 3)):
        for a in range(4):
            for x in range(EXD):
                border[2 + side, x, 4 * a + b, 16 * a + x] = w[a] * w[b]
    return dict(
        col_y=col_y,
        final=order.reshape(EYD * NP, 3 * 4 * EYD),
        lines=lines,
        corner_pt=corner_pt,
        border=border.reshape(4 * EYD * NP, 64),
    )


def hi_lo_arrays(table):
    hi = np.asarray(table, np.float32).astype(jnp.bfloat16)
    lo = (np.asarray(table, np.float32) - hi.astype(np.float32)).astype(jnp.bfloat16)
    return hi, lo


def hi_lo(table):
    return jnp.asarray(np.concatenate(hi_lo_arrays(table), axis=1))


TABLES = constant_tables()


def bf16_table(name):
    return jnp.asarray(TABLES[name].astype(np.float32).astype(jnp.bfloat16))


def dot(left, right):
    return jnp.dot(left, right, preferred_element_type=F32)


def dot_nt(left, right):
    return lax.dot_general(left, right, (((1,), (1,)), ((), ())), preferred_element_type=F32)


def dot_twice(table, right):
    return dot(table, jnp.concatenate([right, right], axis=0))


def split(values):
    hi = values.astype(BF16)
    return hi, (values - hi.astype(F32)).astype(BF16)


def iota(shape, dim):
    return lax.broadcasted_iota(I32, shape, dim)


def one_hot(condition):
    return jnp.where(condition, 1.0, 0.0).astype(BF16)


def as_columns(row, start):
    piece = row[:, start : start + 128].astype(F32)
    return jnp.transpose(jnp.broadcast_to(piece, (128, 128))).astype(I32)


def tile_number(cell, span_y):
    shift = span_y.bit_length() - 1
    assert span_y == 1 << shift
    return ((cell >> shift) & (EXD - 1)) * EYD + (cell & (EYD - 1))


VMEM = pl.BlockSpec(memory_space=pltpu.VMEM)
SMEM = pl.BlockSpec(memory_space=pltpu.SMEM)
ANY = pl.BlockSpec(memory_space=pl.ANY)


def params(mib):
    return pltpu.CompilerParams(vmem_limit_bytes=mib * MB)


def cost(flops, moved):
    return pl.CostEstimate(flops=int(flops), bytes_accessed=int(moved), transcendentals=0)


def column_requests(devices, per_peer, group):
    columns_dev = devices * per_peer
    shift = columns_dev.bit_length() - 1
    source = group >> shift
    local = group & (columns_dev - 1)
    of_source = source == iota((devices, columns_dev), 0)
    marks = one_hot(of_source)
    upper = one_hot(iota((128, 128), 0) <= iota((128, 128), 1))
    before = jnp.zeros((devices, 1), F32)
    ranks = []
    for start in range(0, columns_dev, 128):
        piece = marks[:, start : start + 128]
        counts = dot(piece, upper) + before
        ranks.append(counts)
        before = counts[:, 127:128]
    counts = jnp.concatenate(ranks, axis=1)
    rank = jnp.sum(jnp.where(of_source, counts, 0.0), axis=0, keepdims=True).astype(I32) - 1
    of_rank = one_hot(rank == iota((128, columns_dev), 0))
    high = jnp.where(of_source, (local >> 5).astype(F32), 0.0).astype(BF16)
    low = jnp.where(of_source, (local & 31).astype(F32), 0.0).astype(BF16)
    return dot_nt(high, of_rank), dot_nt(low, of_rank), source * per_peer + rank


def diagonal(sizes, step_x, step_y):
    count_x, count_y = sizes
    x = lax.rem(lax.axis_index("gx") + step_x + count_x, count_x)
    y = lax.rem(lax.axis_index("gy") + step_y + count_y, count_y)
    return x * count_y + y


CHUNKS = 8


def state_copy(state_ref, raw, sems, chunk):
    per = raw.shape[2]
    return pltpu.make_async_copy(
        state_ref.at[:, pl.ds(chunk * per, per)], raw.at[chunk], sems.at[chunk]
    )


def tile_operators(span_y, cell, stiff):
    elements = cell.shape[1]
    marks = one_hot(tile_number(cell, span_y) == iota((elements, elements), 0))
    row = iota(stiff.shape, 0)
    stiff = stiff + jnp.where((row >> 4) == (row & 15), 1.0, 0.0)
    hi, lo = split(stiff)
    return dot_nt(marks, hi), dot_nt(marks, lo)


def place_operators(parts, operators):
    row, col = iota((256, 256), 0), iota((256, 256), 1)
    same_elem = one_hot((row & 15) == (col >> 4))
    tiling = one_hot((row & 15) == (col & 15))
    column = iota((EYD, 256), 1) >> 4
    for x in range(EXD):
        stacked = jnp.concatenate(
            [
                jnp.where(column == n, part[x * EYD : (x + 1) * EYD], 0.0).astype(BF16)
                for part in parts
                for n in range(NP)
            ],
            axis=0,
        )
        placed = dot(stacked, tiling).astype(BF16)
        operators[x, 0:256] = placed[0:256] * same_elem
        operators[x, 256:512] = placed[256:512] * same_elem


def place_states(span_y, cell_smem, state_ref, raw, sems, hi_ref, lo_ref):
    fields, per, _, levels = raw.shape[1:]
    for chunk in range(CHUNKS):
        state_copy(state_ref, raw, sems, chunk).wait()

        def place_slots(i, _, chunk=chunk):
            for u in range(4):
                k = i * 4 + u
                where = tile_number(cell_smem[chunk * per + k], span_y)
                for f in range(fields):
                    hi, lo = split(raw[chunk, f, k])
                    hi_ref[where, :, f * levels : (f + 1) * levels] = hi
                    lo_ref[where, :, f * levels : (f + 1) * levels] = lo
            return 0

        lax.fori_loop(0, per // 4, place_slots, 0, unroll=2)


def row_points(row, operators, hi_ref, lo_ref):
    width = hi_ref.shape[2]
    at = pl.ds(pl.multiple_of(row * EYD, EYD), EYD)
    hi = hi_ref[at].reshape(EYD * NP, width)
    lo = lo_ref[at].reshape(EYD * NP, width)
    both = dot(operators[row], hi)
    return both[0:256] + both[256:512] + dot(operators[row, 0:256], lo)


def shifted(values, step):
    rows = values.shape[0]
    moved = pltpu.roll(values, step % rows, 0)
    free = 0 if step > 0 else rows - 1
    return jnp.where(iota(values.shape, 0) == free, 0.0, moved)


def sum_along_y(nodes):
    for a in range(4):
        first, last = nodes[4 * a], nodes[4 * a + 3]
        nodes[4 * a] = first + shifted(last, 1)
        nodes[4 * a + 3] = last + shifted(first, -1)


def summed_line(line):
    first, last = line[0:16], line[48:64]
    return jnp.concatenate(
        [first + shifted(last, 1), line[16:48], last + shifted(first, -1)], axis=0
    )


def averaged(line):
    line = summed_line(line)
    return jnp.concatenate(
        [
            sum(
                float(HALVES[i, a] * ONE_D[a]) * line[16 * a : 16 * a + 16] for a in range(4)
            )
            for i in range(2)
        ],
        axis=0,
    )


def held_nodes(held, before, next_first):
    nodes = [held[16 * n : 16 * n + 16] for n in range(NP)]
    for b in range(4):
        nodes[b] = nodes[b] + before[16 * b : 16 * b + 16]
        if next_first is not None:
            nodes[12 + b] = nodes[12 + b] + next_first[b]
    return nodes


def front_kernel(
    sizes,
    span_y,
    cell_smem,
    cell_ref,
    group_ref,
    stiff_ref,
    state_ref,
    columns_out,
    blocks_out,
    q_ref,
    x_one,
    x_two,
    y_one,
    y_two,
    raw,
    sems,
    hi_ref,
    lo_ref,
    operators,
    held,
    before,
    lines,
    ends,
    columns,
    blocks_ref,
    out_sem,
):
    devices = sizes[0] * sizes[1]
    width = held.shape[1]
    for chunk in range(CHUNKS):
        state_copy(state_ref, raw, sems, chunk).start()
    place_operators(tile_operators(span_y, cell_ref[...], stiff_ref[...]), operators)
    high, low, q_ref[...] = column_requests(
        devices, group_ref.shape[1] // devices, group_ref[...]
    )
    first = iota((devices, 8, 128), 1) == 0
    blocks_ref[...] = jnp.where(first, high[:, None, :], low[:, None, :])
    place_states(span_y, cell_smem, state_ref, raw, sems, hi_ref, lo_ref)
    before[...] = jnp.zeros_like(before)
    held[...] = jnp.zeros_like(held)

    def emit(row, next_first):
        nodes = held_nodes(held, before, next_first)
        along = [
            [
                sum(float(HALVES[i, a] * ONE_D[a]) * nodes[4 * a + b] for a in range(4))
                for b in range(4)
            ]
            for i in range(2)
        ]
        for i in range(2):
            for j in range(2):
                columns[pl.ds(pl.multiple_of(row * 64 + (2 * i + j) * 16, 16), 16)] = sum(
                    float(HALVES[j, b] * ONE_D[b]) * along[i][b] for b in range(4)
                )

    def one_row(row, _):
        points = row_points(row, operators, hi_ref, lo_ref)

        ends[0, jnp.minimum(row, 1)] = points[0:64]
        ends[1, jnp.maximum(row - EXD + 2, 0)] = points[192:256]
        nodes = [points[16 * n : 16 * n + 16] for n in range(NP)]
        for a in range(4):
            lines[0, pl.ds(16 * a + row, 1)] = nodes[4 * a][0:1]
            lines[1, pl.ds(16 * a + row, 1)] = nodes[4 * a + 3][15:16]
        sum_along_y(nodes)
        emit(jnp.maximum(row - 1, 0), nodes[0:4])
        before[...] = held[192:256]
        for n in range(NP):
            held[16 * n : 16 * n + 16] = nodes[n]
        return 0

    def send(part):
        rows = (pl.ds(0, 576), pl.ds(576, 256), pl.ds(832, 192))[part]
        return pltpu.make_async_copy(columns.at[rows], columns_out.at[rows], out_sem.at[part])

    lax.fori_loop(0, 10, one_row, 0, unroll=5)
    send(0).start()
    lax.fori_loop(10, 14, one_row, 0, unroll=4)
    send(1).start()
    lax.fori_loop(14, EXD, one_row, 0, unroll=2)
    emit(EXD - 1, None)
    send(2).start()
    for axis, low, high, one, two in (
        ("gx", ends[0, 0], ends[1, 1], x_one, x_two),
        ("gy", lines[0], lines[1], y_one, y_two),
    ):
        first, second = by_parity(axis, averaged(low), averaged(high))
        one[...] = first.astype(BF16)
        two[...] = second.astype(BF16)
    for step_x, row in ((-1, 0), (1, 3 * 16 + 15)):
        for step_y, side in ((-1, 0), (1, 1)):
            block = diagonal(sizes, step_x, step_y)
            point = lines[side, row : row + 1]
            for f in range(width // 128):
                blocks_ref[block, 2 + f : 3 + f] = point[:, f * 128 : (f + 1) * 128]
    blocks_out[...] = blocks_ref[...].astype(BF16)
    send(0).wait()
    send(1).wait()
    send(2).wait()


def state_scratch(fields, elements, levels):
    width = fields * levels
    return [
        pltpu.VMEM((CHUNKS, fields, elements // CHUNKS, NP, levels), F32),
        pltpu.SemaphoreType.DMA((CHUNKS,)),
        pltpu.VMEM((elements, NP, width), BF16),
        pltpu.VMEM((elements, NP, width), BF16),
        pltpu.VMEM((EXD, 512, 256), BF16),
        pltpu.VMEM((256, width), F32),
        pltpu.VMEM((64, width), F32),
    ]


FRONT_LIMIT = 56


def front(cell, group, stiff, state, sizes):
    fields, elements, _, levels = state.shape
    width = fields * levels
    devices = sizes[0] * sizes[1]
    line = jax.ShapeDtypeStruct((32, width), BF16)
    return pl.pallas_call(
        functools.partial(front_kernel, sizes, EYD * sizes[1]),
        out_shape=(
            jax.ShapeDtypeStruct((4 * elements, width), F32),
            jax.ShapeDtypeStruct((devices, 8, 128), BF16),
            jax.ShapeDtypeStruct((1, 4 * elements), I32),
            line,
            line,
            line,
            line,
        ),
        in_specs=[SMEM, VMEM, VMEM, VMEM, ANY],
        out_specs=(ANY,) + (VMEM,) * 6,
        scratch_shapes=state_scratch(fields, elements, levels)
        + [
            pltpu.VMEM((2, 64, width), F32),
            pltpu.VMEM((2, 2, 64, width), F32),
            pltpu.VMEM((4 * elements, width), F32),
            pltpu.VMEM((devices, 8, 128), F32),
            pltpu.SemaphoreType.DMA((3,)),
        ],
        compiler_params=params(FRONT_LIMIT),
        cost_estimate=cost(4e9, 2e7),
        name="front",
    )(cell, cell.reshape(1, elements), group, stiff, state)


def dynamics_kernel(
    span_y,
    cell_smem,
    cell_ref,
    stiff_ref,
    state_ref,
    out_ref,
    lines_ref,
    raw,
    sems,
    hi_ref,
    lo_ref,
    operators,
    held,
    before,
    turned,
    ends,
    rows_out,
    out_sems,
):
    fields, _, levels = turned.shape
    for chunk in range(CHUNKS):
        state_copy(state_ref, raw, sems, chunk).start()
    place_operators(tile_operators(span_y, cell_ref[...], stiff_ref[...]), operators)
    place_states(span_y, cell_smem, state_ref, raw, sems, hi_ref, lo_ref)
    before[...] = jnp.zeros_like(before)
    held[...] = jnp.zeros_like(held)

    def emit(row, next_first):
        nodes = held_nodes(held, before, next_first)
        for n in range(NP):
            values = nodes[n] * float(ONE_D[n // 4] * ONE_D[n % 4])
            for f in range(fields):
                turned[f, 16 * n : 16 * n + 16] = values[:, f * levels : (f + 1) * levels]
        slot = row & 1
        for y in range(EYD):
            for f in range(fields):
                rows_out[slot, y, :, f * levels : (f + 1) * levels] = turned[
                    f, pl.ds(y, NP, stride=16)
                ]

    def copy_out(row):
        slot = row & 1
        return pltpu.make_async_copy(
            rows_out.at[slot], out_ref.at[pl.ds(row * EYD, EYD)], out_sems.at[slot]
        )

    def one_row(row, _):
        points = row_points(row, operators, hi_ref, lo_ref)
        nodes = [points[16 * n : 16 * n + 16] for n in range(NP)]
        ends[0, jnp.minimum(row, 1)] = points[0:64]
        ends[1, jnp.maximum(row - EXD + 2, 0)] = points[192:256]
        for a in range(4):
            lines_ref[2, pl.ds(16 * a + row, 1)] = nodes[4 * a][0:1]
            lines_ref[3, pl.ds(16 * a + row, 1)] = nodes[4 * a + 3][15:16]
        sum_along_y(nodes)

        @pl.when(row >= 3)
        def _():
            copy_out(row - 3).wait()

        @pl.when(row >= 1)
        def _():
            emit(row - 1, nodes[0:4])
            copy_out(row - 1).start()

        before[...] = held[192:256]
        for n in range(NP):
            held[16 * n : 16 * n + 16] = nodes[n]
        return 0

    lax.fori_loop(0, EXD, one_row, 0)
    copy_out(EXD - 3).wait()
    emit(EXD - 1, None)
    copy_out(EXD - 1).start()
    lines_ref[0] = ends[0, 0]
    lines_ref[1] = ends[1, 1]
    lines_ref[2] = summed_line(lines_ref[2])
    lines_ref[3] = summed_line(lines_ref[3])
    copy_out(EXD - 2).wait()
    copy_out(EXD - 1).wait()


def dynamics_rows(cell, stiff, state, span_y):
    fields, elements, _, levels = state.shape
    width = fields * levels
    return pl.pallas_call(
        functools.partial(dynamics_kernel, span_y),
        out_shape=(
            jax.ShapeDtypeStruct((elements, NP, width), F32),
            jax.ShapeDtypeStruct((4, 64, width), F32),
        ),
        in_specs=[SMEM, VMEM, VMEM, ANY],
        out_specs=(ANY, VMEM),
        scratch_shapes=state_scratch(fields, elements, levels)
        + [
            pltpu.VMEM((fields, 256, levels), F32),
            pltpu.VMEM((2, 2, 64, width), F32),
            pltpu.VMEM((2, EYD, NP, width), F32),
            pltpu.SemaphoreType.DMA((2,)),
        ],
        compiler_params=params(DYN_LIMIT),
        cost_estimate=cost(4e9, 2e7),
        name="dynamics_rows",
    )(cell, cell.reshape(1, elements), stiff, state)


def message_kernel(x_two, x_one, south_ref, north_ref, table, y_one, y_two):
    both = jnp.concatenate(from_neighbours("gx", x_one[...], x_two[...]), axis=0)
    add = dot(table[...], both)
    one, two = by_parity("gy", south_ref[...] + add[0:64], north_ref[...] + add[64:128])
    y_one[...] = one.astype(BF16)
    y_two[...] = two.astype(BF16)


def messages(one, two, south, north, table):
    width = one.shape[1]
    return pl.pallas_call(
        message_kernel,
        out_shape=(jax.ShapeDtypeStruct((64, width), BF16),) * 2,
        in_specs=[VMEM] * 5,
        out_specs=(VMEM,) * 2,
        compiler_params=params(16),
        cost_estimate=cost(4e7, 6e5),
        name="line_messages",
    )(two, one, south, north, table)


def pairs(axis, first):
    count = lax.axis_size(axis)
    low = range(0 if first else 1, count, 2)
    return [(i, (i + 1) % count) for i in low] + [((i + 1) % count, i) for i in low]


def exchange(axis, one, two):
    second = lax.ppermute(two, axis, pairs(axis, False))
    return lax.ppermute(one, axis, pairs(axis, True)), second


def by_parity(axis, to_low, to_high):
    even = (lax.axis_index(axis) & 1) == 0
    return jnp.where(even, to_high, to_low), jnp.where(even, to_low, to_high)


def from_neighbours(axis, one, two):
    even = (lax.axis_index(axis) & 1) == 0
    return jnp.where(even, two, one), jnp.where(even, one, two)


def send_kernel(
    sizes,
    span_y,
    columns_ref,
    table_ref,
    y_two,
    x_two,
    y_one,
    x_one,
    blocks_in,
    cell_ref,
    out_ref,
    place_ref,
    lines_ref,
    blocks_ref,
    rounded,
    pick,
):
    count, width = columns_ref.shape
    devices = sizes[0] * sizes[1]
    per_peer = count // devices
    blocks_ref[...] = blocks_in[...].astype(F32)
    spread_out = one_hot((iota((128, count), 1) & (per_peer - 1)) == iota((128, count), 0))
    shift = per_peer.bit_length() - 1
    own = (iota((devices, count), 1) >> shift) == iota((devices, count), 0)
    wide = dot(blocks_ref[:, 0, :].astype(BF16), spread_out) * 32.0 + dot(
        blocks_ref[:, 1, :].astype(BF16), spread_out
    )
    requested = jnp.sum(jnp.where(own, wide, 0.0), axis=0, keepdims=True).astype(I32)
    elements = cell_ref.shape[1]
    marks = one_hot((requested >> 2) == iota((elements, count), 0))
    tile_row = tile_number(cell_ref[...], span_y).astype(F32)
    tile_row = jnp.broadcast_to(tile_row, (8, elements)).astype(BF16)
    tile = dot(tile_row, marks)[0:1].astype(I32)
    place = (tile >> 4) * 64 + (requested & 3) * 16 + (tile & 15)
    place_ref[...] = place
    for start in range(0, count, 128):
        column = as_columns(place, start)
        for other in range(0, count, 128):
            pick[start : start + 128, other : other + 128] = one_hot(
                column == iota((128, 128), 1) + other
            )

    lines_ref[0], lines_ref[1] = from_neighbours(
        "gy", y_one[...].astype(F32), y_two[...].astype(F32)
    )
    for side, step_y in enumerate((-1, 1)):
        for step_x, a, x in ((-1, 0, 0), (1, 3, EXD - 1)):
            block = diagonal(sizes, step_x, step_y)
            for i in range(2):
                weight = float(HALVES[i, a] * ONE_D[a])
                for f in range(width // 128):
                    lines_ref[side, 16 * i + x : 16 * i + x + 1, f * 128 : (f + 1) * 128] += (
                        weight * blocks_ref[block, 2 + f : 3 + f]
                    )
    lines = jnp.concatenate([lines_ref[0], lines_ref[1]], axis=0).astype(BF16)
    west, east = from_neighbours("gx", x_one[...].astype(F32), x_two[...].astype(F32))
    west, east = (
        jnp.concatenate([float(HALVES[i, a] * ONE_D[a]) * line for i in range(2)], axis=0)
        for line, a in ((west, 0), (east, 3))
    )
    add = dot_twice(table_ref[...], lines)
    rounded[...] = (columns_ref[...] + add).astype(BF16)
    rounded[0:64] = (columns_ref[0:64] + add[0:64] + west).astype(BF16)
    rounded[count - 64 : count] = (
        columns_ref[count - 64 : count] + add[count - 64 : count] + east
    ).astype(BF16)
    out_ref[...] = dot(pick[...], rounded[...]).astype(BF16)


def send_columns(columns, halos, blocks, cell, sizes):
    count, width = columns.shape
    table = np.concatenate(hi_lo_arrays(TABLES["col_y"]), axis=1)
    return pl.pallas_call(
        functools.partial(send_kernel, sizes, EYD * sizes[1]),
        out_shape=(
            jax.ShapeDtypeStruct((count, width), BF16),
            jax.ShapeDtypeStruct((1, count), I32),
        ),
        in_specs=[VMEM] * 8,
        out_specs=(VMEM,) * 2,
        scratch_shapes=[
            pltpu.VMEM((2, 32, width), F32),
            pltpu.VMEM(blocks.shape, F32),
            pltpu.VMEM((count, width), BF16),
            pltpu.VMEM((count, count), BF16),
        ],
        compiler_params=params(SEND_LIMIT),
        cost_estimate=cost(2e9, 5e6),
        name="send_columns",
    )(columns, jnp.asarray(table), halos[3], halos[1], halos[2], halos[0], blocks, cell)


SEND_LIMIT = 16
DYN_LIMIT = 56


def physics_kernel(
    fields, incoming_ref, q_ref, inverse_hbm, out_ref, inverse, tendency, sem
):
    count, width = incoming_ref.shape
    levels = width // fields
    copy = pltpu.make_async_copy(inverse_hbm, inverse, sem)
    copy.start()
    q = q_ref[...]
    size = count // PARTS
    for part in range(PARTS):
        pick = []
        for start in range(part * size, (part + 1) * size, 128):
            column = as_columns(q, start)
            pick.append(
                jnp.concatenate(
                    [
                        one_hot(column == iota((128, 128), 1) + other)
                        for other in range(0, count, 128)
                    ],
                    axis=1,
                )
            )
        physics = dot(jnp.concatenate(pick, axis=0), incoming_ref[...])
        if part == 0:
            copy.wait()
        for group in range(size // GROUP_COLS):
            rows = physics[group * GROUP_COLS : (group + 1) * GROUP_COLS]
            stacked = jnp.concatenate(
                [rows[:, f * levels : (f + 1) * levels] for f in range(fields)], axis=0
            )
            whole = part * (size // GROUP_COLS) + group
            result = dot_nt(stacked.astype(BF16), inverse[whole]) - stacked
            tendency[whole * GROUP_COLS : (whole + 1) * GROUP_COLS] = jnp.concatenate(
                [result[f * GROUP_COLS : (f + 1) * GROUP_COLS] for f in range(fields)], axis=1
            ).astype(BF16)
    for start in range(0, count, size):
        pick = one_hot(q == iota((size, count), 0) + start)
        out_ref[start : start + size] = dot(pick, tendency[...]).astype(BF16)


def physics_step(incoming, q, inverse, fields):
    count, width = incoming.shape
    return pl.pallas_call(
        functools.partial(physics_kernel, fields),
        out_shape=jax.ShapeDtypeStruct((count, width), BF16),
        in_specs=[VMEM, VMEM, ANY],
        out_specs=VMEM,
        scratch_shapes=[
            pltpu.VMEM(inverse.shape, BF16),
            pltpu.VMEM((count, width), BF16),
            pltpu.SemaphoreType.DMA,
        ],
        compiler_params=params(PHYSICS_LIMIT),
        cost_estimate=cost(3e9, 5e6),
        name="physics",
    )(incoming, q, inverse)


PHYSICS_LIMIT = 16
PARTS = 2


def unpack_kernel(
    received_ref,
    place_ref,
    own_lines,
    lines_table,
    back_ref,
    x_one,
    x_two,
    south_ref,
    north_ref,
    pick,
):
    count = received_ref.shape[0]
    place = place_ref[...]
    for start in range(0, count, 128):
        pick[start : start + 128] = one_hot(place == iota((128, count), 0) + start)
    back_ref[...] = dot(pick[...], received_ref[...]).astype(BF16)
    ends = []
    for kind, (first, a) in enumerate(((0, 0), (count - 64, 3))):
        rows = back_ref[first : first + 64].astype(F32)
        half = [
            sum(float(SPREAD[a, i]) * rows[32 * i + 16 * j : 32 * i + 16 * j + 16] for i in range(2))
            for j in range(2)
        ]
        nodes = [sum(float(SPREAD[b, j]) * half[j] for j in range(2)) for b in range(4)]
        ends.append(own_lines[kind] + jnp.concatenate(nodes, axis=0))
    one, two = by_parity("gx", *ends)
    x_one[...] = one.astype(BF16)
    x_two[...] = two.astype(BF16)
    lines = dot(lines_table[...], back_ref[...])
    south_ref[...] = own_lines[2] + lines[0:64] + lines[128:192]
    north_ref[...] = own_lines[3] + lines[64:128] + lines[192:256]


def unpack(received, place, own_lines):
    count, width = received.shape
    table = jnp.asarray(np.concatenate(hi_lo_arrays(TABLES["lines"]), axis=0))
    return pl.pallas_call(
        unpack_kernel,
        out_shape=(
            jax.ShapeDtypeStruct((count, width), BF16),
            jax.ShapeDtypeStruct((64, width), BF16),
            jax.ShapeDtypeStruct((64, width), BF16),
            jax.ShapeDtypeStruct((64, width), F32),
            jax.ShapeDtypeStruct((64, width), F32),
        ),
        in_specs=[VMEM] * 4,
        out_specs=(VMEM,) * 5,
        scratch_shapes=[pltpu.VMEM((count, count), BF16)],
        compiler_params=params(16),
        cost_estimate=cost(2e9, 4e6),
        name="unpack",
    )(received, place, own_lines, table)


def inner_kernel(dynamics_ref, back_ref, table_ref, total):
    width = total.shape[2]
    count = back_ref.shape[0]

    def near_sum(row, first, rows, skip):
        near = back_ref[pl.ds(first, rows)]
        both = dot(table_ref[:, skip : skip + rows], near)
        at = pl.ds(row * EYD, 2 * EYD)
        sums = both[0:512] + both[512:1024]
        total[at] = dynamics_ref[at] + sums.reshape(2 * EYD, NP, width)

    near_sum(0, 0, 192, 64)
    near_sum(EXD - 2, count - 192, 192, 0)

    def middle(pair, _):
        near_sum(pair * 2, pl.multiple_of(pair * 128 - 64, 64), 256, 0)
        return 0

    lax.fori_loop(1, EXD // 2 - 1, middle, 0, unroll=6)


def inner_sum(dynamics, back):
    one = TABLES["final"].reshape(EYD * NP, 3, 64)
    two = np.zeros((2, EYD * NP, 4, 64))
    two[0, :, 0:3] = one
    two[1, :, 1:4] = one
    table = np.concatenate(hi_lo_arrays(two.reshape(2 * EYD * NP, 256)), axis=0)
    return pl.pallas_call(
        inner_kernel,
        out_shape=jax.ShapeDtypeStruct(dynamics.shape, F32),
        in_specs=[VMEM] * 3,
        out_specs=VMEM,
        input_output_aliases={0: 0},
        compiler_params=params(16),
        cost_estimate=cost(4e9, 2e7),
        name="inner_sum",
    )(dynamics, back, jnp.asarray(table))


def to_slots_kernel(span_y, cell_smem, total, out_ref, slot_ref, buffer, sems):
    elements, _, width = total.shape
    fields, levels = buffer.shape[1], buffer.shape[4]
    per = elements // CHUNKS

    def copy(chunk):
        return pltpu.make_async_copy(
            buffer.at[chunk], out_ref.at[:, pl.ds(chunk * per, per)], sems.at[chunk]
        )

    for chunk in range(CHUNKS):

        def take_slots(i, _, chunk=chunk):
            for u in range(4):
                k = i * 4 + u
                tile = tile_number(cell_smem[chunk * per + k], span_y)
                slot_ref[0, tile] = chunk * per + k
                for f in range(fields):
                    buffer[chunk, f, k] = total[tile, :, f * levels : (f + 1) * levels]
            return 0

        lax.fori_loop(0, per // 4, take_slots, 0)
        copy(chunk).start()
    for chunk in range(CHUNKS):
        copy(chunk).wait()


def to_slots(cell, total, fields, span_y):
    elements, _, width = total.shape
    levels = width // fields
    return pl.pallas_call(
        functools.partial(to_slots_kernel, span_y),
        out_shape=(
            jax.ShapeDtypeStruct((fields, elements, NP, levels), F32),
            jax.ShapeDtypeStruct((1, elements), I32),
        ),
        in_specs=[SMEM, VMEM],
        out_specs=(ANY, SMEM),
        scratch_shapes=[
            pltpu.VMEM((CHUNKS, fields, elements // CHUNKS, NP, levels), F32),
            pltpu.SemaphoreType.DMA((CHUNKS,)),
        ],
        compiler_params=params(16),
        cost_estimate=cost(4e9, 2e7),
        name="to_slots",
    )(cell, total)


def border_kernel(
    fields, slot_ref, y_two, y_one, x_two, x_one, total_ref, table_ref, _, out_ref, buffer, sem
):
    width = x_one.shape[1]
    levels = width // fields
    halos = from_neighbours("gx", x_one[...], x_two[...])
    halos = halos + from_neighbours("gy", y_one[...], y_two[...])
    adds = []
    for kind, halo in enumerate(halos):
        table = table_ref[kind * 256 : kind * 256 + 256]
        adds.append(dot(table, halo).reshape(16, NP, width))
    for kind in range(4):
        for k in range(16):
            if kind >= 2 and k in (0, 15):
                continue
            tile = (k, (EXD - 1) * EYD + k, k * EYD, k * EYD + EYD - 1)[kind]
            whole = total_ref[tile] + adds[kind][k]
            if kind < 2 and k in (0, 15):
                whole = whole + adds[2 if k == 0 else 3][0 if kind == 0 else 15]
            for f in range(fields):
                buffer[kind, f, k] = whole[:, f * levels : (f + 1) * levels]
            pltpu.make_async_copy(
                buffer.at[kind, :, k], out_ref.at[:, slot_ref[0, tile]], sem.at[kind]
            ).start()
    for kind in range(4):
        part = buffer.at[kind] if kind < 2 else buffer.at[kind, :, 1:15]
        pltpu.make_async_copy(part, part, sem.at[kind]).wait()


def border_sum(slot, halos, total, out):
    fields, levels = out.shape[0], out.shape[3]
    table = jnp.asarray(TABLES["border"].astype(np.float32).astype(jnp.bfloat16))
    return pl.pallas_call(
        functools.partial(border_kernel, fields),
        out_shape=jax.ShapeDtypeStruct(out.shape, F32),
        in_specs=[SMEM] + [VMEM] * 6 + [ANY],
        out_specs=ANY,
        scratch_shapes=[
            pltpu.VMEM((4, fields, 16, NP, levels), F32),
            pltpu.SemaphoreType.DMA((4,)),
        ],
        input_output_aliases={7: 0},
        compiler_params=params(16),
        cost_estimate=cost(2e8, 4e6),
        name="border_sum",
    )(slot, *halos[::-1], total, table, out)


def regroup(blocks):
    return lax.all_to_all(blocks, ("gx", "gy"), split_axis=0, concat_axis=0, tiled=True)


def per_device(state_in, stiffness, elem_cell, group_column, group_inverse):
    fields, elements = state_in.shape[:2]
    sizes = (lax.axis_size("gx"), lax.axis_size("gy"))
    columns_dev = 4 * elements
    span_y = EYD * sizes[1]
    stiff = stiffness.reshape(NP * NP, elements)

    columns, blocks, q, x_one, x_two, y_one, y_two = front(
        elem_cell, group_column.reshape(1, columns_dev), stiff, state_in, sizes
    )
    hy = exchange("gy", y_one, y_two)
    hx = exchange("gx", x_one, x_two)
    blocks = regroup(blocks)

    outgoing, place = send_columns(
        columns, (*hx, *hy), blocks, elem_cell.reshape(1, elements), sizes
    )
    incoming = regroup(outgoing)
    dynamics, own_lines = dynamics_rows(elem_cell, stiff, state_in, span_y)
    incoming, dynamics, own_lines = lax.optimization_barrier((incoming, dynamics, own_lines))
    received = regroup(physics_step(incoming, q, group_inverse, fields))

    back, x_one, x_two, south, north = unpack(received, place, own_lines)
    bx = exchange("gx", x_one, x_two)
    by = exchange("gy", *messages(*bx, south, north, bf16_table("corner_pt")))
    total = inner_sum(dynamics, back)
    inner, slot = to_slots(elem_cell, total, fields, span_y)
    return border_sum(slot, (*bx, *by), total, inner)


def solution(mesh):
    placed = (
        P(None, ("gx", "gy"), None, None),
        P(None, None, ("gx", "gy")),
        P(("gx", "gy")),
        P(("gx", "gy")),
        P(("gx", "gy"), None, None),
    )
    return jax.shard_map(
        per_device,
        mesh=mesh,
        in_specs=placed,
        out_specs=P(None, ("gx", "gy"), None, None),
        check_vma=False,
    )
```

```python
import functools
import math

import jax
import jax.numpy as jnp
import numpy as np
from jax import lax
from jax.experimental import pallas as pl
from jax.experimental.pallas import tpu as pltpu
from jax.sharding import PartitionSpec as P

GROUP_COLS = 16
EXD = 16
EYD = 16
NP = 16
F32 = jnp.float32
BF16 = jnp.bfloat16
I32 = jnp.int32
MB = 1024 * 1024


def lagrange_value(node_index, position, gll_nodes):
    running = 1.0
    for other_index in range(4):
        if other_index != node_index:
            running = (
                running
                * (position - gll_nodes[other_index])
                / (gll_nodes[node_index] - gll_nodes[other_index])
            )
    return running


def half_tables():
    gll_nodes = [-1.0, -1.0 / math.sqrt(5.0), 1.0 / math.sqrt(5.0), 1.0]
    halves = np.zeros((2, 4))
    for half_index, (lower_end, upper_end) in enumerate(((-1.0, 0.0), (0.0, 1.0))):
        centre = 0.5 * (lower_end + upper_end)
        offset = 0.5 * (upper_end - lower_end) / math.sqrt(3.0)
        for node in range(4):
            first = lagrange_value(node, centre - offset, gll_nodes)
            second = lagrange_value(node, centre + offset, gll_nodes)
            halves[half_index, node] = 0.5 * (upper_end - lower_end) * (first + second)
    product = halves @ halves.T
    determinant = product[0, 0] * product[1, 1] - product[0, 1] * product[1, 0]
    inverse = (
        np.array([[product[1, 1], -product[0, 1]], [-product[1, 0], product[0, 0]]]) / determinant
    )
    spread = halves.T @ inverse
    return halves.astype(np.float32), spread.astype(np.float32)


HALVES, SPREAD = half_tables()
ONE_D = np.array([0.5, 1.0, 1.0, 0.5])


def shift_down(n):
    return np.eye(n, k=-1)


def local_pass(n):
    table = np.einsum("ab,xy->axby", np.eye(4), np.eye(n))
    table[0, :, 3, :] += shift_down(n)
    table[3, :, 0, :] += shift_down(n).T
    return table


def constant_tables():
    h = HALVES.astype(np.float64)
    s = SPREAD.astype(np.float64)
    w = ONE_D
    eye = np.eye(EXD)
    line = local_pass(EYD)
    col_y = np.zeros((EXD, 2, 2, EYD, 2, 2, EXD))
    for side, (b, y) in enumerate(((0, 0), (3, EYD - 1))):
        col_y[:, :, :, y, side] = np.einsum("j,ik,xz->xijkz", h[:, b] * w[b], np.eye(2), eye)
    col_y = col_y.reshape(EXD * 4 * EYD, 2 * 2 * EXD)
    nodes = np.einsum("ai,bj,yz->abyijz", s, s, np.eye(EYD))
    across = np.zeros((4, 4, EYD, 3, 2, 2, EYD))
    across[:, :, :, 1] = nodes
    across[0, :, :, 0] = nodes[3]
    across[3, :, :, 2] = nodes[0]
    full = np.einsum("byez,aezdijt->abydijt", line, across)
    full = full * w[:, None, None, None, None, None, None] * w[:, None, None, None, None, None]
    final = full.reshape(NP * EYD, 3 * 4 * EYD)
    along = local_pass(EXD)
    lines = np.zeros((2, 4, EXD, EXD, 2, 2, EYD))
    corner_pt = np.zeros((2, 4, EXD, 2, 4, EYD))
    for side, (b, y) in enumerate(((0, 0), (3, EYD - 1))):
        lines[side, :, :, :, :, :, y] = np.einsum("axcz,ci,j->axzij", along, s, s[b])
        corner_pt[side, 0, 0, 0, b, y] = 1.0
        corner_pt[side, 3, EXD - 1, 1, b, y] = 1.0
    lines = lines.reshape(2 * 4 * EXD, EXD * 4 * EYD)
    corner_pt = corner_pt.reshape(2 * 4 * EXD, 2 * 4 * EYD)
    border = np.zeros((4, EYD, NP, 64))
    order = full.transpose(2, 0, 1, 3, 4, 5, 6).reshape(EYD, NP, 3, 4 * EYD)
    for kind, a in enumerate((0, 3)):
        border[kind, :, 4 * a : 4 * a + 4] = np.einsum("b,byez->ybez", w[a] * w, line).reshape(
            EYD, 4, 4 * EYD
        )
    for side, b in enumerate((0, 3)):
        for a in range(4):
            for x in range(EXD):
                border[2 + side, x, 4 * a + b, 16 * a + x] = w[a] * w[b]
    return dict(
        col_y=col_y,
        final=order.reshape(EYD * NP, 3 * 4 * EYD),
        lines=lines,
        corner_pt=corner_pt,
        border=border.reshape(4 * EYD * NP, 64),
    )


def hi_lo_arrays(table):
    hi = np.asarray(table, np.float32).astype(jnp.bfloat16)
    lo = (np.asarray(table, np.float32) - hi.astype(np.float32)).astype(jnp.bfloat16)
    return hi, lo


def hi_lo(table):
    return jnp.asarray(np.concatenate(hi_lo_arrays(table), axis=1))


TABLES = constant_tables()


def bf16_table(name):
    return jnp.asarray(TABLES[name].astype(np.float32).astype(jnp.bfloat16))


def dot(left, right):
    return jnp.dot(left, right, preferred_element_type=F32)


def dot_nt(left, right):
    return lax.dot_general(left, right, (((1,), (1,)), ((), ())), preferred_element_type=F32)


def dot_twice(table, right):
    return dot(table, jnp.concatenate([right, right], axis=0))


def split(values):
    hi = values.astype(BF16)
    return hi, (values - hi.astype(F32)).astype(BF16)


def iota(shape, dim):
    return lax.broadcasted_iota(I32, shape, dim)


def one_hot(condition):
    return jnp.where(condition, 1.0, 0.0).astype(BF16)


def as_columns(row, start):
    piece = row[:, start : start + 128].astype(F32)
    return jnp.transpose(jnp.broadcast_to(piece, (128, 128))).astype(I32)


def tile_number(cell, span_y):
    shift = span_y.bit_length() - 1
    assert span_y == 1 << shift
    return ((cell >> shift) & (EXD - 1)) * EYD + (cell & (EYD - 1))


VMEM = pl.BlockSpec(memory_space=pltpu.VMEM)
SMEM = pl.BlockSpec(memory_space=pltpu.SMEM)
ANY = pl.BlockSpec(memory_space=pl.ANY)


def params(mib):
    return pltpu.CompilerParams(vmem_limit_bytes=mib * MB)


def cost(flops, moved):
    return pl.CostEstimate(flops=int(flops), bytes_accessed=int(moved), transcendentals=0)


def column_requests(devices, per_peer, group):
    columns_dev = devices * per_peer
    shift = columns_dev.bit_length() - 1
    source = group >> shift
    local = group & (columns_dev - 1)
    of_source = source == iota((devices, columns_dev), 0)
    marks = one_hot(of_source)
    upper = one_hot(iota((128, 128), 0) <= iota((128, 128), 1))
    before = jnp.zeros((devices, 1), F32)
    ranks = []
    for start in range(0, columns_dev, 128):
        piece = marks[:, start : start + 128]
        counts = dot(piece, upper) + before
        ranks.append(counts)
        before = counts[:, 127:128]
    counts = jnp.concatenate(ranks, axis=1)
    rank = jnp.sum(jnp.where(of_source, counts, 0.0), axis=0, keepdims=True).astype(I32) - 1
    of_rank = one_hot(rank == iota((128, columns_dev), 0))
    high = jnp.where(of_source, (local >> 5).astype(F32), 0.0).astype(BF16)
    low = jnp.where(of_source, (local & 31).astype(F32), 0.0).astype(BF16)
    return dot_nt(high, of_rank), dot_nt(low, of_rank), source * per_peer + rank


def diagonal(sizes, step_x, step_y):
    count_x, count_y = sizes
    x = lax.rem(lax.axis_index("gx") + step_x + count_x, count_x)
    y = lax.rem(lax.axis_index("gy") + step_y + count_y, count_y)
    return x * count_y + y


CHUNKS = 8


def state_copy(state_ref, raw, sems, chunk):
    per = raw.shape[2]
    return pltpu.make_async_copy(
        state_ref.at[:, pl.ds(chunk * per, per)], raw.at[chunk], sems.at[chunk]
    )


def tile_operators(span_y, cell, stiff):
    elements = cell.shape[1]
    marks = one_hot(tile_number(cell, span_y) == iota((elements, elements), 0))
    row = iota(stiff.shape, 0)
    stiff = stiff + jnp.where((row >> 4) == (row & 15), 1.0, 0.0)
    hi, lo = split(stiff)
    return dot_nt(marks, hi), dot_nt(marks, lo)


def place_operators(parts, operators):
    row, col = iota((256, 256), 0), iota((256, 256), 1)
    same_elem = one_hot((row & 15) == (col >> 4))
    tiling = one_hot((row & 15) == (col & 15))
    column = iota((EYD, 256), 1) >> 4
    for x in range(EXD):
        stacked = jnp.concatenate(
            [
                jnp.where(column == n, part[x * EYD : (x + 1) * EYD], 0.0).astype(BF16)
                for part in parts
                for n in range(NP)
            ],
            axis=0,
        )
        placed = dot(stacked, tiling).astype(BF16)
        operators[x, 0:256] = placed[0:256] * same_elem
        operators[x, 256:512] = placed[256:512] * same_elem


def place_states(span_y, cell_smem, state_ref, raw, sems, hi_ref, lo_ref):
    fields, per, _, levels = raw.shape[1:]
    for chunk in range(CHUNKS):
        state_copy(state_ref, raw, sems, chunk).wait()

        def place_slots(i, _, chunk=chunk):
            for u in range(4):
                k = i * 4 + u
                where = tile_number(cell_smem[chunk * per + k], span_y)
                for f in range(fields):
                    hi, lo = split(raw[chunk, f, k])
                    hi_ref[where, :, f * levels : (f + 1) * levels] = hi
                    lo_ref[where, :, f * levels : (f + 1) * levels] = lo
            return 0

        lax.fori_loop(0, per // 4, place_slots, 0, unroll=4)


def row_points(row, operators, hi_ref, lo_ref):
    width = hi_ref.shape[2]
    at = pl.ds(pl.multiple_of(row * EYD, EYD), EYD)
    hi = hi_ref[at].reshape(EYD * NP, width)
    lo = lo_ref[at].reshape(EYD * NP, width)
    both = dot(operators[row], hi)
    return both[0:256] + both[256:512] + dot(operators[row, 0:256], lo)


def shifted(values, step):
    rows = values.shape[0]
    moved = pltpu.roll(values, step % rows, 0)
    free = 0 if step > 0 else rows - 1
    return jnp.where(iota(values.shape, 0) == free, 0.0, moved)


def sum_along_y(nodes):
    for a in range(4):
        first, last = nodes[4 * a], nodes[4 * a + 3]
        nodes[4 * a] = first + shifted(last, 1)
        nodes[4 * a + 3] = last + shifted(first, -1)


def summed_line(line):
    first, last = line[0:16], line[48:64]
    return jnp.concatenate(
        [first + shifted(last, 1), line[16:48], last + shifted(first, -1)], axis=0
    )


def averaged(line):
    line = summed_line(line)
    return jnp.concatenate(
        [
            sum(
                float(HALVES[i, a] * ONE_D[a]) * line[16 * a : 16 * a + 16] for a in range(4)
            )
            for i in range(2)
        ],
        axis=0,
    )


def held_nodes(held, before, next_first):
    nodes = [held[16 * n : 16 * n + 16] for n in range(NP)]
    for b in range(4):
        nodes[b] = nodes[b] + before[16 * b : 16 * b + 16]
        if next_first is not None:
            nodes[12 + b] = nodes[12 + b] + next_first[b]
    return nodes


def front_kernel(
    sizes,
    span_y,
    cell_smem,
    cell_ref,
    group_ref,
    stiff_ref,
    state_ref,
    columns_out,
    blocks_out,
    q_ref,
    x_one,
    x_two,
    y_one,
    y_two,
    raw,
    sems,
    hi_ref,
    lo_ref,
    operators,
    held,
    before,
    lines,
    ends,
    columns,
    blocks_ref,
    out_sem,
):
    devices = sizes[0] * sizes[1]
    width = held.shape[1]
    for chunk in range(CHUNKS):
        state_copy(state_ref, raw, sems, chunk).start()
    place_operators(tile_operators(span_y, cell_ref[...], stiff_ref[...]), operators)
    high, low, q_ref[...] = column_requests(
        devices, group_ref.shape[1] // devices, group_ref[...]
    )
    first = iota((devices, 8, 128), 1) == 0
    blocks_ref[...] = jnp.where(first, high[:, None, :], low[:, None, :])
    place_states(span_y, cell_smem, state_ref, raw, sems, hi_ref, lo_ref)
    before[...] = jnp.zeros_like(before)
    held[...] = jnp.zeros_like(held)

    def emit(row, next_first):
        nodes = held_nodes(held, before, next_first)
        along = [
            [
                sum(float(HALVES[i, a] * ONE_D[a]) * nodes[4 * a + b] for a in range(4))
                for b in range(4)
            ]
            for i in range(2)
        ]
        for i in range(2):
            for j in range(2):
                columns[pl.ds(pl.multiple_of(row * 64 + (2 * i + j) * 16, 16), 16)] = sum(
                    float(HALVES[j, b] * ONE_D[b]) * along[i][b] for b in range(4)
                )

    def one_row(row, _):
        points = row_points(row, operators, hi_ref, lo_ref)

        ends[0, jnp.minimum(row, 1)] = points[0:64]
        ends[1, jnp.maximum(row - EXD + 2, 0)] = points[192:256]
        nodes = [points[16 * n : 16 * n + 16] for n in range(NP)]
        for a in range(4):
            lines[0, pl.ds(16 * a + row, 1)] = nodes[4 * a][0:1]
            lines[1, pl.ds(16 * a + row, 1)] = nodes[4 * a + 3][15:16]
        sum_along_y(nodes)
        emit(jnp.maximum(row - 1, 0), nodes[0:4])
        before[...] = held[192:256]
        for n in range(NP):
            held[16 * n : 16 * n + 16] = nodes[n]
        return 0

    def send(part):
        rows = (pl.ds(0, 576), pl.ds(576, 256), pl.ds(832, 192))[part]
        return pltpu.make_async_copy(columns.at[rows], columns_out.at[rows], out_sem.at[part])

    lax.fori_loop(0, 10, one_row, 0, unroll=10)
    send(0).start()
    lax.fori_loop(10, 14, one_row, 0, unroll=4)
    send(1).start()
    lax.fori_loop(14, EXD, one_row, 0, unroll=2)
    emit(EXD - 1, None)
    send(2).start()
    for axis, low, high, one, two in (
        ("gx", ends[0, 0], ends[1, 1], x_one, x_two),
        ("gy", lines[0], lines[1], y_one, y_two),
    ):
        first, second = by_parity(axis, averaged(low), averaged(high))
        one[...] = first.astype(BF16)
        two[...] = second.astype(BF16)
    for step_x, row in ((-1, 0), (1, 3 * 16 + 15)):
        for step_y, side in ((-1, 0), (1, 1)):
            block = diagonal(sizes, step_x, step_y)
            point = lines[side, row : row + 1]
            for f in range(width // 128):
                blocks_ref[block, 2 + f : 3 + f] = point[:, f * 128 : (f + 1) * 128]
    blocks_out[...] = blocks_ref[...].astype(BF16)
    send(0).wait()
    send(1).wait()
    send(2).wait()


def state_scratch(fields, elements, levels):
    width = fields * levels
    return [
        pltpu.VMEM((CHUNKS, fields, elements // CHUNKS, NP, levels), F32),
        pltpu.SemaphoreType.DMA((CHUNKS,)),
        pltpu.VMEM((elements, NP, width), BF16),
        pltpu.VMEM((elements, NP, width), BF16),
        pltpu.VMEM((EXD, 512, 256), BF16),
        pltpu.VMEM((256, width), F32),
        pltpu.VMEM((64, width), F32),
    ]


FRONT_LIMIT = 56


def front(cell, group, stiff, state, sizes):
    fields, elements, _, levels = state.shape
    width = fields * levels
    devices = sizes[0] * sizes[1]
    line = jax.ShapeDtypeStruct((32, width), BF16)
    return pl.pallas_call(
        functools.partial(front_kernel, sizes, EYD * sizes[1]),
        out_shape=(
            jax.ShapeDtypeStruct((4 * elements, width), F32),
            jax.ShapeDtypeStruct((devices, 8, 128), BF16),
            jax.ShapeDtypeStruct((1, 4 * elements), I32),
            line,
            line,
            line,
            line,
        ),
        in_specs=[SMEM, VMEM, VMEM, VMEM, ANY],
        out_specs=(ANY,) + (VMEM,) * 6,
        scratch_shapes=state_scratch(fields, elements, levels)
        + [
            pltpu.VMEM((2, 64, width), F32),
            pltpu.VMEM((2, 2, 64, width), F32),
            pltpu.VMEM((4 * elements, width), F32),
            pltpu.VMEM((devices, 8, 128), F32),
            pltpu.SemaphoreType.DMA((3,)),
        ],
        compiler_params=params(FRONT_LIMIT),
        cost_estimate=cost(4e9, 2e7),
        name="front",
    )(cell, cell.reshape(1, elements), group, stiff, state)


def dynamics_kernel(
    span_y,
    cell_smem,
    cell_ref,
    stiff_ref,
    state_ref,
    out_ref,
    lines_ref,
    raw,
    sems,
    hi_ref,
    lo_ref,
    operators,
    held,
    before,
    turned,
    ends,
    rows_out,
    out_sems,
):
    fields, _, levels = turned.shape
    for chunk in range(CHUNKS):
        state_copy(state_ref, raw, sems, chunk).start()
    place_operators(tile_operators(span_y, cell_ref[...], stiff_ref[...]), operators)
    place_states(span_y, cell_smem, state_ref, raw, sems, hi_ref, lo_ref)
    before[...] = jnp.zeros_like(before)
    held[...] = jnp.zeros_like(held)

    def emit(row, next_first):
        nodes = held_nodes(held, before, next_first)
        for n in range(NP):
            values = nodes[n] * float(ONE_D[n // 4] * ONE_D[n % 4])
            for f in range(fields):
                turned[f, 16 * n : 16 * n + 16] = values[:, f * levels : (f + 1) * levels]
        slot = row & 1
        for y in range(EYD):
            for f in range(fields):
                rows_out[slot, y, :, f * levels : (f + 1) * levels] = turned[
                    f, pl.ds(y, NP, stride=16)
                ]

    def copy_out(row):
        slot = row & 1
        return pltpu.make_async_copy(
            rows_out.at[slot], out_ref.at[pl.ds(row * EYD, EYD)], out_sems.at[slot]
        )

    def one_row(row, _):
        points = row_points(row, operators, hi_ref, lo_ref)
        nodes = [points[16 * n : 16 * n + 16] for n in range(NP)]
        ends[0, jnp.minimum(row, 1)] = points[0:64]
        ends[1, jnp.maximum(row - EXD + 2, 0)] = points[192:256]
        for a in range(4):
            lines_ref[2, pl.ds(16 * a + row, 1)] = nodes[4 * a][0:1]
            lines_ref[3, pl.ds(16 * a + row, 1)] = nodes[4 * a + 3][15:16]
        sum_along_y(nodes)

        @pl.when(row >= 3)
        def _():
            copy_out(row - 3).wait()

        @pl.when(row >= 1)
        def _():
            emit(row - 1, nodes[0:4])
            copy_out(row - 1).start()

        before[...] = held[192:256]
        for n in range(NP):
            held[16 * n : 16 * n + 16] = nodes[n]
        return 0

    lax.fori_loop(0, EXD, one_row, 0)
    copy_out(EXD - 3).wait()
    emit(EXD - 1, None)
    copy_out(EXD - 1).start()
    lines_ref[0] = ends[0, 0]
    lines_ref[1] = ends[1, 1]
    lines_ref[2] = summed_line(lines_ref[2])
    lines_ref[3] = summed_line(lines_ref[3])
    copy_out(EXD - 2).wait()
    copy_out(EXD - 1).wait()


def dynamics_rows(cell, stiff, state, span_y):
    fields, elements, _, levels = state.shape
    width = fields * levels
    return pl.pallas_call(
        functools.partial(dynamics_kernel, span_y),
        out_shape=(
            jax.ShapeDtypeStruct((elements, NP, width), F32),
            jax.ShapeDtypeStruct((4, 64, width), F32),
        ),
        in_specs=[SMEM, VMEM, VMEM, ANY],
        out_specs=(ANY, VMEM),
        scratch_shapes=state_scratch(fields, elements, levels)
        + [
            pltpu.VMEM((fields, 256, levels), F32),
            pltpu.VMEM((2, 2, 64, width), F32),
            pltpu.VMEM((2, EYD, NP, width), F32),
            pltpu.SemaphoreType.DMA((2,)),
        ],
        compiler_params=params(DYN_LIMIT),
        cost_estimate=cost(4e9, 2e7),
        name="dynamics_rows",
    )(cell, cell.reshape(1, elements), stiff, state)


def message_kernel(x_two, x_one, south_ref, north_ref, table, y_one, y_two):
    both = jnp.concatenate(from_neighbours("gx", x_one[...], x_two[...]), axis=0)
    add = dot(table[...], both)
    one, two = by_parity("gy", south_ref[...] + add[0:64], north_ref[...] + add[64:128])
    y_one[...] = one.astype(BF16)
    y_two[...] = two.astype(BF16)


def messages(one, two, south, north, table):
    width = one.shape[1]
    return pl.pallas_call(
        message_kernel,
        out_shape=(jax.ShapeDtypeStruct((64, width), BF16),) * 2,
        in_specs=[VMEM] * 5,
        out_specs=(VMEM,) * 2,
        compiler_params=params(16),
        cost_estimate=cost(4e7, 6e5),
        name="line_messages",
    )(two, one, south, north, table)


def pairs(axis, first):
    count = lax.axis_size(axis)
    low = range(0 if first else 1, count, 2)
    return [(i, (i + 1) % count) for i in low] + [((i + 1) % count, i) for i in low]


def exchange(axis, one, two):
    second = lax.ppermute(two, axis, pairs(axis, False))
    return lax.ppermute(one, axis, pairs(axis, True)), second


def by_parity(axis, to_low, to_high):
    even = (lax.axis_index(axis) & 1) == 0
    return jnp.where(even, to_high, to_low), jnp.where(even, to_low, to_high)


def from_neighbours(axis, one, two):
    even = (lax.axis_index(axis) & 1) == 0
    return jnp.where(even, two, one), jnp.where(even, one, two)


def places_kernel(
    sizes,
    span_y,
    columns_in,
    blocks_in,
    cell_ref,
    columns_ref,
    pick,
    place_ref,
    blocks_ref,
):
    count = pick.shape[0]
    devices = sizes[0] * sizes[1]
    per_peer = count // devices
    blocks_ref[...] = blocks_in[...].astype(F32)
    spread_out = one_hot((iota((128, count), 1) & (per_peer - 1)) == iota((128, count), 0))
    shift = per_peer.bit_length() - 1
    own = (iota((devices, count), 1) >> shift) == iota((devices, count), 0)
    wide = dot(blocks_ref[:, 0, :].astype(BF16), spread_out) * 32.0 + dot(
        blocks_ref[:, 1, :].astype(BF16), spread_out
    )
    requested = jnp.sum(jnp.where(own, wide, 0.0), axis=0, keepdims=True).astype(I32)
    elements = cell_ref.shape[1]
    marks = one_hot((requested >> 2) == iota((elements, count), 0))
    tile_row = tile_number(cell_ref[...], span_y).astype(F32)
    tile_row = jnp.broadcast_to(tile_row, (8, elements)).astype(BF16)
    tile = dot(tile_row, marks)[0:1].astype(I32)
    place = (tile >> 4) * 64 + (requested & 3) * 16 + (tile & 15)
    place_ref[...] = place
    for start in range(0, count, 128):
        column = as_columns(place, start)
        for other in range(0, count, 128):
            pick[start : start + 128, other : other + 128] = one_hot(
                column == iota((128, 128), 1) + other
            )


def send_places(columns, blocks, cell, sizes):
    count, width = columns.shape
    return pl.pallas_call(
        functools.partial(places_kernel, sizes, EYD * sizes[1]),
        out_shape=(
            jax.ShapeDtypeStruct((count, width), F32),
            jax.ShapeDtypeStruct((count, count), BF16),
            jax.ShapeDtypeStruct((1, count), I32),
            jax.ShapeDtypeStruct(blocks.shape, F32),
        ),
        in_specs=[VMEM] * 3,
        out_specs=(VMEM,) * 4,
        input_output_aliases={0: 0},
        compiler_params=params(16),
        cost_estimate=cost(4e9, 2e7),
        name="send_places",
    )(columns, blocks, cell)


def send_kernel(
    sizes,
    columns_ref,
    pick,
    blocks_ref,
    table_ref,
    y_two,
    y_one,
    x_two,
    x_one,
    out_ref,
    lines_ref,
    rounded,
):
    count, width = columns_ref.shape
    lines_ref[0], lines_ref[1] = from_neighbours(
        "gy", y_one[...].astype(F32), y_two[...].astype(F32)
    )
    for side, step_y in enumerate((-1, 1)):
        for step_x, a, x in ((-1, 0, 0), (1, 3, EXD - 1)):
            block = diagonal(sizes, step_x, step_y)
            for i in range(2):
                weight = float(HALVES[i, a] * ONE_D[a])
                for f in range(width // 128):
                    lines_ref[side, 16 * i + x : 16 * i + x + 1, f * 128 : (f + 1) * 128] += (
                        weight * blocks_ref[block, 2 + f : 3 + f]
                    )
    lines = jnp.concatenate([lines_ref[0], lines_ref[1]], axis=0).astype(BF16)
    west, east = from_neighbours("gx", x_one[...].astype(F32), x_two[...].astype(F32))
    west, east = (
        jnp.concatenate([float(HALVES[i, a] * ONE_D[a]) * line for i in range(2)], axis=0)
        for line, a in ((west, 0), (east, 3))
    )
    add = dot_twice(table_ref[...], lines)
    rounded[...] = (columns_ref[...] + add).astype(BF16)
    rounded[0:64] = (columns_ref[0:64] + add[0:64] + west).astype(BF16)
    rounded[count - 64 : count] = (
        columns_ref[count - 64 : count] + add[count - 64 : count] + east
    ).astype(BF16)
    out_ref[...] = dot(pick[...], rounded[...]).astype(BF16)


def send_columns(columns, pick, blocks, halos, sizes):
    count, width = columns.shape
    table = np.concatenate(hi_lo_arrays(TABLES["col_y"]), axis=1)
    return pl.pallas_call(
        functools.partial(send_kernel, sizes),
        out_shape=jax.ShapeDtypeStruct((count, width), BF16),
        in_specs=[VMEM] * 8,
        out_specs=VMEM,
        scratch_shapes=[
            pltpu.VMEM((2, 32, width), F32),
            pltpu.VMEM((count, width), BF16),
        ],
        compiler_params=params(SEND_LIMIT),
        cost_estimate=cost(2e9, 5e6),
        name="send_columns",
    )(columns, pick, blocks, jnp.asarray(table), halos[3], halos[2], halos[1], halos[0])


SEND_LIMIT = 16
DYN_LIMIT = 56


def physics_kernel(
    fields, incoming_ref, q_ref, inverse_hbm, out_ref, inverse, tendency, sem
):
    count, width = incoming_ref.shape
    levels = width // fields
    copy = pltpu.make_async_copy(inverse_hbm, inverse, sem)
    copy.start()
    q = q_ref[...]
    size = count // PARTS
    for part in range(PARTS):
        pick = []
        for start in range(part * size, (part + 1) * size, 128):
            column = as_columns(q, start)
            pick.append(
                jnp.concatenate(
                    [
                        one_hot(column == iota((128, 128), 1) + other)
                        for other in range(0, count, 128)
                    ],
                    axis=1,
                )
            )
        physics = dot(jnp.concatenate(pick, axis=0), incoming_ref[...])
        if part == 0:
            copy.wait()
        for group in range(size // GROUP_COLS):
            rows = physics[group * GROUP_COLS : (group + 1) * GROUP_COLS]
            stacked = jnp.concatenate(
                [rows[:, f * levels : (f + 1) * levels] for f in range(fields)], axis=0
            )
            whole = part * (size // GROUP_COLS) + group
            result = dot_nt(stacked.astype(BF16), inverse[whole]) - stacked
            tendency[whole * GROUP_COLS : (whole + 1) * GROUP_COLS] = jnp.concatenate(
                [result[f * GROUP_COLS : (f + 1) * GROUP_COLS] for f in range(fields)], axis=1
            ).astype(BF16)
    for start in range(0, count, size):
        pick = one_hot(q == iota((size, count), 0) + start)
        out_ref[start : start + size] = dot(pick, tendency[...]).astype(BF16)


def physics_step(incoming, q, inverse, fields):
    count, width = incoming.shape
    return pl.pallas_call(
        functools.partial(physics_kernel, fields),
        out_shape=jax.ShapeDtypeStruct((count, width), BF16),
        in_specs=[VMEM, VMEM, ANY],
        out_specs=VMEM,
        scratch_shapes=[
            pltpu.VMEM(inverse.shape, BF16),
            pltpu.VMEM((count, width), BF16),
            pltpu.SemaphoreType.DMA,
        ],
        compiler_params=params(PHYSICS_LIMIT),
        cost_estimate=cost(3e9, 5e6),
        name="physics",
    )(incoming, q, inverse)


PHYSICS_LIMIT = 16
PARTS = 2


def unpack_kernel(
    received_ref,
    place_ref,
    own_lines,
    lines_table,
    back_ref,
    x_one,
    x_two,
    south_ref,
    north_ref,
    pick,
):
    count = received_ref.shape[0]
    place = place_ref[...]
    for start in range(0, count, 128):
        pick[start : start + 128] = one_hot(place == iota((128, count), 0) + start)
    back_ref[...] = dot(pick[...], received_ref[...]).astype(BF16)
    ends = []
    for kind, (first, a) in enumerate(((0, 0), (count - 64, 3))):
        rows = back_ref[first : first + 64].astype(F32)
        half = [
            sum(float(SPREAD[a, i]) * rows[32 * i + 16 * j : 32 * i + 16 * j + 16] for i in range(2))
            for j in range(2)
        ]
        nodes = [sum(float(SPREAD[b, j]) * half[j] for j in range(2)) for b in range(4)]
        ends.append(own_lines[kind] + jnp.concatenate(nodes, axis=0))
    one, two = by_parity("gx", *ends)
    x_one[...] = one.astype(BF16)
    x_two[...] = two.astype(BF16)
    lines = dot(lines_table[...], back_ref[...])
    south_ref[...] = own_lines[2] + lines[0:64] + lines[128:192]
    north_ref[...] = own_lines[3] + lines[64:128] + lines[192:256]


def unpack(received, place, own_lines):
    count, width = received.shape
    table = jnp.asarray(np.concatenate(hi_lo_arrays(TABLES["lines"]), axis=0))
    return pl.pallas_call(
        unpack_kernel,
        out_shape=(
            jax.ShapeDtypeStruct((count, width), BF16),
            jax.ShapeDtypeStruct((64, width), BF16),
            jax.ShapeDtypeStruct((64, width), BF16),
            jax.ShapeDtypeStruct((64, width), F32),
            jax.ShapeDtypeStruct((64, width), F32),
        ),
        in_specs=[VMEM] * 4,
        out_specs=(VMEM,) * 5,
        scratch_shapes=[pltpu.VMEM((count, count), BF16)],
        compiler_params=params(16),
        cost_estimate=cost(2e9, 4e6),
        name="unpack",
    )(received, place, own_lines, table)


def inner_kernel(dynamics_ref, back_ref, table_ref, total):
    width = total.shape[2]
    count = back_ref.shape[0]

    def near_sum(row, first, rows, skip):
        near = back_ref[pl.ds(first, rows)]
        both = dot(table_ref[:, skip : skip + rows], near)
        at = pl.ds(row * EYD, 2 * EYD)
        sums = both[0:512] + both[512:1024]
        total[at] = dynamics_ref[at] + sums.reshape(2 * EYD, NP, width)

    near_sum(0, 0, 192, 64)
    near_sum(EXD - 2, count - 192, 192, 0)

    def middle(pair, _):
        near_sum(pair * 2, pl.multiple_of(pair * 128 - 64, 64), 256, 0)
        return 0

    lax.fori_loop(1, EXD // 2 - 1, middle, 0, unroll=6)


def inner_sum(dynamics, back):
    one = TABLES["final"].reshape(EYD * NP, 3, 64)
    two = np.zeros((2, EYD * NP, 4, 64))
    two[0, :, 0:3] = one
    two[1, :, 1:4] = one
    table = np.concatenate(hi_lo_arrays(two.reshape(2 * EYD * NP, 256)), axis=0)
    return pl.pallas_call(
        inner_kernel,
        out_shape=jax.ShapeDtypeStruct(dynamics.shape, F32),
        in_specs=[VMEM] * 3,
        out_specs=VMEM,
        input_output_aliases={0: 0},
        compiler_params=params(16),
        cost_estimate=cost(4e9, 2e7),
        name="inner_sum",
    )(dynamics, back, jnp.asarray(table))


def to_slots_kernel(span_y, cell_smem, total, out_ref, slot_ref, buffer, sems):
    elements, _, width = total.shape
    fields, levels = buffer.shape[1], buffer.shape[4]
    per = elements // CHUNKS

    def copy(chunk):
        return pltpu.make_async_copy(
            buffer.at[chunk], out_ref.at[:, pl.ds(chunk * per, per)], sems.at[chunk]
        )

    for chunk in range(CHUNKS):

        def take_slots(i, _, chunk=chunk):
            for u in range(4):
                k = i * 4 + u
                tile = tile_number(cell_smem[chunk * per + k], span_y)
                slot_ref[0, tile] = chunk * per + k
                for f in range(fields):
                    buffer[chunk, f, k] = total[tile, :, f * levels : (f + 1) * levels]
            return 0

        lax.fori_loop(0, per // 4, take_slots, 0, unroll=4)
        copy(chunk).start()
    for chunk in range(CHUNKS):
        copy(chunk).wait()


def to_slots(cell, total, fields, span_y):
    elements, _, width = total.shape
    levels = width // fields
    return pl.pallas_call(
        functools.partial(to_slots_kernel, span_y),
        out_shape=(
            jax.ShapeDtypeStruct((fields, elements, NP, levels), F32),
            jax.ShapeDtypeStruct((1, elements), I32),
        ),
        in_specs=[SMEM, VMEM],
        out_specs=(ANY, SMEM),
        scratch_shapes=[
            pltpu.VMEM((CHUNKS, fields, elements // CHUNKS, NP, levels), F32),
            pltpu.SemaphoreType.DMA((CHUNKS,)),
        ],
        compiler_params=params(16),
        cost_estimate=cost(4e9, 2e7),
        name="to_slots",
    )(cell, total)


def border_kernel(
    fields, slot_ref, y_two, y_one, x_two, x_one, total_ref, table_ref, _, out_ref, buffer, sem
):
    width = x_one.shape[1]
    levels = width // fields
    halos = from_neighbours("gx", x_one[...], x_two[...])
    halos = halos + from_neighbours("gy", y_one[...], y_two[...])
    adds = []
    for kind, halo in enumerate(halos):
        table = table_ref[kind * 256 : kind * 256 + 256]
        adds.append(dot(table, halo).reshape(16, NP, width))
    for kind in range(4):
        for k in range(16):
            if kind >= 2 and k in (0, 15):
                continue
            tile = (k, (EXD - 1) * EYD + k, k * EYD, k * EYD + EYD - 1)[kind]
            whole = total_ref[tile] + adds[kind][k]
            if kind < 2 and k in (0, 15):
                whole = whole + adds[2 if k == 0 else 3][0 if kind == 0 else 15]
            for f in range(fields):
                buffer[kind, f, k] = whole[:, f * levels : (f + 1) * levels]
            pltpu.make_async_copy(
                buffer.at[kind, :, k], out_ref.at[:, slot_ref[0, tile]], sem.at[kind]
            ).start()
    for kind in range(4):
        part = buffer.at[kind] if kind < 2 else buffer.at[kind, :, 1:15]
        pltpu.make_async_copy(part, part, sem.at[kind]).wait()


def border_sum(slot, halos, total, out):
    fields, levels = out.shape[0], out.shape[3]
    table = jnp.asarray(TABLES["border"].astype(np.float32).astype(jnp.bfloat16))
    return pl.pallas_call(
        functools.partial(border_kernel, fields),
        out_shape=jax.ShapeDtypeStruct(out.shape, F32),
        in_specs=[SMEM] + [VMEM] * 6 + [ANY],
        out_specs=ANY,
        scratch_shapes=[
            pltpu.VMEM((4, fields, 16, NP, levels), F32),
            pltpu.SemaphoreType.DMA((4,)),
        ],
        input_output_aliases={7: 0},
        compiler_params=params(16),
        cost_estimate=cost(2e8, 4e6),
        name="border_sum",
    )(slot, *halos[::-1], total, table, out)


def regroup(blocks):
    return lax.all_to_all(blocks, ("gx", "gy"), split_axis=0, concat_axis=0, tiled=True)


def per_device(state_in, stiffness, elem_cell, group_column, group_inverse):
    fields, elements = state_in.shape[:2]
    sizes = (lax.axis_size("gx"), lax.axis_size("gy"))
    columns_dev = 4 * elements
    span_y = EYD * sizes[1]
    stiff = stiffness.reshape(NP * NP, elements)

    columns, blocks, q, x_one, x_two, y_one, y_two = front(
        elem_cell, group_column.reshape(1, columns_dev), stiff, state_in, sizes
    )
    hy = exchange("gy", y_one, y_two)
    hx = exchange("gx", x_one, x_two)
    blocks = regroup(blocks)

    columns, pick, place, blocks = send_places(
        columns, blocks, elem_cell.reshape(1, elements), sizes
    )
    outgoing = send_columns(columns, pick, blocks, (*hx, *hy), sizes)
    incoming = regroup(outgoing)
    dynamics, own_lines = dynamics_rows(elem_cell, stiff, state_in, span_y)
    incoming, dynamics, own_lines = lax.optimization_barrier((incoming, dynamics, own_lines))
    received = regroup(physics_step(incoming, q, group_inverse, fields))

    back, x_one, x_two, south, north = unpack(received, place, own_lines)
    bx = exchange("gx", x_one, x_two)
    by = exchange("gy", *messages(*bx, south, north, bf16_table("corner_pt")))
    total = inner_sum(dynamics, back)
    inner, slot = to_slots(elem_cell, total, fields, span_y)
    return border_sum(slot, (*bx, *by), total, inner)


def solution(mesh):
    placed = (
        P(None, ("gx", "gy"), None, None),
        P(None, None, ("gx", "gy")),
        P(("gx", "gy")),
        P(("gx", "gy")),
        P(("gx", "gy"), None, None),
    )
    return jax.shard_map(
        per_device,
        mesh=mesh,
        in_specs=placed,
        out_specs=P(None, ("gx", "gy"), None, None),
        check_vma=False,
    )
```
